32 devices in a mesh: seq: 8 (over z, x), head: 4 (over y, core).
Axes of the slice: x: 2, y: 2, z: 4, core: 2. Of those that a mesh axis runs over, the one named last changes fastest.
Arguments:
- prompt_q: bfloat16 [8192, 2048], P('seq', 'head'), may hold values from -6 to 6
- prompt_k: bfloat16 [8192, 2048], P('seq', 'head'), may hold values from -6 to 6
- prompt_v: bfloat16 [8192, 2048], P('seq', 'head'), may hold values from -6 to 6
- prompt_grad: bfloat16 [8192, 2048], P('seq', 'head'), may hold values from -6 to 6
- cand_q: bfloat16 [4096, 2048], P('seq', 'head'), may hold values from -6 to 6
- cand_k: bfloat16 [4096, 2048], P('seq', 'head'), may hold values from -6 to 6
- cand_v: bfloat16 [4096, 2048], P('seq', 'head'), may hold values from -6 to 6
- readout: float32 [2048], P('head'), may hold values from -0.24 to 0.24
- prompt_ends: int32 [8], replicated, may hold values from 1 to 8192, as said below
- cand_lengths: int32 [8, 2], P('seq'), may hold values from 1 to 384, 512 in all within a row
- cand_prompt: int32 [16], replicated, may hold values from 0 to 7
- cand_ranks: int32 [16], replicated, may hold values from 0 to 3
Outputs:
- prompt_dq: bfloat16 [8192, 2048], P('seq', 'head')
- prompt_dk: bfloat16 [8192, 2048], P('seq', 'head')
- prompt_dv: bfloat16 [8192, 2048], P('seq', 'head')
- cand_dq: bfloat16 [4096, 2048], P('seq', 'head')
- cand_dk: bfloat16 [4096, 2048], P('seq', 'head')
- cand_dv: bfloat16 [4096, 2048], P('seq', 'head')
- list_loss: float32 [], replicated
The draws below stay inside these ranges and needn't reach their ends.
Inputs may be any that keep to these rules, and one draw needn't show every extreme that they name: `prompt_ends`: strictly increasing; the last equals 8192; at most 2 ends lie in each range (d * 1024, (d + 1) * 1024], and in some range exactly 2. `cand_lengths`: each row sums to 512, and no entry exceeds 384.
All inputs are finite; a program needn't handle non-finite values.
Results may differ from the reference program's by a relative error of at most 0.0062.
Values may be sent and summed in bfloat16 or wider, within the bound.
No kernel may reach another device: no remote copies, remote signals or barrier semaphores. Data moves between devices by JAX's collectives and lax.ppermute only.
A program may use at most 128 MiB of HBM per device.

```python
import math
import jax
import jax.numpy as jnp
import numpy as np
from jax import lax

HEADS = 16
E = 128
P_DEV = 1024
C_DEV = 512
NC_DEV = 2
ENDS = 2
PROMPTS = 8
TOTAL = 8192
CTOTAL = 4096
NCAND = 16
CMAX = 384
N_SEQ = 8


def draw_prompt_ends(key, part):
    device_count = PROMPTS
    slot_total = device_count * ENDS
    slot_span = P_DEV // ENDS
    early_blocks = device_count // 2 + 1
    key_order, key_device, key_offset = jax.random.split(jax.random.fold_in(key, 7), 3)
    slot_order = jax.random.permutation(key_order, slot_total).astype(jnp.int32)
    chosen = jax.random.randint(key_device, (), 0, early_blocks).astype(jnp.int32)
    slot_ids = jnp.arange(slot_total, dtype=jnp.int32)
    device_of = slot_ids // ENDS
    slot_of = slot_ids % ENDS
    forced_full = device_of == chosen
    forced_last = slot_ids == slot_total - 1
    eligible = device_of < early_blocks
    normal_rank = jnp.where(eligible, slot_order, slot_total + slot_ids)
    priority = jnp.where(jnp.logical_or(forced_full, forced_last), -1 - slot_ids, normal_rank)
    ranked = jnp.argsort(priority, stable=True)
    selected = jnp.zeros((slot_total,), jnp.int32).at[ranked[:device_count]].set(1)
    offsets = slot_of * slot_span + jax.random.randint(key_offset, (slot_total,), 1, slot_span + 1).astype(jnp.int32)
    offsets = jnp.where(forced_last, P_DEV, offsets)
    positions = device_of * P_DEV + offsets
    marked = jnp.where(selected > 0, positions, slot_total * P_DEV + 1)
    return jnp.sort(marked)[:device_count].astype(jnp.int32)


def place_ends(result, stream_key, least, high):
    longest = result.shape.index(max(result.shape))
    spots = []
    for shift in (0, 1):
        where = [jax.random.randint(jax.random.fold_in(stream_key, axis), (), 0, length) for axis, length in enumerate(result.shape)]
        where[longest] = (where[longest] + shift) % result.shape[longest]
        spots.append(tuple(where))
    return result.at[spots[0]].set(least).at[spots[1]].set(high)


def block_levels(own_key, extent, cuts, low, high):
    level = 1.0
    for axis_at, blocks in cuts:
        steps = jax.random.uniform(jax.random.fold_in(jax.random.fold_in(own_key, 6), axis_at), (blocks,), jnp.float32, low / len(cuts), high / len(cuts))
        level = level * jnp.repeat(jnp.exp(steps), extent[axis_at] // blocks).reshape((-1,) + (1,) * (len(extent) - 1 - axis_at))
    return level


def split_up(number_of, total, bound, lean):
    portions = [(1 << 20) // math.isqrt(rank ** lean) + 1 for rank in range(2, number_of + 1)]
    rest, counts = total - bound - (number_of - 1), [1] * (number_of - 1)
    while rest > 0:
        candidates = [i for i in range(number_of - 1) if counts[i] < bound]
        pool, left = sum([portions[i] for i in candidates]), rest
        for i in candidates:
            extra = min(bound - counts[i], max(1, left * portions[i] // pool), rest)
            counts[i] = counts[i] + extra
            rest = rest - extra
    return np.array([bound] + counts)


def uneven_parts(key, count, total, most, skew):
    if count == 2:
        one = jax.random.randint(key, (), max(1, total - most), min(most, total - 1) + 1)
        return jnp.stack([one, total - one])
    sizes = jnp.asarray(split_up(count, total, most, skew), jnp.int32)
    couples = (count - 1) // 2
    donor, receiver = sizes[1:1 + 2 * couples:2], sizes[2:2 + 2 * couples:2]
    room = jnp.minimum(donor - 1, most - receiver)
    shifted = jax.random.randint(jax.random.fold_in(key, 1), (couples,), 0, 1 << 20) % (room + 1)
    sizes = sizes.at[1:1 + 2 * couples:2].set(donor - shifted).at[2:2 + 2 * couples:2].set(receiver + shifted)
    return sizes[jax.random.permutation(jax.random.fold_in(key, 2), count)]


def noise(own_key, dims, width, reach, cuts=(), kind=jnp.bfloat16):
    array = jax.random.normal(own_key, dims, jnp.float32) * width
    if len(cuts) > 0:
        array = block_levels(own_key, dims, cuts, -0.22, 0.18) * array
    return jnp.clip(array, min=-reach, max=reach).astype(kind)


def setup_inputs(seed: int = 0) -> dict:
    key_of = jax.random.split(jax.random.key(seed), 13)
    return {
        "prompt_q": noise(key_of[0], (TOTAL, HEADS * E), 1.0, 6.0, ((0, 8), (1, 4))),
        "prompt_k": noise(key_of[1], (TOTAL, HEADS * E), 1.0, 6.0, ((0, 8), (1, 4))),
        "prompt_v": noise(key_of[2], (TOTAL, HEADS * E), 1.0, 6.0, ((0, 8), (1, 4))),
        "prompt_grad": noise(key_of[3], (TOTAL, HEADS * E), 1.0, 6.0, ((0, 8), (1, 4))),
        "cand_q": noise(key_of[4], (CTOTAL, HEADS * E), 1.0, 6.0, ((0, 8), (1, 4))),
        "cand_k": noise(key_of[5], (CTOTAL, HEADS * E), 1.0, 6.0, ((0, 8), (1, 4))),
        "cand_v": noise(key_of[6], (CTOTAL, HEADS * E), 1.0, 6.0, ((0, 8), (1, 4))),
        "readout": noise(key_of[7], (HEADS * E,), 0.04, 0.24, ((0, 4),), jnp.float32),
        "prompt_ends": draw_prompt_ends(jax.random.fold_in(key_of[12], 71), 0),
        "cand_lengths": jax.vmap(lambda own: uneven_parts(own, NC_DEV, C_DEV, CMAX, 1))(jax.random.split(key_of[9], N_SEQ)).reshape((N_SEQ, NC_DEV)).astype(jnp.int32),
        "cand_prompt": place_ends(jax.random.randint(key_of[10], (NCAND,), 0, PROMPTS), jax.random.fold_in(key_of[10], 1), 0, PROMPTS - 1).astype(jnp.int32),
        "cand_ranks": place_ends(jax.random.randint(key_of[11], (NCAND,), 0, 4), jax.random.fold_in(key_of[11], 1), 0, 3).astype(jnp.int32),
    }


grad_scale = 1048576.0

def product_of(form, left, right):
    return jnp.einsum(form, left.astype(jnp.float32), right.astype(jnp.float32), precision=lax.Precision.HIGHEST)

def pick_value(table, wanted):
    spots = jnp.arange(table.shape[0], dtype=jnp.int32)
    return jnp.sum(jnp.where(spots == wanted, table, 0)).astype(jnp.int32)

def slab_layout(prompt_ends, slab_index, slab_width, slot_count):
    prompt_count = prompt_ends.shape[0]
    slab_start = slab_index * slab_width
    position = slab_start + jnp.arange(slab_width, dtype=jnp.int32)
    segment = lax.optimization_barrier(jnp.sum((prompt_ends[None, :] <= position[:, None]).astype(jnp.int32), axis=1)).astype(jnp.int32)
    begins = jnp.logical_or(slab_index == 0, jnp.any(prompt_ends == slab_start))
    first_seg = segment[0]
    last_seg = segment[slab_width - 1]
    first_end = jnp.sum((prompt_ends <= slab_start).astype(jnp.int32)).astype(jnp.int32)
    slot_pid = first_end + jnp.arange(slot_count, dtype=jnp.int32)
    prompt_ids = jnp.arange(prompt_count, dtype=jnp.int32)
    slot_end = lax.optimization_barrier(jnp.sum(jnp.where(prompt_ids[None, :] == slot_pid[:, None], prompt_ends[None, :], 0), axis=1)).astype(jnp.int32)
    slot_valid = jnp.logical_and(slot_pid < prompt_count, slot_end <= slab_start + slab_width)
    slot_masks = jnp.logical_and(segment[None, :] == slot_pid[:, None], slot_valid[:, None])
    row_masks = jnp.concatenate([slot_masks, (segment == last_seg)[None, :]], axis=0).astype(jnp.float32)
    start_flag = jnp.logical_or(begins, first_seg != last_seg).astype(jnp.float32)
    end_flag = slot_valid[0].astype(jnp.float32)
    cont_right = (pick_value(prompt_ends, last_seg) != slab_start + slab_width).astype(jnp.float32)
    contin = 1.0 - begins.astype(jnp.float32)
    first_mask = (segment == first_seg).astype(jnp.float32)
    from_first = jnp.logical_and(slot_pid == first_seg, slot_valid).astype(jnp.float32)
    return (segment, row_masks, first_mask, contin, from_first, slot_pid, slot_valid, start_flag, end_flag, cont_right)

def cand_layout(lengths, cand_width):
    bounds = jnp.cumsum(lengths).astype(jnp.int32)
    tok_pos = jnp.arange(cand_width, dtype=jnp.int32)
    cand_id = lax.optimization_barrier(jnp.sum((bounds[None, :] <= tok_pos[:, None]).astype(jnp.int32), axis=1)).astype(jnp.int32)
    cand_masks = (cand_id[None, :] == jnp.arange(lengths.shape[0], dtype=jnp.int32)[:, None]).astype(jnp.float32)
    same_cand = jnp.logical_and(cand_id[:, None] == cand_id[None, :], tok_pos[None, :] <= tok_pos[:, None])
    return (cand_masks, same_cand)

def listwise(raw_scores, cand_prompt, cand_ranks, prompt_count):
    squashed = 3.0 * jnp.tanh(raw_scores)
    same_group = (cand_prompt[:, None] == cand_prompt[None, :]).astype(jnp.float32)
    exp_scores = jnp.exp(squashed)
    denoms = lax.optimization_barrier(jnp.sum(same_group * exp_scores[None, :], axis=1))
    rank_weight = jnp.exp(-cand_ranks.astype(jnp.float32))
    targets = rank_weight / lax.optimization_barrier(jnp.sum(same_group * rank_weight[None, :], axis=1))
    list_loss = -jnp.sum(targets * (squashed - jnp.log(denoms))) / prompt_count
    tanh_raw = jnp.tanh(raw_scores)
    raw_grad = grad_scale / prompt_count * (exp_scores / denoms - targets) * 3.0 * (1.0 - tanh_raw * tanh_raw)
    return (list_loss, raw_grad)

def reference(prompt_q, prompt_k, prompt_v, prompt_grad, cand_q, cand_k, cand_v, readout, prompt_ends, cand_lengths, cand_prompt, cand_ranks):
    scaling = 1.0 / math.sqrt(E * P_DEV)
    slab_ids = jnp.arange(N_SEQ, dtype=jnp.int32)
    queries = prompt_q.reshape(N_SEQ, P_DEV, HEADS, E)
    keys_in = prompt_k.reshape(N_SEQ, P_DEV, HEADS, E)
    values_in = prompt_v.reshape(N_SEQ, P_DEV, HEADS, E)
    grads_in = prompt_grad.reshape(N_SEQ, P_DEV, HEADS, E)
    cand_queries = cand_q.reshape(N_SEQ, C_DEV, HEADS, E)
    cand_keys = cand_k.reshape(N_SEQ, C_DEV, HEADS, E)
    cand_values = cand_v.reshape(N_SEQ, C_DEV, HEADS, E)
    readout_heads = readout.reshape(HEADS, E)

    def layout_of(slab_index):
        return slab_layout(prompt_ends, slab_index, P_DEV, ENDS)
    segments, row_masks, first_masks, contins, from_first, slot_pid, slot_valid, start_flags, end_flags, cont_rights = jax.vmap(layout_of)(slab_ids)

    def local_sums(inputs):
        masks_one, keys_blk, values_blk = inputs
        return product_of('mthd,the->mhde', masks_one[:, :, None, None] * keys_blk[None].astype(jnp.float32), values_blk)
    slab_sums = lax.map(local_sums, (row_masks, keys_in, values_in))

    def forward_chain(running, inputs):
        tail_state, start_flag = inputs
        return (tail_state + (1.0 - start_flag) * running, running)
    zero_state = jnp.zeros((HEADS, E, E), jnp.float32)
    unused_state, incoming = lax.scan(forward_chain, zero_state, (slab_sums[:, ENDS], start_flags))
    incoming_first = contins[:, None, None, None] * incoming
    valid_float = slot_valid.astype(jnp.float32)
    end_slots = (slab_sums[:, :ENDS] + from_first[:, :, None, None, None] * incoming_first[:, None]) * valid_float[:, :, None, None, None]
    end_states = end_slots.astype(jnp.bfloat16)
    target_rows = jnp.where(slot_valid, slot_pid, PROMPTS).reshape(-1).astype(jnp.int32)
    by_prompt = jnp.zeros((PROMPTS + 1, HEADS, E, E), jnp.float32).at[target_rows].add(end_states.reshape(-1, HEADS, E, E).astype(jnp.float32))
    cand_states = by_prompt[cand_prompt].astype(jnp.bfloat16).reshape(N_SEQ, NC_DEV, HEADS, E, E)

    def cand_forward(slab_q, slab_k, slab_v, slab_lengths, slab_states):
        cand_masks, same_cand = cand_layout(slab_lengths, C_DEV)
        qk_scores = product_of('thd,shd->hts', slab_q, slab_k)
        attn_weights = jnp.where(same_cand[None], qk_scores, 0.0).astype(jnp.bfloat16)
        masked_queries = cand_masks[:, :, None, None] * slab_q[None].astype(jnp.float32)
        outputs = scaling * (product_of('hts,she->the', attn_weights, slab_v) + product_of('jthd,jhde->the', masked_queries, slab_states))
        return (cand_masks, same_cand, attn_weights, masked_queries, outputs)

    def cand_scores(inputs):
        slab_q, slab_k, slab_v, slab_lengths, slab_states = inputs
        cand_masks, same_cand, attn_weights, masked_queries, outputs = cand_forward(slab_q, slab_k, slab_v, slab_lengths, slab_states)
        token_score = lax.optimization_barrier(jnp.sum(jax.nn.silu(outputs) * readout_heads[None], axis=(1, 2)))
        return lax.optimization_barrier(jnp.sum(cand_masks * token_score[None, :], axis=1)) / slab_lengths.astype(jnp.float32)
    raw_scores = lax.map(cand_scores, (cand_queries, cand_keys, cand_values, cand_lengths, cand_states)).reshape(-1)
    list_loss, raw_grad = listwise(raw_scores, cand_prompt, cand_ranks, PROMPTS)

    def cand_backward(inputs):
        slab_q, slab_k, slab_v, slab_lengths, slab_states, slab_grad = inputs
        cand_masks, same_cand, attn_weights, masked_queries, outputs = cand_forward(slab_q, slab_k, slab_v, slab_lengths, slab_states)
        token_coef = lax.optimization_barrier(jnp.sum(cand_masks * (slab_grad / slab_lengths.astype(jnp.float32))[:, None], axis=0))
        sigma = jax.nn.sigmoid(outputs)
        out_grad = (token_coef[:, None, None] * readout_heads[None] * sigma * (1.0 + outputs * (1.0 - sigma))).astype(jnp.bfloat16)
        gv_scores = product_of('the,she->hts', out_grad, slab_v)
        grad_weights = jnp.where(same_cand[None], gv_scores, 0.0).astype(jnp.bfloat16)
        masked_grads = cand_masks[:, :, None, None] * out_grad[None].astype(jnp.float32)
        grad_q = scaling * (product_of('hts,shd->thd', grad_weights, slab_k) + product_of('jthe,jhde->thd', masked_grads, slab_states))
        grad_k = scaling * product_of('hts,thd->shd', grad_weights, slab_q)
        grad_v = scaling * product_of('hts,the->she', attn_weights, out_grad)
        state_grads = (scaling * product_of('jthd,the->jhde', masked_queries, out_grad)).astype(jnp.bfloat16)
        return (grad_q.astype(jnp.bfloat16), grad_k.astype(jnp.bfloat16), grad_v.astype(jnp.bfloat16), state_grads)
    cand_dq, cand_dk, cand_dv, state_grads = lax.map(cand_backward, (cand_queries, cand_keys, cand_values, cand_lengths, cand_states, raw_grad.reshape(N_SEQ, NC_DEV)))
    end_grads = jnp.zeros((PROMPTS, HEADS, E, E), jnp.float32).at[cand_prompt].add(state_grads.reshape(-1, HEADS, E, E).astype(jnp.float32))
    slot_grads = end_grads[jnp.minimum(slot_pid, PROMPTS - 1)] * valid_float[:, :, None, None, None]

    def head_terms(inputs):
        mask_one, slab_q, slab_g = inputs
        return scaling * product_of('thd,the->hde', mask_one[:, None, None] * slab_q.astype(jnp.float32), slab_g)
    head_states = lax.map(head_terms, (first_masks, queries, grads_in)) + end_flags[:, None, None, None] * slot_grads[:, 0]

    def reverse_chain(running, inputs):
        head_state, end_flag = inputs
        return (head_state + (1.0 - end_flag) * running, running)
    unused_right, from_right = lax.scan(reverse_chain, zero_state, (head_states, end_flags), reverse=True)
    right_states = jnp.concatenate([slot_grads, (cont_rights[:, None, None, None] * from_right)[:, None]], axis=1).astype(jnp.bfloat16)
    incoming_bf = incoming_first.astype(jnp.bfloat16)

    def prompt_backward(inputs):
        segment, masks_one, mask_first, slab_q, slab_k, slab_v, slab_g, incoming_one, right_one = inputs
        tok_pos = jnp.arange(P_DEV, dtype=jnp.int32)
        same_prompt = jnp.logical_and(segment[:, None] == segment[None, :], tok_pos[None, :] <= tok_pos[:, None])
        attn_prompt = jnp.where(same_prompt[None], product_of('thd,shd->hts', slab_q, slab_k), 0.0).astype(jnp.bfloat16)
        grad_prompt = jnp.where(same_prompt[None], product_of('the,she->hts', slab_g, slab_v), 0.0).astype(jnp.bfloat16)
        grad_q = scaling * (product_of('hts,shd->thd', grad_prompt, slab_k) + mask_first[:, None, None] * product_of('the,hde->thd', slab_g, incoming_one))
        grad_k = scaling * product_of('hts,thd->shd', grad_prompt, slab_q) + product_of('mshe,mhde->shd', masks_one[:, :, None, None] * slab_v[None].astype(jnp.float32), right_one)
        grad_v = scaling * product_of('hts,the->she', attn_prompt, slab_g) + product_of('mshd,mhde->she', masks_one[:, :, None, None] * slab_k[None].astype(jnp.float32), right_one)
        return (grad_q.astype(jnp.bfloat16), grad_k.astype(jnp.bfloat16), grad_v.astype(jnp.bfloat16))
    prompt_dq, prompt_dk, prompt_dv = lax.map(prompt_backward, (segments, row_masks, first_masks, queries, keys_in, values_in, grads_in, incoming_bf, right_states))
    return (prompt_dq.reshape(TOTAL, HEADS * E), prompt_dk.reshape(TOTAL, HEADS * E), prompt_dv.reshape(TOTAL, HEADS * E), cand_dq.reshape(CTOTAL, HEADS * E), cand_dk.reshape(CTOTAL, HEADS * E), cand_dv.reshape(CTOTAL, HEADS * E), list_loss)
```

```python
import math

import jax
import jax.numpy as jnp
from jax import lax
from jax.sharding import PartitionSpec as P

E = 128
ENDS = 2


grad_scale = 1048576.0


def prefix(part, axis, combine, identity, reverse):
    count = lax.axis_size(axis)
    place = lax.axis_index(axis)
    ahead = count - 1 - place if reverse else place
    gathered = jax.tree.map(lambda a: lax.all_gather(a, axis), part)
    state = jax.tree.map(lambda a, e: jnp.zeros_like(a) + jnp.asarray(e, a.dtype), part, identity)

    def one(lap, state):
        source = count - 1 - lap if reverse else lap
        return combine(
            state, jax.tree.map(lambda a: lax.dynamic_index_in_dim(a, source, 0, False), gathered)
        )

    return lax.fori_loop(0, ahead, one, state)


def pick_value(table, wanted):
    spots = jnp.arange(table.shape[0], dtype=jnp.int32)
    return jnp.sum(jnp.where(spots == wanted, table, 0))


def slab_layout(prompt_ends, slab_index, slab_width, slot_count):
    prompt_count = prompt_ends.shape[0]
    slab_start = slab_index * slab_width
    position = slab_start + jnp.arange(slab_width, dtype=jnp.int32)
    segment = jnp.sum((prompt_ends[None, :] <= position[:, None]).astype(jnp.int32), axis=1)
    begins = jnp.logical_or(slab_index == 0, jnp.any(prompt_ends == slab_start))
    first_seg = segment[0]
    last_seg = segment[slab_width - 1]
    first_end = jnp.sum((prompt_ends <= slab_start).astype(jnp.int32))
    slot_pid = first_end + jnp.arange(slot_count, dtype=jnp.int32)
    prompt_ids = jnp.arange(prompt_count, dtype=jnp.int32)
    slot_end = jnp.sum(
        jnp.where(prompt_ids[None, :] == slot_pid[:, None], prompt_ends[None, :], 0), axis=1
    )
    slot_valid = jnp.logical_and(slot_pid < prompt_count, slot_end <= slab_start + slab_width)
    slot_masks = jnp.logical_and(segment[None, :] == slot_pid[:, None], slot_valid[:, None])
    row_masks = jnp.concatenate([slot_masks, (segment == last_seg)[None, :]], axis=0)
    start_flag = jnp.logical_or(begins, first_seg != last_seg).astype(jnp.float32)
    end_flag = slot_valid[0].astype(jnp.float32)
    cont_right = (pick_value(prompt_ends, last_seg) != slab_start + slab_width).astype(jnp.float32)
    contin = 1.0 - begins.astype(jnp.float32)
    first_mask = segment == first_seg
    from_first = jnp.logical_and(slot_pid == first_seg, slot_valid).astype(jnp.float32)
    return (
        segment,
        row_masks,
        first_mask,
        contin,
        from_first,
        slot_pid,
        slot_valid,
        start_flag,
        end_flag,
        cont_right,
    )


def slot_rows(row_ids, prompt_ends, slab_width, slot_count):
    prompt_count = prompt_ends.shape[0]
    device_of = row_ids // slot_count
    slot_of = row_ids % slot_count
    first_end = jnp.sum(
        (prompt_ends[None, :] <= (device_of * slab_width)[:, None]).astype(jnp.int32), axis=1
    )
    row_pid = first_end + slot_of
    prompt_ids = jnp.arange(prompt_count, dtype=jnp.int32)
    row_end = jnp.sum(
        jnp.where(prompt_ids[None, :] == row_pid[:, None], prompt_ends[None, :], 0), axis=1
    )
    row_valid = jnp.logical_and(row_pid < prompt_count, row_end <= (device_of + 1) * slab_width)
    return (row_pid, row_valid)


def chain_combine(earlier, later):
    return (later[0] + (1.0 - later[1]) * earlier[0], jnp.maximum(earlier[1], later[1]))


def listwise(raw_scores, cand_prompt, cand_ranks, prompt_count):
    squashed = 3.0 * jnp.tanh(raw_scores)
    same_group = (cand_prompt[:, None] == cand_prompt[None, :]).astype(jnp.float32)
    exp_scores = jnp.exp(squashed)
    denoms = jnp.sum(same_group * exp_scores[None, :], axis=1)
    rank_weight = jnp.exp(-cand_ranks.astype(jnp.float32))
    targets = rank_weight / jnp.sum(same_group * rank_weight[None, :], axis=1)
    list_loss = -jnp.sum(targets * (squashed - jnp.log(denoms))) / prompt_count
    tanh_raw = jnp.tanh(raw_scores)
    raw_grad = (
        grad_scale
        / prompt_count
        * (exp_scores / denoms - targets)
        * 3.0
        * (1.0 - tanh_raw * tanh_raw)
    )
    return (list_loss, raw_grad)


def per_device(
    prompt_q,
    prompt_k,
    prompt_v,
    prompt_grad,
    cand_q,
    cand_k,
    cand_v,
    readout,
    prompt_ends,
    cand_lengths,
    cand_prompt,
    cand_ranks,
):
    slab_width = prompt_q.shape[0]
    cand_width = cand_q.shape[0]
    local_heads = prompt_q.shape[1] // E
    slab_count = lax.axis_size("seq")
    slab_index = lax.axis_index("seq")
    cand_count = cand_prompt.shape[0]
    per_slab = cand_lengths.shape[1]
    prompt_count = prompt_ends.shape[0]
    slot_count = ENDS
    scaling = 1.0 / math.sqrt(E * slab_width)
    queries = prompt_q.reshape(slab_width, local_heads, E)
    keys_in = prompt_k.reshape(slab_width, local_heads, E)
    values_in = prompt_v.reshape(slab_width, local_heads, E)
    grads_in = prompt_grad.reshape(slab_width, local_heads, E)
    cand_queries = cand_q.reshape(cand_width, local_heads, E)
    cand_keys = cand_k.reshape(cand_width, local_heads, E)
    cand_values = cand_v.reshape(cand_width, local_heads, E)
    readout_heads = readout.reshape(local_heads, E)
    (
        segment,
        row_masks,
        first_mask,
        contin,
        from_first,
        slot_pid,
        slot_valid,
        start_flag,
        end_flag,
        cont_right,
    ) = slab_layout(prompt_ends, slab_index, slab_width, slot_count)
    mask_rows = row_masks.astype(jnp.bfloat16)
    masked_keys = mask_rows[:, :, None, None] * keys_in[None]
    masked_values = mask_rows[:, :, None, None] * values_in[None]
    slab_sums = jnp.einsum(
        "mthd,the->mhde", masked_keys, values_in, preferred_element_type=jnp.float32
    )
    tail_state = slab_sums[slot_count]
    zero_state = jnp.zeros_like(tail_state)
    valid_float = slot_valid.astype(jnp.float32)
    lengths = cand_lengths[0]
    spots = jnp.arange(per_slab, dtype=jnp.int32)
    bounds = jnp.sum(jnp.where(spots[None, :] <= spots[:, None], lengths[None, :], 0), axis=1)
    tok_pos = jnp.arange(cand_width, dtype=jnp.int32)
    cand_id = jnp.sum((bounds[None, :] <= tok_pos[:, None]).astype(jnp.int32), axis=1)
    cand_masks = cand_id[None, :] == jnp.arange(per_slab, dtype=jnp.int32)[:, None]
    cand_float = cand_masks.astype(jnp.float32)
    cand_bf = cand_masks.astype(jnp.bfloat16)
    same_cand = jnp.logical_and(
        cand_id[:, None] == cand_id[None, :], tok_pos[None, :] <= tok_pos[:, None]
    )
    own_prompts = lax.dynamic_slice_in_dim(cand_prompt, slab_index * per_slab, per_slab)
    incoming, unused_flag = prefix(
        (tail_state, start_flag),
        "seq",
        chain_combine,
        (zero_state, jnp.zeros((), jnp.float32)),
        False,
    )
    incoming_first = contin * incoming
    end_slots = (
        slab_sums[:slot_count] + from_first[:, None, None, None] * incoming_first[None]
    ) * valid_float[:, None, None, None]
    shard_rows = lax.all_gather(end_slots.astype(jnp.bfloat16), "seq", axis=0, tiled=True)
    row_ids = jnp.arange(shard_rows.shape[0], dtype=jnp.int32)
    row_pid, row_valid = slot_rows(row_ids, prompt_ends, slab_width, slot_count)
    matches = jnp.logical_and(own_prompts[:, None] == row_pid[None, :], row_valid[None, :]).astype(
        jnp.bfloat16
    )
    cand_states = jnp.einsum(
        "jr,rhde->jhde", matches, shard_rows, preferred_element_type=jnp.float32
    ).astype(jnp.bfloat16)
    qk_scores = jnp.einsum(
        "thd,shd->hts", cand_queries, cand_keys, preferred_element_type=jnp.float32
    )
    attn_weights = jnp.where(same_cand[None], qk_scores, 0.0).astype(jnp.bfloat16)
    masked_queries = cand_bf[:, :, None, None] * cand_queries[None]
    outputs = scaling * (
        jnp.einsum("hts,she->the", attn_weights, cand_values, preferred_element_type=jnp.float32)
        + jnp.einsum(
            "jthd,jhde->the", masked_queries, cand_states, preferred_element_type=jnp.float32
        )
    )
    token_score = jnp.sum(jax.nn.silu(outputs) * readout_heads[None], axis=(1, 2))
    partial_raw = jnp.sum(cand_float * token_score[None, :], axis=1) / lengths.astype(jnp.float32)
    all_slots = jnp.arange(cand_count, dtype=jnp.int32)
    placed = jnp.where(all_slots // per_slab == slab_index, jnp.tile(partial_raw, slab_count), 0.0)
    raw_scores = lax.psum(placed, ("seq", "head"))
    list_loss, raw_grad = listwise(raw_scores, cand_prompt, cand_ranks, prompt_count)
    own_grad = lax.dynamic_slice_in_dim(raw_grad, slab_index * per_slab, per_slab) / lengths.astype(
        jnp.float32
    )
    token_coef = jnp.sum(cand_float * own_grad[:, None], axis=0)
    sigma = jax.nn.sigmoid(outputs)
    out_grad = (
        token_coef[:, None, None] * readout_heads[None] * sigma * (1.0 + outputs * (1.0 - sigma))
    ).astype(jnp.bfloat16)
    gv_scores = jnp.einsum(
        "the,she->hts", out_grad, cand_values, preferred_element_type=jnp.float32
    )
    grad_weights = jnp.where(same_cand[None], gv_scores, 0.0).astype(jnp.bfloat16)
    masked_grads = cand_bf[:, :, None, None] * out_grad[None]
    cand_dq = scaling * (
        jnp.einsum("hts,shd->thd", grad_weights, cand_keys, preferred_element_type=jnp.float32)
        + jnp.einsum(
            "jthe,jhde->thd", masked_grads, cand_states, preferred_element_type=jnp.float32
        )
    )
    cand_dk = scaling * jnp.einsum(
        "hts,thd->shd", grad_weights, cand_queries, preferred_element_type=jnp.float32
    )
    cand_dv = scaling * jnp.einsum(
        "hts,the->she", attn_weights, out_grad, preferred_element_type=jnp.float32
    )
    state_grads = (
        scaling
        * jnp.einsum("jthd,the->jhde", masked_queries, out_grad, preferred_element_type=jnp.float32)
    ).astype(jnp.bfloat16)
    matches = jnp.logical_and(
        slot_pid[:, None] == cand_prompt[None, :], slot_valid[:, None]
    ).astype(jnp.bfloat16)
    slot_grads = jnp.einsum(
        "kr,rhde->khde",
        matches,
        lax.all_gather(state_grads, "seq", axis=0, tiled=True),
        preferred_element_type=jnp.float32,
    )
    slot_grads = slot_grads * valid_float[:, None, None, None]
    first_bf = first_mask.astype(jnp.bfloat16)
    head_state = (
        scaling
        * jnp.einsum(
            "thd,the->hde",
            first_bf[:, None, None] * queries,
            grads_in,
            preferred_element_type=jnp.float32,
        )
        + end_flag * slot_grads[0]
    )
    from_right, unused_back = prefix(
        (head_state, end_flag), "seq", chain_combine, (zero_state, jnp.zeros((), jnp.float32)), True
    )
    right_states = jnp.concatenate([slot_grads, (cont_right * from_right)[None]], axis=0).astype(
        jnp.bfloat16
    )
    incoming_bf = incoming_first.astype(jnp.bfloat16)
    slab_pos = jnp.arange(slab_width, dtype=jnp.int32)
    same_prompt = jnp.logical_and(
        segment[:, None] == segment[None, :], slab_pos[None, :] <= slab_pos[:, None]
    )
    attn_prompt = jnp.where(
        same_prompt[None],
        jnp.einsum("thd,shd->hts", queries, keys_in, preferred_element_type=jnp.float32),
        0.0,
    ).astype(jnp.bfloat16)
    grad_prompt = jnp.where(
        same_prompt[None],
        jnp.einsum("the,she->hts", grads_in, values_in, preferred_element_type=jnp.float32),
        0.0,
    ).astype(jnp.bfloat16)
    first_float = first_mask.astype(jnp.float32)
    prompt_dq = scaling * (
        jnp.einsum("hts,shd->thd", grad_prompt, keys_in, preferred_element_type=jnp.float32)
        + first_float[:, None, None]
        * jnp.einsum("the,hde->thd", grads_in, incoming_bf, preferred_element_type=jnp.float32)
    )
    prompt_dk = scaling * jnp.einsum(
        "hts,thd->shd", grad_prompt, queries, preferred_element_type=jnp.float32
    ) + jnp.einsum(
        "mshe,mhde->shd", masked_values, right_states, preferred_element_type=jnp.float32
    )
    prompt_dv = scaling * jnp.einsum(
        "hts,the->she", attn_prompt, grads_in, preferred_element_type=jnp.float32
    ) + jnp.einsum("mshd,mhde->she", masked_keys, right_states, preferred_element_type=jnp.float32)
    flat_width = local_heads * E
    return (
        prompt_dq.astype(jnp.bfloat16).reshape(slab_width, flat_width),
        prompt_dk.astype(jnp.bfloat16).reshape(slab_width, flat_width),
        prompt_dv.astype(jnp.bfloat16).reshape(slab_width, flat_width),
        cand_dq.astype(jnp.bfloat16).reshape(cand_width, flat_width),
        cand_dk.astype(jnp.bfloat16).reshape(cand_width, flat_width),
        cand_dv.astype(jnp.bfloat16).reshape(cand_width, flat_width),
        list_loss,
    )


def solution(mesh):
    return jax.shard_map(
        per_device,
        mesh=mesh,
        in_specs=(
            P("seq", "head"),
            P("seq", "head"),
            P("seq", "head"),
            P("seq", "head"),
            P("seq", "head"),
            P("seq", "head"),
            P("seq", "head"),
            P("head"),
            P(),
            P("seq", None),
            P(),
            P(),
        ),
        out_specs=(
            P("seq", "head"),
            P("seq", "head"),
            P("seq", "head"),
            P("seq", "head"),
            P("seq", "head"),
            P("seq", "head"),
            P(),
        ),
        check_vma=False,
    )
```

```python
import math

import jax
import jax.numpy as jnp
from jax import lax
from jax.experimental import pallas as pl
from jax.experimental.pallas import tpu as pltpu
from jax.sharding import PartitionSpec as P

E = 128
ENDS = 2
PIECES = ENDS + 1
STRIP = 256
grad_scale = 1048576.0
f32 = jnp.float32
bf16 = jnp.bfloat16
SMEM = pl.BlockSpec(memory_space=pltpu.SMEM)
VMEM = pl.BlockSpec(memory_space=pltpu.VMEM)


def dot(a, b, ca, cb):
    return lax.dot_general(a, b, (((ca,), (cb,)), ((), ())), preferred_element_type=f32)


def call(body, **kw):
    return pl.pallas_call(
        body,
        compiler_params=pltpu.CompilerParams(vmem_limit_bytes=48 * 1024 * 1024),
        **kw,
    )


def count_ends(ends, limit):
    total = jnp.int32(0)
    for p in range(ends.shape[0]):
        total += (ends[p] <= limit).astype(jnp.int32)
    return total


def end_of(ends, pid, none):
    last = ends.shape[0] - 1
    return jnp.where(pid <= last, ends[jnp.minimum(pid, last)], none)


def slab_bounds(ends, slab, width):
    start = slab * width
    first = count_ends(ends, start)
    far = start + width
    return [jnp.minimum(end_of(ends, first + m, far) - start, width) for m in range(ENDS)]


def pick_rows(rows, bounds, options):
    out = options[-1]
    for b, o in zip(reversed(bounds), reversed(options[:-1])):
        out = jnp.where(rows < b, o, out)
    return out


def rows_of(shape, start=0):
    return lax.broadcasted_iota(jnp.int32, shape, 0) + start


def strip_mask(lo, size, width, bounds):
    s = rows_of((size, 1), lo)
    t = lax.broadcasted_iota(jnp.int32, (size, width - lo), 1) + lo
    stop = pick_rows(s, bounds, [jnp.full((size, 1), b, jnp.int32) for b in bounds] + [width])
    return jnp.logical_and(t >= s, t < stop)


def store_parts(out, place, mat):
    parts, rows = out.shape[0], out.shape[2]
    for o in range(parts):
        out[o, place] = mat[o * rows : (o + 1) * rows].astype(bf16)


def load_matrix(ref, place):
    return jnp.concatenate([ref[o, place] for o in range(ref.shape[0])], axis=0)


def sums_kernel(ends, q, k, v, g, out):
    width = q.shape[0]
    bounds = slab_bounds(ends, lax.axis_index("seq"), width)
    scaling = 1.0 / math.sqrt(E * width)
    rows = rows_of((width, E))
    zero = jnp.zeros((width, E), f32)
    values = v[...].astype(f32)
    pieces = []
    low = 0
    for b in bounds + [width]:
        inside = jnp.logical_and(rows >= low, rows < b)
        pieces.append(jnp.where(inside, values, zero).astype(bf16))
        low = b
    sums = dot(k[...], jnp.concatenate(pieces, axis=1), 0, 0)
    for m in range(PIECES):
        store_parts(out, m, sums[:, m * E : (m + 1) * E])
    first = jnp.where(rows < bounds[0], g[...].astype(f32), zero).astype(bf16)
    store_parts(out, PIECES, scaling * dot(q[...], first, 0, 0))


def chain_kernel(ends, cand_prompt, parts, out, held, *, width):
    count = parts.shape[0]
    per_slab = cand_prompt.shape[0] // count
    running = jnp.zeros(parts.shape[2:], f32)
    for e in range(count):
        start = e * width
        first = count_ends(ends, start)
        last = count_ends(ends, start + width - 1)
        begins = jnp.bool_(True) if e == 0 else ends[jnp.maximum(first - 1, 0)] == start
        if e > 0:
            begins = jnp.logical_and(first > 0, begins)
        incoming = jnp.where(begins, 0.0, running)
        out[e, per_slab] = incoming.astype(bf16)
        firsts = parts[e, 0].astype(f32) + incoming
        second = parts[e, 1].astype(f32)
        third = parts[e, 2].astype(f32)
        spare = ends.shape[0]
        for m, piece in enumerate((firsts, second)):
            ended = end_of(ends, first + m, start + width + 1) <= start + width
            held[jnp.where(ended, first + m, spare)] = piece
        running = jnp.where(last == first, firsts, jnp.where(last == first + 1, second, third))
    for c in range(cand_prompt.shape[0]):
        out[c // per_slab, c % per_slab] = held[cand_prompt[c]].astype(bf16)


def inside_kernel(lengths, q, k, v, out):
    width = q.shape[0]
    bounds = cand_bounds(lengths)
    for lo in range(0, width, STRIP):
        hi = lo + STRIP
        scores = dot(q[lo:hi], k[:hi], 1, 1)
        t = rows_of((STRIP, hi), lo)
        s = lax.broadcasted_iota(jnp.int32, (STRIP, hi), 1)
        begin = pick_rows(t[:, :1], bounds, [0] + [jnp.full((STRIP, 1), b, jnp.int32) for b in bounds])
        keep = jnp.logical_and(s <= t, s >= begin)
        out[lo:hi] = dot(jnp.where(keep, scores, 0.0).astype(bf16), v[:hi], 1, 0)


def cand_bounds(lengths):
    bounds = []
    total = jnp.int32(0)
    for j in range(lengths.shape[1] - 1):
        total += lengths[0, j]
        bounds.append(total)
    return bounds


def scores_kernel(lengths, q, inside, readout, states, slope_out, raw_out, grads_out, *, scaling):
    h = pl.program_id(0)
    width = q.shape[0]
    per_slab = lengths.shape[1]
    bounds = cand_bounds(lengths)
    rows = rows_of((width, E))
    wide = jnp.concatenate([load_matrix(states, j) for j in range(per_slab)], axis=1)
    crossed = dot(q[...], wide, 1, 0)
    crossed = pick_rows(rows, bounds, [crossed[:, j * E : (j + 1) * E] for j in range(per_slab)])
    out = scaling * (inside[...] + crossed)
    inverse = [1.0 / jnp.full((1, E), lengths[0, j], jnp.int32).astype(f32) for j in range(per_slab)]
    weight = pick_rows(rows, bounds, inverse) * readout[...]
    sigma = jax.nn.sigmoid(out)
    silu = out * sigma * weight
    slope = weight * sigma * (1.0 + out * (1.0 - sigma))
    slope_out[...] = slope
    zero = jnp.zeros((width, E), f32)
    masked = []
    totals = []
    low = 0
    for b in bounds + [width]:
        mine = jnp.logical_and(rows >= low, rows < b)
        masked.append(jnp.where(mine, slope, zero).astype(bf16))
        column = jnp.sum(jnp.where(mine, silu, zero), axis=0, keepdims=True)
        totals.append(jnp.broadcast_to(jnp.sum(column, axis=1, keepdims=True), (1, E)))
        low = b
    grads = scaling * dot(q[...], jnp.concatenate(masked, axis=1), 0, 0)
    for j in range(per_slab):
        store_parts(grads_out, j, grads[:, j * E : (j + 1) * E])
    spare = jnp.zeros((8 - per_slab, E), f32)
    tile = jnp.concatenate(totals + [spare], axis=0)

    @pl.when(h == 0)
    def _():
        raw_out[...] = jnp.broadcast_to(tile[None], raw_out.shape)

    @pl.when(h > 0)
    def _():
        raw_out[...] += jnp.broadcast_to(tile[None], raw_out.shape)


def listwise_kernel(
    ends,
    prompts,
    prompt_row,
    rank_row,
    raws,
    grads,
    parts,
    out,
    coef_out,
    loss_out,
    raw_held,
    coef_held,
    held,
    *,
    width,
):
    count = grads.shape[0]
    per_slab = grads.shape[1]
    groups = raws.shape[0] // count
    cands = count * per_slab
    prompt_count = ends.shape[0]
    for e in range(count):
        total = raws[e * groups, :per_slab]
        for i in range(1, groups):
            total += raws[e * groups + i, :per_slab]
        raw_held[e * per_slab : (e + 1) * per_slab] = total
    raw = raw_held[...]
    square = (cands, cands)
    down = lax.broadcasted_iota(jnp.int32, square, 0)
    across = lax.broadcasted_iota(jnp.int32, square, 1)
    same_spot = down == across
    own = jnp.broadcast_to(prompt_row[...], square)
    own_down = jnp.sum(jnp.where(same_spot, own, 0.0), axis=1, keepdims=True)
    group = own == own_down
    rank_weight = jnp.broadcast_to(jnp.exp(-rank_row[...]), square)
    rank_down = jnp.sum(jnp.where(same_spot, rank_weight, 0.0), axis=1, keepdims=True)
    target = rank_down / jnp.sum(jnp.where(group, rank_weight, 0.0), axis=1, keepdims=True)
    tanh_raw = jnp.tanh(raw)
    squashed = 3.0 * tanh_raw
    exp_scores = jnp.exp(squashed)
    exp_across = jnp.sum(jnp.where(same_spot, exp_scores[:, :cands], 0.0), axis=0, keepdims=True)
    denom = jnp.sum(jnp.where(group, jnp.broadcast_to(exp_across, square), 0.0), axis=1, keepdims=True)
    terms = target * (squashed - jnp.log(denom))
    loss_out[...] = -jnp.sum(terms, axis=0, keepdims=True) / prompt_count
    coef = grad_scale / prompt_count * (exp_scores / denom - target) * 3.0 * (1.0 - tanh_raw * tanh_raw)
    coef_held[...] = coef
    me = lax.axis_index("seq")
    for j in range(per_slab):
        coef_out[j : j + 1] = coef_held[pl.ds(me * per_slab + j, 1)]
    held[...] = jnp.zeros_like(held)
    for c in range(cands):
        piece = grads[c // per_slab, c % per_slab].astype(f32) * coef[c : c + 1]
        held[prompts[c]] += piece.astype(bf16).astype(f32)
    running = jnp.zeros(parts.shape[2:], f32)
    for e in reversed(range(count)):
        start = e * width
        far = start + width
        first = count_ends(ends, start)
        last = count_ends(ends, far - 1)
        goes_on = ends[last] != far
        from_right = jnp.where(goes_on, running, 0.0)
        from_right_bf = from_right.astype(bf16)
        for m in range(ENDS):
            pid = first + m
            ended = end_of(ends, pid, far + 1) <= far
            here = held[jnp.minimum(pid, prompt_count - 1)]
            out[e, m] = jnp.where(ended, here, from_right).astype(bf16)
            if m == 0:
                running = parts[e, PIECES].astype(f32) + jnp.where(ended, here, running)
        out[e, ENDS] = from_right_bf


def cand_kernel(lengths, coef, q, k, v, slope, states, dq, dk, dv, *, scaling):
    width = q.shape[0]
    per_slab = lengths.shape[1]
    bounds = cand_bounds(lengths)
    rows = rows_of((width, E))
    dout = (pick_rows(rows, bounds, [coef[j : j + 1] for j in range(per_slab)]) * slope[...]).astype(bf16)
    wide = jnp.concatenate([load_matrix(states, j) for j in range(per_slab)], axis=0)
    crossed = dot(dout, wide, 1, 1)
    total = pick_rows(rows, bounds, [crossed[:, j * E : (j + 1) * E] for j in range(per_slab)])
    blocks = []
    for lo in range(0, width, STRIP):
        hi = lo + STRIP
        keep = strip_mask(lo, STRIP, width, bounds)
        keys = k[lo:hi]
        attn = jnp.where(keep, dot(keys, q[lo:], 1, 1), 0.0).astype(bf16)
        gw = jnp.where(keep, dot(v[lo:hi], dout[lo:], 1, 1), 0.0).astype(bf16)
        dk[lo:hi] = (scaling * dot(gw, q[lo:], 1, 0)).astype(bf16)
        dv[lo:hi] = (scaling * dot(attn, dout[lo:], 1, 0)).astype(bf16)
        total = total + dot(gw, keys, 0, 0)
        blocks.append((lo, hi, total[:STRIP]))
        total = total[STRIP:]
    for lo, hi, block in blocks:
        dq[lo:hi] = (scaling * block).astype(bf16)


def prompt_kernel(ends, q, k, v, g, dq, dk, dv):
    width = q.shape[0]
    scaling = 1.0 / math.sqrt(E * width)
    bounds = slab_bounds(ends, lax.axis_index("seq"), width)
    for lo in range(0, width, STRIP):
        hi = lo + STRIP
        keep = strip_mask(lo, STRIP, width, bounds)
        keys = k[lo:hi]
        attn = jnp.where(keep, dot(keys, q[lo:], 1, 1), 0.0).astype(bf16)
        gw = jnp.where(keep, dot(v[lo:hi], g[lo:], 1, 1), 0.0).astype(bf16)
        dk[lo:hi] = scaling * dot(gw, q[lo:], 1, 0)
        dv[lo:hi] = scaling * dot(attn, g[lo:], 1, 0)
        part = dot(gw, keys, 0, 0)
        if lo == 0:
            dq[...] = part
        else:
            dq[lo:] += part


def query_kernel(ends, part, g, states, dq):
    width = g.shape[0]
    scaling = 1.0 / math.sqrt(E * width)
    bounds = slab_bounds(ends, lax.axis_index("seq"), width)
    carry = load_matrix(states, states.shape[1] - 1)
    crossed = dot(g[...], carry, 1, 1)
    rows = rows_of((width, E))
    dq[...] = (scaling * (part[...] + jnp.where(rows < bounds[0], crossed, 0.0))).astype(bf16)


def right_kernel(ends, dk_part, dv_part, k, v, states, dk, dv):
    width = k.shape[0]
    bounds = slab_bounds(ends, lax.axis_index("seq"), width)
    rows = rows_of((width, E))
    mats = [load_matrix(states, m) for m in range(PIECES)]
    by_v = dot(v[...], jnp.concatenate(mats, axis=0), 1, 1)
    by_k = dot(k[...], jnp.concatenate(mats, axis=1), 1, 0)
    cut = lambda a: [a[:, m * E : (m + 1) * E] for m in range(PIECES)]
    dk[...] = (dk_part[...] + pick_rows(rows, bounds, cut(by_v))).astype(bf16)
    dv[...] = (dv_part[...] + pick_rows(rows, bounds, cut(by_k))).astype(bf16)


def exchange(a):
    return lax.all_to_all(a, "seq", 0, 0, tiled=True)


def per_device(
    prompt_q,
    prompt_k,
    prompt_v,
    prompt_grad,
    cand_q,
    cand_k,
    cand_v,
    readout,
    prompt_ends,
    cand_lengths,
    cand_prompt,
    cand_ranks,
):
    width = prompt_q.shape[0]
    cand_width = cand_q.shape[0]
    flat = prompt_q.shape[1]
    heads = flat // E
    count = lax.axis_size("seq")
    groups = lax.axis_size("head")
    per_slab = cand_lengths.shape[1]
    cands = cand_prompt.shape[0]
    scaling = 1.0 / math.sqrt(E * width)
    rows = flat // count
    share = count // heads
    whole = pl.BlockSpec((width, E), lambda h: (0, h))
    cand_block = pl.BlockSpec((cand_width, E), lambda h: (0, h))
    like = jax.ShapeDtypeStruct

    def parts_block(n):
        return pl.BlockSpec((share, n, rows, E), lambda h: (h, 0, 0, 0))

    pieces = call(
        sums_kernel,
        grid=(heads,),
        in_specs=[SMEM] + [whole] * 4,
        out_specs=parts_block(PIECES + 1),
        out_shape=like((count, PIECES + 1, rows, E), bf16),
        name="sums",
    )(prompt_ends, prompt_q, prompt_k, prompt_v, prompt_grad)
    parts = exchange(pieces)

    dq_part, dk_part, dv_part = call(
        prompt_kernel,
        grid=(heads,),
        in_specs=[SMEM] + [whole] * 4,
        out_specs=[whole] * 3,
        out_shape=[like((width, flat), f32)] * 3,
        name="prompt",
    )(prompt_ends, prompt_q, prompt_k, prompt_v, prompt_grad)

    chained = call(
        lambda *refs: chain_kernel(*refs, width=width),
        in_specs=[SMEM, SMEM, VMEM],
        out_specs=VMEM,
        out_shape=like((count, per_slab + 1, rows, E), bf16),
        scratch_shapes=[pltpu.VMEM((prompt_ends.shape[0] + 1, rows, E), f32)],
        name="chain",
    )(prompt_ends, cand_prompt, parts)
    states = exchange(chained)

    inside = call(
        inside_kernel,
        grid=(heads,),
        in_specs=[SMEM] + [cand_block] * 3,
        out_specs=cand_block,
        out_shape=like((cand_width, flat), f32),
        name="inside",
    )(cand_lengths, cand_q, cand_k, cand_v)

    slope, raw, grads = call(
        lambda *refs: scores_kernel(*refs, scaling=scaling),
        grid=(heads,),
        in_specs=[
            SMEM,
            cand_block,
            cand_block,
            pl.BlockSpec((1, E), lambda h: (0, h)),
            parts_block(per_slab + 1),
        ],
        out_specs=[
            cand_block,
            pl.BlockSpec((count * groups, 8, E), lambda h: (0, 0, 0)),
            parts_block(per_slab),
        ],
        out_shape=[
            like((cand_width, flat), f32),
            like((count * groups, 8, E), f32),
            like((count, per_slab, rows, E), bf16),
        ],
        name="scores",
    )(cand_lengths, cand_q, inside, readout.reshape(1, flat), states)
    raws = lax.all_to_all(raw, ("seq", "head"), 0, 0, tiled=True)
    all_grads = exchange(grads)

    prompt_dq = call(
        query_kernel,
        grid=(heads,),
        in_specs=[SMEM, whole, whole, parts_block(per_slab + 1)],
        out_specs=whole,
        out_shape=like((width, flat), bf16),
        name="query",
    )(prompt_ends, dq_part, prompt_grad, states)

    right, coef, loss = call(
        lambda *refs: listwise_kernel(*refs, width=width),
        in_specs=[SMEM, SMEM] + [VMEM] * 5,
        out_specs=[VMEM] * 3,
        out_shape=[
            like((count, PIECES, rows, E), bf16),
            like((8, E), f32),
            like((1, E), f32),
        ],
        scratch_shapes=[
            pltpu.VMEM((cands, E), f32),
            pltpu.VMEM((cands, E), f32),
            pltpu.VMEM((prompt_ends.shape[0], rows, E), f32),
        ],
        name="listwise",
    )(
        prompt_ends,
        cand_prompt,
        cand_prompt.astype(f32).reshape(1, cands),
        cand_ranks.astype(f32).reshape(1, cands),
        raws,
        all_grads,
        parts,
    )
    rights = exchange(right)

    cand_dq, cand_dk, cand_dv = call(
        lambda *refs: cand_kernel(*refs, scaling=scaling),
        grid=(heads,),
        in_specs=[SMEM, pl.BlockSpec((8, E), lambda h: (0, 0))]
        + [cand_block] * 4
        + [parts_block(per_slab + 1)],
        out_specs=[cand_block] * 3,
        out_shape=[like((cand_width, flat), bf16)] * 3,
        name="cand",
    )(cand_lengths, coef, cand_q, cand_k, cand_v, slope, states)

    prompt_dk, prompt_dv = call(
        right_kernel,
        grid=(heads,),
        in_specs=[SMEM] + [whole] * 4 + [parts_block(PIECES)],
        out_specs=[whole] * 2,
        out_shape=[like((width, flat), bf16)] * 2,
        name="right",
    )(prompt_ends, dk_part, dv_part, prompt_k, prompt_v, rights)
    return (
        prompt_dq,
        prompt_dk,
        prompt_dv,
        cand_dq,
        cand_dk,
        cand_dv,
        loss[0, 0],
    )


def solution(mesh):
    tile = P("seq", "head")
    return jax.shard_map(
        per_device,
        mesh=mesh,
        in_specs=(tile,) * 7 + (P("head"), P(), P("seq", None), P(), P()),
        out_specs=(tile,) * 6 + (P(),),
        check_vma=False,
    )
```

```python
import math

import jax
import jax.numpy as jnp
from jax import lax
from jax.experimental import pallas as pl
from jax.experimental.pallas import tpu as pltpu
from jax.sharding import PartitionSpec as P

E = 128
ENDS = 2
PIECES = ENDS + 1
STRIP = 256
grad_scale = 1048576.0
f32 = jnp.float32
bf16 = jnp.bfloat16
SMEM = pl.BlockSpec(memory_space=pltpu.SMEM)
VMEM = pl.BlockSpec(memory_space=pltpu.VMEM)
ANY = pl.BlockSpec(memory_space=pl.ANY)
SCORE_ROWS = 16
SCORE_PARTS = 3


def dot(a, b, ca, cb):
    return lax.dot_general(a, b, (((ca,), (cb,)), ((), ())), preferred_element_type=f32)


def call(body, **kw):
    return pl.pallas_call(
        body,
        compiler_params=pltpu.CompilerParams(vmem_limit_bytes=24 * 1024 * 1024),
        **kw,
    )


def count_ends(ends, limit):
    total = jnp.int32(0)
    for p in range(ends.shape[0]):
        total += (ends[p] <= limit).astype(jnp.int32)
    return total


def end_of(ends, pid, none):
    last = ends.shape[0] - 1
    return jnp.where(pid <= last, ends[jnp.minimum(pid, last)], none)


def slab_bounds(ends, slab, width):
    start = slab * width
    first = count_ends(ends, start)
    far = start + width
    return [jnp.minimum(end_of(ends, first + m, far) - start, width) for m in range(ENDS)]


def pick_rows(rows, bounds, options):
    out = options[-1]
    for b, o in zip(reversed(bounds), reversed(options[:-1])):
        out = jnp.where(rows < b, o, out)
    return out


def rows_of(shape, start=0):
    return lax.broadcasted_iota(jnp.int32, shape, 0) + start


def strip_mask(lo, size, width, bounds):
    s = rows_of((size, 1), lo)
    t = lax.broadcasted_iota(jnp.int32, (size, width - lo), 1) + lo
    stop = pick_rows(s, bounds, [jnp.full((size, 1), b, jnp.int32) for b in bounds] + [width])
    return jnp.logical_and(t >= s, t < stop)


def store_parts(out, place, mat):
    parts, rows = out.shape[0], out.shape[2]
    for o in range(parts):
        out[o, place] = mat[o * rows : (o + 1) * rows].astype(bf16)


def load_matrix(ref, place, h=0, share=None):
    share = ref.shape[0] if share is None else share
    return jnp.concatenate([ref[h * share + o, place] for o in range(share)], axis=0)


def sums_kernel(ends, q_in, k_in, v_in, g_in, out, q, k, v, g, sems):
    width, flat = q.shape
    heads = flat // E
    share = out.shape[0] // heads
    columns = [pl.ds(h * E, E) for h in range(heads)]
    copies = [
        [
            pltpu.make_async_copy(a.at[:, columns[h]], b.at[:, columns[h]], sems.at[h, i])
            for i, (a, b) in enumerate(((k_in, k), (v_in, v), (q_in, q), (g_in, g)))
        ]
        for h in range(heads)
    ]
    for group in copies:
        for c in group:
            c.start()
    bounds = slab_bounds(ends, lax.axis_index("seq"), width)
    scaling = 1.0 / math.sqrt(E * width)
    rows = rows_of((width, E))
    zero = jnp.zeros((width, E), f32)
    for h in range(heads):
        for c in copies[h]:
            c.wait()
        at = slice(h * E, (h + 1) * E)
        values = v[:, at].astype(f32)
        pieces = []
        low = 0
        for b in bounds + [width]:
            inside = jnp.logical_and(rows >= low, rows < b)
            pieces.append(jnp.where(inside, values, zero).astype(bf16))
            low = b
        sums = dot(k[:, at], jnp.concatenate(pieces, axis=1), 0, 0)
        mine = out.at[pl.ds(h * share, share)]
        for m in range(PIECES):
            store_parts(mine, m, sums[:, m * E : (m + 1) * E])
        first = jnp.where(rows < bounds[0], g[:, at].astype(f32), zero).astype(bf16)
        store_parts(mine, PIECES, scaling * dot(q[:, at], first, 0, 0))


def chain_kernel(ends, cand_prompt, parts, out, held, *, width):
    count = parts.shape[0]
    per_slab = cand_prompt.shape[0] // count
    running = jnp.zeros(parts.shape[2:], f32)
    for e in range(count):
        start = e * width
        first = count_ends(ends, start)
        last = count_ends(ends, start + width - 1)
        begins = jnp.bool_(True) if e == 0 else ends[jnp.maximum(first - 1, 0)] == start
        if e > 0:
            begins = jnp.logical_and(first > 0, begins)
        incoming = jnp.where(begins, 0.0, running)
        out[e, per_slab] = incoming.astype(bf16)
        firsts = parts[e, 0].astype(f32) + incoming
        second = parts[e, 1].astype(f32)
        third = parts[e, 2].astype(f32)
        spare = ends.shape[0]
        for m, piece in enumerate((firsts, second)):
            ended = end_of(ends, first + m, start + width + 1) <= start + width
            held[jnp.where(ended, first + m, spare)] = piece
        running = jnp.where(last == first, firsts, jnp.where(last == first + 1, second, third))
    for c in range(cand_prompt.shape[0]):
        out[c // per_slab, c % per_slab] = held[cand_prompt[c]].astype(bf16)


def inside_kernel(lengths, q, k, v, out):
    width = q.shape[0]
    bounds = cand_bounds(lengths)
    for lo in range(0, width, STRIP):
        hi = lo + STRIP
        scores = dot(q[lo:hi], k[:hi], 1, 1)
        t = rows_of((STRIP, hi), lo)
        s = lax.broadcasted_iota(jnp.int32, (STRIP, hi), 1)
        begin = pick_rows(t[:, :1], bounds, [0] + [jnp.full((STRIP, 1), b, jnp.int32) for b in bounds])
        keep = jnp.logical_and(s <= t, s >= begin)
        out[lo:hi] = dot(jnp.where(keep, scores, 0.0).astype(bf16), v[:hi], 1, 0)


def cand_bounds(lengths):
    bounds = []
    total = jnp.int32(0)
    for j in range(lengths.shape[1] - 1):
        total += lengths[0, j]
        bounds.append(total)
    return bounds


def scores_kernel(lengths, q, inside, readout, states, slope_out, raw_out, slope_far, sems, *, scaling):
    width, flat = q.shape
    heads = flat // E
    per_slab = lengths.shape[1]
    bounds = cand_bounds(lengths)
    rows = rows_of((width, E))
    zero = jnp.zeros((width, E), f32)
    inverse = [1.0 / jnp.full((1, E), lengths[0, j], jnp.int32).astype(f32) for j in range(per_slab)]
    totals = [jnp.zeros((1, E), f32) for j in range(per_slab)]
    copies = []
    for h in range(heads):
        at = slice(h * E, (h + 1) * E)
        wide = [load_matrix(states, j, h, states.shape[0] // heads) for j in range(per_slab)]
        crossed = dot(q[:, at], jnp.concatenate(wide, axis=1), 1, 0)
        crossed = pick_rows(rows, bounds, [crossed[:, j * E : (j + 1) * E] for j in range(per_slab)])
        out = scaling * (inside[:, at] + crossed)
        weight = pick_rows(rows, bounds, inverse) * readout[:, at]
        sigma = jax.nn.sigmoid(out)
        slope_out[:, at] = weight * sigma * (1.0 + out * (1.0 - sigma))
        columns = pl.ds(h * E, E)
        copies.append(pltpu.make_async_copy(slope_out.at[:, columns], slope_far.at[:, columns], sems.at[h]))
        copies[-1].start()
        silu = out * sigma * weight
        low = 0
        for j, b in enumerate(bounds + [width]):
            mine = jnp.logical_and(rows >= low, rows < b)
            totals[j] += jnp.sum(jnp.where(mine, silu, zero), axis=0, keepdims=True)
            low = b
    raw_out[...] = jnp.zeros_like(raw_out)
    for j in range(per_slab):
        raw_out[j : j + 1] = jnp.broadcast_to(jnp.sum(totals[j], axis=1, keepdims=True), (1, E))
    for c in copies:
        c.wait()


def grads_kernel(lengths, q, slope, *refs, scaling):
    raws, out = refs[:-1], refs[-1]
    width, flat = q.shape
    heads = flat // E
    count = out.shape[0]
    share = count // heads
    size = flat // count
    per_slab = lengths.shape[1]
    bounds = cand_bounds(lengths)
    rows = rows_of((width, E))
    zero = jnp.zeros((width, E), f32)
    for h in range(heads):
        at = slice(h * E, (h + 1) * E)
        mine = slope[:, at]
        high, low_part = [], []
        low = 0
        for b in bounds + [width]:
            kept = jnp.where(jnp.logical_and(rows >= low, rows < b), mine, zero)
            top = kept.astype(bf16)
            high.append(top)
            low_part.append((kept - top.astype(f32)).astype(bf16))
            low = b
        grads = dot(q[:, at], jnp.concatenate(high + low_part, axis=1), 0, 0)
        for j in range(per_slab):
            grad = grads[:, j * E : (j + 1) * E] + grads[:, (per_slab + j) * E : (per_slab + j + 1) * E]
            grad = (scaling * grad).astype(bf16)
            for o in range(share):
                out[h * share + o, j * size : (j + 1) * size] = grad[o * size : (o + 1) * size]
    total = raws[0][...]
    for r in raws[1:]:
        total += r[...]
    lines = []
    for j in range(per_slab):
        left = total[j : j + 1]
        for i in range(SCORE_PARTS):
            line = left.astype(bf16).astype(f32)
            lines.append(line)
            left = left - line
    lines.append(jnp.zeros((SCORE_ROWS - len(lines), E), f32))
    tile = jnp.concatenate(lines, axis=0).astype(bf16)
    for o in range(count):
        out[o, per_slab * size :] = tile


def listwise_kernel(
    ends,
    prompts,
    prompt_row,
    rank_row,
    grads,
    parts,
    out,
    coef_out,
    loss_out,
    raw_held,
    coef_held,
    held,
    *,
    width,
):
    count = grads.shape[0]
    size = parts.shape[2]
    per_slab = prompts.shape[0] // count
    cands = count * per_slab
    prompt_count = ends.shape[0]
    for e in range(count):
        tile = grads[e, per_slab * size :].astype(f32)
        for j in range(per_slab):
            total = tile[SCORE_PARTS * j : SCORE_PARTS * j + 1]
            for i in range(1, SCORE_PARTS):
                total = total + tile[SCORE_PARTS * j + i : SCORE_PARTS * j + i + 1]
            raw_held[e * per_slab + j : e * per_slab + j + 1] = total
    raw = raw_held[...]
    square = (cands, cands)
    down = lax.broadcasted_iota(jnp.int32, square, 0)
    across = lax.broadcasted_iota(jnp.int32, square, 1)
    same_spot = down == across
    own = jnp.broadcast_to(prompt_row[...].astype(f32), square)
    own_down = jnp.sum(jnp.where(same_spot, own, 0.0), axis=1, keepdims=True)
    group = own == own_down
    rank_weight = jnp.broadcast_to(jnp.exp(-rank_row[...].astype(f32)), square)
    rank_down = jnp.sum(jnp.where(same_spot, rank_weight, 0.0), axis=1, keepdims=True)
    target = rank_down / jnp.sum(jnp.where(group, rank_weight, 0.0), axis=1, keepdims=True)
    tanh_raw = jnp.tanh(raw)
    squashed = 3.0 * tanh_raw
    exp_scores = jnp.exp(squashed)
    exp_across = jnp.sum(jnp.where(same_spot, exp_scores[:, :cands], 0.0), axis=0, keepdims=True)
    denom = jnp.sum(jnp.where(group, jnp.broadcast_to(exp_across, square), 0.0), axis=1, keepdims=True)
    terms = target * (squashed - jnp.log(denom))
    loss_out[...] = -jnp.sum(terms, axis=0, keepdims=True) / prompt_count
    coef = grad_scale / prompt_count * (exp_scores / denom - target) * 3.0 * (1.0 - tanh_raw * tanh_raw)
    coef_held[...] = coef
    me = lax.axis_index("seq")
    for j in range(per_slab):
        coef_out[j : j + 1] = coef_held[pl.ds(me * per_slab + j, 1)]
    held[...] = jnp.zeros_like(held)
    for c in range(cands):
        j = c % per_slab
        held[prompts[c]] += grads[c // per_slab, j * size : (j + 1) * size].astype(f32) * coef[c : c + 1]
    running = jnp.zeros(parts.shape[2:], f32)
    for e in reversed(range(count)):
        start = e * width
        far = start + width
        first = count_ends(ends, start)
        last = count_ends(ends, far - 1)
        goes_on = ends[last] != far
        from_right = jnp.where(goes_on, running, 0.0)
        from_right_bf = from_right.astype(bf16)
        for m in range(ENDS):
            pid = first + m
            ended = end_of(ends, pid, far + 1) <= far
            here = held[jnp.minimum(pid, prompt_count - 1)]
            out[e, m] = jnp.where(ended, here, from_right).astype(bf16)
            if m == 0:
                running = parts[e, PIECES].astype(f32) + jnp.where(ended, here, running)
        out[e, ENDS] = from_right_bf


def cand_kernel(lengths, coef, q, k, v, slope, states, dq, dk, dv, *, scaling):
    width = q.shape[0]
    per_slab = lengths.shape[1]
    bounds = cand_bounds(lengths)
    rows = rows_of((width, E))
    dout = (pick_rows(rows, bounds, [coef[j : j + 1] for j in range(per_slab)]) * slope[...]).astype(bf16)
    wide = jnp.concatenate([load_matrix(states, j) for j in range(per_slab)], axis=0)
    crossed = dot(dout, wide, 1, 1)
    total = pick_rows(rows, bounds, [crossed[:, j * E : (j + 1) * E] for j in range(per_slab)])
    blocks = []
    for lo in range(0, width, STRIP):
        hi = lo + STRIP
        keep = strip_mask(lo, STRIP, width, bounds)
        keys = k[lo:hi]
        attn = jnp.where(keep, dot(keys, q[lo:], 1, 1), 0.0).astype(bf16)
        gw = jnp.where(keep, dot(v[lo:hi], dout[lo:], 1, 1), 0.0).astype(bf16)
        dk[lo:hi] = (scaling * dot(gw, q[lo:], 1, 0)).astype(bf16)
        dv[lo:hi] = (scaling * dot(attn, dout[lo:], 1, 0)).astype(bf16)
        total = total + dot(gw, keys, 0, 0)
        blocks.append((lo, hi, total[:STRIP]))
        total = total[STRIP:]
    for lo, hi, block in blocks:
        dq[lo:hi] = (scaling * block).astype(bf16)


def prompt_kernel(ends, q, k, v, g, dq, dk, dv):
    width = q.shape[0]
    scaling = 1.0 / math.sqrt(E * width)
    bounds = slab_bounds(ends, lax.axis_index("seq"), width)
    for lo in range(0, width, STRIP):
        hi = lo + STRIP
        keep = strip_mask(lo, STRIP, width, bounds)
        keys = k[lo:hi]
        attn = jnp.where(keep, dot(keys, q[lo:], 1, 1), 0.0).astype(bf16)
        gw = jnp.where(keep, dot(v[lo:hi], g[lo:], 1, 1), 0.0).astype(bf16)
        dk[lo:hi] = scaling * dot(gw, q[lo:], 1, 0)
        dv[lo:hi] = scaling * dot(attn, g[lo:], 1, 0)
        part = dot(gw, keys, 0, 0)
        if lo == 0:
            dq[...] = part
        else:
            dq[lo:] += part


def query_kernel(ends, part, g, states, dq):
    width = g.shape[0]
    scaling = 1.0 / math.sqrt(E * width)
    bounds = slab_bounds(ends, lax.axis_index("seq"), width)
    carry = load_matrix(states, states.shape[1] - 1)
    crossed = dot(g[...], carry, 1, 1)
    rows = rows_of((width, E))
    dq[...] = (scaling * (part[...] + jnp.where(rows < bounds[0], crossed, 0.0))).astype(bf16)


def right_kernel(ends, dk_in, dv_in, k, v, states, dk_out, dv_out, dk_part, dv_part, dk, dv, sems):
    width, flat = k.shape
    heads = flat // E
    bounds = slab_bounds(ends, lax.axis_index("seq"), width)
    rows = rows_of((width, E))
    cut = lambda a: [a[:, m * E : (m + 1) * E] for m in range(PIECES)]
    copies = []
    fetches = []
    for h in range(heads):
        columns = pl.ds(h * E, E)
        for i, (a, b) in enumerate(((dk_in, dk_part), (dv_in, dv_part))):
            fetches.append(pltpu.make_async_copy(a.at[:, columns], b.at[:, columns], sems.at[h, 2 + i]))
            fetches[-1].start()
    for h in range(heads):
        at = slice(h * E, (h + 1) * E)
        mats = [load_matrix(states, m, h, states.shape[0] // heads) for m in range(PIECES)]
        by_v = dot(v[:, at], jnp.concatenate(mats, axis=0), 1, 1)
        fetches[2 * h].wait()
        dk[:, at] = (dk_part[:, at] + pick_rows(rows, bounds, cut(by_v))).astype(bf16)
        by_k = dot(k[:, at], jnp.concatenate(mats, axis=1), 1, 0)
        fetches[2 * h + 1].wait()
        dv[:, at] = (dv_part[:, at] + pick_rows(rows, bounds, cut(by_k))).astype(bf16)
        columns = pl.ds(h * E, E)
        for i, (a, b) in enumerate(((dk, dk_out), (dv, dv_out))):
            copies.append(pltpu.make_async_copy(a.at[:, columns], b.at[:, columns], sems.at[h, i]))
            copies[-1].start()
    for c in copies:
        c.wait()


def exchange(a):
    return lax.all_to_all(a, "seq", 0, 0, tiled=True)


def per_device(
    prompt_q,
    prompt_k,
    prompt_v,
    prompt_grad,
    cand_q,
    cand_k,
    cand_v,
    readout,
    prompt_ends,
    cand_lengths,
    cand_prompt,
    cand_ranks,
):
    width = prompt_q.shape[0]
    cand_width = cand_q.shape[0]
    flat = prompt_q.shape[1]
    heads = flat // E
    count = lax.axis_size("seq")
    groups = lax.axis_size("head")
    per_slab = cand_lengths.shape[1]
    cands = cand_prompt.shape[0]
    scaling = 1.0 / math.sqrt(E * width)
    rows = flat // count
    share = count // heads
    whole = pl.BlockSpec((width, E), lambda h: (0, h))
    cand_block = pl.BlockSpec((cand_width, E), lambda h: (0, h))
    like = jax.ShapeDtypeStruct

    def parts_block(n):
        return pl.BlockSpec((share, n, rows, E), lambda h: (h, 0, 0, 0))

    def hbm(*arrays):
        return [pltpu.with_memory_space_constraint(a, pltpu.HBM) for a in arrays]

    def near(*arrays):
        return [pltpu.with_memory_space_constraint(a, pltpu.VMEM) for a in arrays]

    prompt_in = (prompt_q, prompt_k, prompt_v, prompt_grad)
    pieces = call(
        sums_kernel,
        in_specs=[SMEM] + [ANY] * 4,
        out_specs=VMEM,
        out_shape=like((count, PIECES + 1, rows, E), bf16),
        scratch_shapes=[pltpu.VMEM((width, flat), bf16)] * 4 + [pltpu.SemaphoreType.DMA((heads, 4))],
        name="sums",
    )(prompt_ends, *hbm(*prompt_in))
    parts = exchange(pieces)

    pieces, late_in = lax.optimization_barrier((pieces, prompt_in))
    dq_part, dk_part, dv_part = call(
        prompt_kernel,
        grid=(heads,),
        in_specs=[SMEM] + [whole] * 4,
        out_specs=[whole] * 3,
        out_shape=[pltpu.HBM((width, flat), f32)] * 3,
        name="prompt",
    )(prompt_ends, *hbm(*late_in))
    parts, dq_part, dk_part, dv_part = lax.optimization_barrier((parts, dq_part, dk_part, dv_part))

    chained = call(
        lambda *refs: chain_kernel(*refs, width=width),
        in_specs=[SMEM, SMEM, VMEM],
        out_specs=VMEM,
        out_shape=like((count, per_slab + 1, rows, E), bf16),
        scratch_shapes=[pltpu.VMEM((prompt_ends.shape[0] + 1, rows, E), f32)],
        name="chain",
    )(prompt_ends, cand_prompt, parts)
    states = exchange(chained)

    chained, cand_in = lax.optimization_barrier((chained, (cand_q, cand_k, cand_v)))
    inside = call(
        inside_kernel,
        grid=(heads,),
        in_specs=[SMEM] + [cand_block] * 3,
        out_specs=cand_block,
        out_shape=like((cand_width, flat), f32),
        name="inside",
    )(cand_lengths, *hbm(*cand_in))

    near_q = near(cand_in[0])[0]
    slope, raw, slope_far = call(
        lambda *refs: scores_kernel(*refs, scaling=scaling),
        in_specs=[SMEM] + [VMEM] * 4,
        out_specs=[VMEM, VMEM, ANY],
        out_shape=[
            pltpu.VMEM((cand_width, flat), f32),
            like((8, E), f32),
            pltpu.HBM((cand_width, flat), f32),
        ],
        scratch_shapes=[pltpu.SemaphoreType.DMA((heads,))],
        name="scores",
    )(cand_lengths, near_q, inside, readout.reshape(1, flat), states)
    raws = [raw]
    for step in range(1, groups):
        raws.append(lax.ppermute(raw, "head", [(i, (i + step) % groups) for i in range(groups)]))
    grads = call(
        lambda *refs: grads_kernel(*refs, scaling=scaling),
        in_specs=[SMEM] + [VMEM] * (2 + groups),
        out_specs=VMEM,
        out_shape=like((count, per_slab * rows + SCORE_ROWS, E), bf16),
        name="grads",
    )(cand_lengths, near_q, *near(slope), *raws)
    all_grads = exchange(grads)

    grads, late_grad = lax.optimization_barrier((grads, prompt_grad))
    prompt_dq = call(
        query_kernel,
        grid=(heads,),
        in_specs=[SMEM, whole, whole, parts_block(per_slab + 1)],
        out_specs=whole,
        out_shape=pltpu.HBM((width, flat), bf16),
        name="query",
    )(prompt_ends, *hbm(dq_part, late_grad), states)
    all_grads, prompt_dq = lax.optimization_barrier((all_grads, prompt_dq))

    right, coef, loss = call(
        lambda *refs: listwise_kernel(*refs, width=width),
        in_specs=[SMEM, SMEM] + [VMEM] * 4,
        out_specs=[VMEM] * 3,
        out_shape=[
            like((count, PIECES, rows, E), bf16),
            like((8, E), f32),
            like((1, E), f32),
        ],
        scratch_shapes=[
            pltpu.VMEM((cands, E), f32),
            pltpu.VMEM((cands, E), f32),
            pltpu.VMEM((prompt_ends.shape[0], rows, E), f32),
        ],
        name="listwise",
    )(
        prompt_ends,
        cand_prompt,
        cand_prompt.reshape(1, cands),
        cand_ranks.reshape(1, cands),
        all_grads,
        parts,
    )
    rights = exchange(right)

    cand_dq, cand_dk, cand_dv = call(
        lambda *refs: cand_kernel(*refs, scaling=scaling),
        grid=(heads,),
        in_specs=[SMEM, pl.BlockSpec((8, E), lambda h: (0, 0))]
        + [cand_block] * 4
        + [parts_block(per_slab + 1)],
        out_specs=[cand_block] * 3,
        out_shape=[pltpu.HBM((cand_width, flat), bf16)] * 3,
        name="cand",
    )(cand_lengths, coef, *hbm(*cand_in, slope_far), states)
    rights, cand_dq, cand_dk, cand_dv = lax.optimization_barrier((rights, cand_dq, cand_dk, cand_dv))

    prompt_dk, prompt_dv = call(
        right_kernel,
        in_specs=[SMEM, ANY, ANY] + [VMEM] * 3,
        out_specs=[ANY] * 2,
        out_shape=[pltpu.HBM((width, flat), bf16)] * 2,
        scratch_shapes=[pltpu.VMEM((width, flat), f32)] * 2
        + [pltpu.VMEM((width, flat), bf16)] * 2
        + [pltpu.SemaphoreType.DMA((heads, 4))],
        name="right",
    )(prompt_ends, *hbm(dk_part, dv_part), *near(prompt_k, prompt_v), rights)
    return (
        prompt_dq,
        prompt_dk,
        prompt_dv,
        cand_dq,
        cand_dk,
        cand_dv,
        loss[0, 0],
    )


def solution(mesh):
    tile = P("seq", "head")
    return jax.shard_map(
        per_device,
        mesh=mesh,
        in_specs=(tile,) * 7 + (P("head"), P(), P("seq", None), P(), P()),
        out_specs=(tile,) * 6 + (P(),),
        check_vma=False,
    )
```

```python
import math

import jax
import jax.numpy as jnp
from jax import lax
from jax.experimental import pallas as pl
from jax.experimental.pallas import tpu as pltpu
from jax.sharding import PartitionSpec as P

E = 128
ENDS = 2
PIECES = ENDS + 1
STRIP = 256
grad_scale = 1048576.0
f32 = jnp.float32
bf16 = jnp.bfloat16
SMEM = pl.BlockSpec(memory_space=pltpu.SMEM)
VMEM = pl.BlockSpec(memory_space=pltpu.VMEM)
ANY = pl.BlockSpec(memory_space=pl.ANY)
SCORE_ROWS = 16
SCORE_PARTS = 3


def dot(a, b, ca, cb):
    return lax.dot_general(a, b, (((ca,), (cb,)), ((), ())), preferred_element_type=f32)


def call(body, **kw):
    return pl.pallas_call(
        body,
        compiler_params=pltpu.CompilerParams(vmem_limit_bytes=24 * 1024 * 1024),
        **kw,
    )


def count_ends(ends, limit):
    total = jnp.int32(0)
    for p in range(ends.shape[0]):
        total += (ends[p] <= limit).astype(jnp.int32)
    return total


def end_of(ends, pid, none):
    last = ends.shape[0] - 1
    return jnp.where(pid <= last, ends[jnp.minimum(pid, last)], none)


def slab_bounds(ends, slab, width):
    start = slab * width
    first = count_ends(ends, start)
    far = start + width
    return [jnp.minimum(end_of(ends, first + m, far) - start, width) for m in range(ENDS)]


def pick_rows(rows, bounds, options):
    out = options[-1]
    for b, o in zip(reversed(bounds), reversed(options[:-1])):
        out = jnp.where(rows < b, o, out)
    return out


def rows_of(shape, start=0):
    return lax.broadcasted_iota(jnp.int32, shape, 0) + start


def strip_mask(lo, size, width, bounds):
    s = rows_of((size, 1), lo)
    t = lax.broadcasted_iota(jnp.int32, (size, width - lo), 1) + lo
    stop = pick_rows(s, bounds, [jnp.full((size, 1), b, jnp.int32) for b in bounds] + [width])
    return jnp.logical_and(t >= s, t < stop)


def store_parts(out, place, mat):
    parts, rows = out.shape[0], out.shape[2]
    for o in range(parts):
        out[o, place] = mat[o * rows : (o + 1) * rows].astype(bf16)


def load_matrix(ref, place, h=0, share=None):
    share = ref.shape[0] if share is None else share
    return jnp.concatenate([ref[h * share + o, place] for o in range(share)], axis=0)


def sums_kernel(ends, q_in, k_in, v_in, g_in, out, both_out, q, k, v, g, sems):
    width, flat = q.shape
    heads = flat // E
    share = out.shape[0] // heads
    columns = [pl.ds(h * E, E) for h in range(heads)]
    copies = [
        [
            pltpu.make_async_copy(a.at[:, columns[h]], b.at[:, columns[h]], sems.at[h, i])
            for i, (a, b) in enumerate(((k_in, k), (v_in, v), (q_in, q), (g_in, g)))
        ]
        for h in range(heads)
    ]
    for group in copies:
        for c in group:
            c.start()
    bounds = slab_bounds(ends, lax.axis_index("seq"), width)
    scaling = 1.0 / math.sqrt(E * width)
    rows = rows_of((width, E))
    zero = jnp.zeros((width, E), f32)
    for h in range(heads):
        for c in copies[h]:
            c.wait()
        at = slice(h * E, (h + 1) * E)
        values = v[:, at].astype(f32)
        pieces = []
        low = 0
        for b in bounds + [width]:
            inside = jnp.logical_and(rows >= low, rows < b)
            pieces.append(jnp.where(inside, values, zero).astype(bf16))
            low = b
        sums = dot(k[:, at], jnp.concatenate(pieces, axis=1), 0, 0)
        mine = out.at[pl.ds(h * share, share)]
        for m in range(PIECES):
            store_parts(mine, m, sums[:, m * E : (m + 1) * E])
        first = jnp.where(rows < bounds[0], g[:, at].astype(f32), zero).astype(bf16)
        both_out[1, h] = (scaling * dot(q[:, at], first, 0, 0)).astype(bf16)
        cuts = [sums[:, m * E : (m + 1) * E] for m in range(PIECES)]
        final = cuts[0]
        for b, piece in zip(bounds, cuts[1:]):
            final = jnp.where(b < width, piece, final)
        both_out[0, h] = final.astype(bf16)


def chain_kernel(ends, cand_prompt, parts, out, held, *, width):
    count = parts.shape[0]
    per_slab = cand_prompt.shape[0] // count
    running = jnp.zeros(parts.shape[2:], f32)
    for e in range(count):
        start = e * width
        first = count_ends(ends, start)
        last = count_ends(ends, start + width - 1)
        begins = jnp.bool_(True) if e == 0 else ends[jnp.maximum(first - 1, 0)] == start
        if e > 0:
            begins = jnp.logical_and(first > 0, begins)
        incoming = jnp.where(begins, 0.0, running)
        firsts = parts[e, 0].astype(f32) + incoming
        second = parts[e, 1].astype(f32)
        third = parts[e, 2].astype(f32)
        spare = ends.shape[0]
        for m, piece in enumerate((firsts, second)):
            ended = end_of(ends, first + m, start + width + 1) <= start + width
            held[jnp.where(ended, first + m, spare)] = piece
        running = jnp.where(last == first, firsts, jnp.where(last == first + 1, second, third))
    for c in range(cand_prompt.shape[0]):
        out[c // per_slab, c % per_slab] = held[cand_prompt[c]].astype(bf16)


def inside_kernel(lengths, q, k, v, out):
    width = q.shape[0]
    bounds = cand_bounds(lengths)
    for lo in range(0, width, STRIP):
        hi = lo + STRIP
        scores = dot(q[lo:hi], k[:hi], 1, 1)
        t = rows_of((STRIP, hi), lo)
        s = lax.broadcasted_iota(jnp.int32, (STRIP, hi), 1)
        begin = pick_rows(t[:, :1], bounds, [0] + [jnp.full((STRIP, 1), b, jnp.int32) for b in bounds])
        keep = jnp.logical_and(s <= t, s >= begin)
        out[lo:hi] = dot(jnp.where(keep, scores, 0.0).astype(bf16), v[:hi], 1, 0)


def cand_bounds(lengths):
    bounds = []
    total = jnp.int32(0)
    for j in range(lengths.shape[1] - 1):
        total += lengths[0, j]
        bounds.append(total)
    return bounds


def scores_kernel(lengths, q, inside, readout, states, slope_out, raw_out, slope_far, sems, *, scaling):
    width, flat = q.shape
    heads = flat // E
    per_slab = lengths.shape[1]
    bounds = cand_bounds(lengths)
    rows = rows_of((width, E))
    zero = jnp.zeros((width, E), f32)
    inverse = [1.0 / jnp.full((1, E), lengths[0, j], jnp.int32).astype(f32) for j in range(per_slab)]
    totals = [jnp.zeros((1, E), f32) for j in range(per_slab)]
    copies = []
    for h in range(heads):
        at = slice(h * E, (h + 1) * E)
        wide = [load_matrix(states, j, h, states.shape[0] // heads) for j in range(per_slab)]
        crossed = dot(q[:, at], jnp.concatenate(wide, axis=1), 1, 0)
        crossed = pick_rows(rows, bounds, [crossed[:, j * E : (j + 1) * E] for j in range(per_slab)])
        out = scaling * (inside[:, at] + crossed)
        weight = pick_rows(rows, bounds, inverse) * readout[:, at]
        sigma = jax.nn.sigmoid(out)
        slope_out[:, at] = weight * sigma * (1.0 + out * (1.0 - sigma))
        columns = pl.ds(h * E, E)
        copies.append(pltpu.make_async_copy(slope_out.at[:, columns], slope_far.at[:, columns], sems.at[h]))
        copies[-1].start()
        silu = out * sigma * weight
        low = 0
        for j, b in enumerate(bounds + [width]):
            mine = jnp.logical_and(rows >= low, rows < b)
            totals[j] += jnp.sum(jnp.where(mine, silu, zero), axis=0, keepdims=True)
            low = b
    raw_out[...] = jnp.zeros_like(raw_out)
    for j in range(per_slab):
        raw_out[j : j + 1] = jnp.broadcast_to(jnp.sum(totals[j], axis=1, keepdims=True), (1, E))
    for c in copies:
        c.wait()


def grads_kernel(lengths, q, slope, *refs, scaling):
    raws, out = refs[:-1], refs[-1]
    width, flat = q.shape
    heads = flat // E
    count = out.shape[0]
    share = count // heads
    size = flat // count
    per_slab = lengths.shape[1]
    bounds = cand_bounds(lengths)
    rows = rows_of((width, E))
    zero = jnp.zeros((width, E), f32)
    for h in range(heads):
        at = slice(h * E, (h + 1) * E)
        mine = slope[:, at]
        high, low_part = [], []
        low = 0
        for b in bounds + [width]:
            kept = jnp.where(jnp.logical_and(rows >= low, rows < b), mine, zero)
            top = kept.astype(bf16)
            high.append(top)
            low_part.append((kept - top.astype(f32)).astype(bf16))
            low = b
        grads = dot(q[:, at], jnp.concatenate(high + low_part, axis=1), 0, 0)
        for j in range(per_slab):
            grad = grads[:, j * E : (j + 1) * E] + grads[:, (per_slab + j) * E : (per_slab + j + 1) * E]
            grad = (scaling * grad).astype(bf16)
            for o in range(share):
                out[h * share + o, j * size : (j + 1) * size] = grad[o * size : (o + 1) * size]
    total = raws[0][...]
    for r in raws[1:]:
        total += r[...]
    lines = []
    for j in range(per_slab):
        left = total[j : j + 1]
        for i in range(SCORE_PARTS):
            line = left.astype(bf16).astype(f32)
            lines.append(line)
            left = left - line
    lines.append(jnp.zeros((SCORE_ROWS - len(lines), E), f32))
    tile = jnp.concatenate(lines, axis=0).astype(bf16)
    for o in range(count):
        out[o, per_slab * size :] = tile


def listwise_kernel(
    ends,
    prompts,
    prompt_row,
    rank_row,
    grads,
    out,
    coef_out,
    loss_out,
    raw_held,
    coef_held,
    held,
    *,
    width,
):
    count = grads.shape[0]
    size = held.shape[1]
    per_slab = prompts.shape[0] // count
    cands = count * per_slab
    prompt_count = ends.shape[0]
    for e in range(count):
        tile = grads[e, per_slab * size :].astype(f32)
        for j in range(per_slab):
            total = tile[SCORE_PARTS * j : SCORE_PARTS * j + 1]
            for i in range(1, SCORE_PARTS):
                total = total + tile[SCORE_PARTS * j + i : SCORE_PARTS * j + i + 1]
            raw_held[e * per_slab + j : e * per_slab + j + 1] = total
    raw = raw_held[...]
    square = (cands, cands)
    down = lax.broadcasted_iota(jnp.int32, square, 0)
    across = lax.broadcasted_iota(jnp.int32, square, 1)
    same_spot = down == across
    own = jnp.broadcast_to(prompt_row[...].astype(f32), square)
    own_down = jnp.sum(jnp.where(same_spot, own, 0.0), axis=1, keepdims=True)
    group = own == own_down
    rank_weight = jnp.broadcast_to(jnp.exp(-rank_row[...].astype(f32)), square)
    rank_down = jnp.sum(jnp.where(same_spot, rank_weight, 0.0), axis=1, keepdims=True)
    target = rank_down / jnp.sum(jnp.where(group, rank_weight, 0.0), axis=1, keepdims=True)
    tanh_raw = jnp.tanh(raw)
    squashed = 3.0 * tanh_raw
    exp_scores = jnp.exp(squashed)
    exp_across = jnp.sum(jnp.where(same_spot, exp_scores[:, :cands], 0.0), axis=0, keepdims=True)
    denom = jnp.sum(jnp.where(group, jnp.broadcast_to(exp_across, square), 0.0), axis=1, keepdims=True)
    terms = target * (squashed - jnp.log(denom))
    loss_out[...] = -jnp.sum(terms, axis=0, keepdims=True) / prompt_count
    coef = grad_scale / prompt_count * (exp_scores / denom - target) * 3.0 * (1.0 - tanh_raw * tanh_raw)
    coef_held[...] = coef
    me = lax.axis_index("seq")
    for j in range(per_slab):
        coef_out[j : j + 1] = coef_held[pl.ds(me * per_slab + j, 1)]
    held[...] = jnp.zeros_like(held)
    for c in range(cands):
        j = c % per_slab
        held[prompts[c]] += grads[c // per_slab, j * size : (j + 1) * size].astype(f32) * coef[c : c + 1]
    nothing = jnp.zeros((size, E), f32)
    for e in range(count):
        start = e * width
        far = start + width
        first = count_ends(ends, start)
        last = count_ends(ends, far - 1)
        open_grad = jnp.where(ends[last] != far, held[last], nothing).astype(bf16)
        for m in range(ENDS):
            pid = first + m
            ended = end_of(ends, pid, far + 1) <= far
            here = held[jnp.minimum(pid, prompt_count - 1)].astype(bf16)
            out[e, m] = jnp.where(ended, here, open_grad)
        out[e, ENDS] = open_grad


def cand_kernel(lengths, coef, q, k, v, slope, states, dq, dk, dv, *, scaling):
    width = q.shape[0]
    per_slab = lengths.shape[1]
    bounds = cand_bounds(lengths)
    rows = rows_of((width, E))
    dout = (pick_rows(rows, bounds, [coef[j : j + 1] for j in range(per_slab)]) * slope[...]).astype(bf16)
    wide = jnp.concatenate([load_matrix(states, j) for j in range(per_slab)], axis=0)
    crossed = dot(dout, wide, 1, 1)
    total = pick_rows(rows, bounds, [crossed[:, j * E : (j + 1) * E] for j in range(per_slab)])
    blocks = []
    for lo in range(0, width, STRIP):
        hi = lo + STRIP
        keep = strip_mask(lo, STRIP, width, bounds)
        keys = k[lo:hi]
        attn = jnp.where(keep, dot(keys, q[lo:], 1, 1), 0.0).astype(bf16)
        gw = jnp.where(keep, dot(v[lo:hi], dout[lo:], 1, 1), 0.0).astype(bf16)
        dk[lo:hi] = (scaling * dot(gw, q[lo:], 1, 0)).astype(bf16)
        dv[lo:hi] = (scaling * dot(attn, dout[lo:], 1, 0)).astype(bf16)
        total = total + dot(gw, keys, 0, 0)
        blocks.append((lo, hi, total[:STRIP]))
        total = total[STRIP:]
    for lo, hi, block in blocks:
        dq[lo:hi] = (scaling * block).astype(bf16)


def prompt_kernel(ends, q, k, v, g, dq, dk, dv):
    width = q.shape[0]
    scaling = 1.0 / math.sqrt(E * width)
    bounds = slab_bounds(ends, lax.axis_index("seq"), width)
    for lo in range(0, width, STRIP):
        hi = lo + STRIP
        keep = strip_mask(lo, STRIP, width, bounds)
        keys = k[lo:hi]
        attn = jnp.where(keep, dot(keys, q[lo:], 1, 1), 0.0).astype(bf16)
        gw = jnp.where(keep, dot(v[lo:hi], g[lo:], 1, 1), 0.0).astype(bf16)
        dk[lo:hi] = scaling * dot(gw, q[lo:], 1, 0)
        dv[lo:hi] = scaling * dot(attn, g[lo:], 1, 0)
        part = dot(gw, keys, 0, 0)
        if lo == 0:
            dq[...] = part
        else:
            dq[lo:] += part


def query_kernel(ends, part, g, tails, firsts, dq, later):
    width = g.shape[0]
    scaling = 1.0 / math.sqrt(E * width)
    me = lax.axis_index("seq")
    bounds = slab_bounds(ends, me, width)
    first = count_ends(ends, me * width)
    last = count_ends(ends, me * width + width - 1)
    carry = jnp.zeros((E, E), f32)
    ahead = jnp.zeros((E, E), f32)
    for e in range(tails.shape[0]):
        before = jnp.logical_and(e < me, count_ends(ends, e * width + width - 1) == first)
        carry += jnp.where(before, tails[e, 0, 0].astype(f32), 0.0)
        after = jnp.logical_and(e > me, count_ends(ends, e * width) == last)
        ahead += jnp.where(after, firsts[e, 0, 0].astype(f32), 0.0)
    later[0] = ahead
    crossed = dot(g[...], carry.astype(bf16), 1, 1)
    rows = rows_of((width, E))
    dq[...] = (scaling * (part[...] + jnp.where(rows < bounds[0], crossed, 0.0))).astype(bf16)


def right_kernel(ends, dk_in, dv_in, k, v, later, states, dk_out, dv_out, dk_part, dv_part, dk, dv, mats, total, sems):
    width, flat = k.shape
    heads = flat // E
    bounds = slab_bounds(ends, lax.axis_index("seq"), width)
    copies = []
    fetches = []
    for h in range(heads):
        columns = pl.ds(h * E, E)
        for i, (a, b) in enumerate(((dk_in, dk_part), (dv_in, dv_part))):
            fetches.append(pltpu.make_async_copy(a.at[:, columns], b.at[:, columns], sems.at[h, 2 + i]))
            fetches[-1].start()
    zero = jnp.zeros((E, E), bf16)
    strips = []
    for lo in range(0, width, STRIP):
        low = jnp.int32(0)
        high = jnp.int32(0)
        for b in bounds:
            low += (b <= lo).astype(jnp.int32)
            high += (b < lo + STRIP).astype(jnp.int32)
        strips.append((lo, low, high))
    start = lax.axis_index("seq") * width
    first = count_ends(ends, start)
    still_open = [end_of(ends, first + m, start + width + 1) > start + width for m in range(PIECES)]
    starts = [jnp.int32(0)] + bounds
    stops = bounds + [jnp.int32(width)]

    def chosen(table, m):
        out = table[-1]
        for i in reversed(range(PIECES - 1)):
            out = jnp.where(m == i, table[i], out)
        return out

    for h in range(heads):
        at = slice(h * E, (h + 1) * E)
        for m in range(PIECES):
            mat = load_matrix(states, m, h, states.shape[0] // heads).astype(f32)
            mat = (mat + jnp.where(still_open[m], later[h], 0.0)).astype(bf16)
            mats[h, m, :E, :E] = mat.T
            mats[h, m, :E, E:] = zero
            mats[h, m, E:, :E] = zero
            mats[h, m, E:, E:] = mat
        fetches[2 * h].wait()
        fetches[2 * h + 1].wait()
        for lo, low, high in strips:
            hi = lo + STRIP
            both = jnp.concatenate([v[lo:hi, at], k[lo:hi, at]], axis=1)
            rows = rows_of((STRIP, 2 * E), lo)

            def part(m):
                keep = jnp.logical_and(rows >= chosen(starts, m), rows < chosen(stops, m))
                return dot(jnp.where(keep, both.astype(f32), 0.0).astype(bf16), mats[h, m], 1, 0)

            @pl.when(low == high)
            def _():
                whole = dot(both, mats[h, low], 1, 0)
                dk[lo:hi, at] = (dk_part[lo:hi, at] + whole[:, :E]).astype(bf16)
                dv[lo:hi, at] = (dv_part[lo:hi, at] + whole[:, E:]).astype(bf16)

            @pl.when(low != high)
            def _():
                total[...] = part(low) + part(low + 1)

                @pl.when(high > low + 1)
                def _():
                    total[...] += part(low + 2)

                dk[lo:hi, at] = (dk_part[lo:hi, at] + total[:, :E]).astype(bf16)
                dv[lo:hi, at] = (dv_part[lo:hi, at] + total[:, E:]).astype(bf16)

        columns = pl.ds(h * E, E)
        for i, (a, b) in enumerate(((dk, dk_out), (dv, dv_out))):
            copies.append(pltpu.make_async_copy(a.at[:, columns], b.at[:, columns], sems.at[h, i]))
            copies[-1].start()
    for c in copies:
        c.wait()


def exchange(a):
    return lax.all_to_all(a, "seq", 0, 0, tiled=True)


def per_device(
    prompt_q,
    prompt_k,
    prompt_v,
    prompt_grad,
    cand_q,
    cand_k,
    cand_v,
    readout,
    prompt_ends,
    cand_lengths,
    cand_prompt,
    cand_ranks,
):
    width = prompt_q.shape[0]
    cand_width = cand_q.shape[0]
    flat = prompt_q.shape[1]
    heads = flat // E
    count = lax.axis_size("seq")
    groups = lax.axis_size("head")
    per_slab = cand_lengths.shape[1]
    cands = cand_prompt.shape[0]
    scaling = 1.0 / math.sqrt(E * width)
    rows = flat // count
    share = count // heads
    whole = pl.BlockSpec((width, E), lambda h: (0, h))
    cand_block = pl.BlockSpec((cand_width, E), lambda h: (0, h))
    like = jax.ShapeDtypeStruct

    def parts_block(n):
        return pl.BlockSpec((share, n, rows, E), lambda h: (h, 0, 0, 0))

    def hbm(*arrays):
        return [pltpu.with_memory_space_constraint(a, pltpu.HBM) for a in arrays]

    def near(*arrays):
        return [pltpu.with_memory_space_constraint(a, pltpu.VMEM) for a in arrays]

    prompt_in = (prompt_q, prompt_k, prompt_v, prompt_grad)
    pieces, open_sums = call(
        sums_kernel,
        in_specs=[SMEM] + [ANY] * 4,
        out_specs=[VMEM] * 2,
        out_shape=[like((count, PIECES, rows, E), bf16), like((2, heads, E, E), bf16)],
        scratch_shapes=[pltpu.VMEM((width, flat), bf16)] * 4 + [pltpu.SemaphoreType.DMA((heads, 4))],
        name="sums",
    )(prompt_ends, *hbm(*prompt_in))
    parts = exchange(pieces)
    open_sums = lax.all_gather(open_sums, "seq")

    pieces, late_in = lax.optimization_barrier((pieces, prompt_in))
    dq_part, dk_part, dv_part = call(
        prompt_kernel,
        grid=(heads,),
        in_specs=[SMEM] + [whole] * 4,
        out_specs=[whole] * 3,
        out_shape=[pltpu.HBM((width, flat), f32)] * 3,
        name="prompt",
    )(prompt_ends, *hbm(*late_in))
    parts, dq_part, dk_part, dv_part = lax.optimization_barrier((parts, dq_part, dk_part, dv_part))

    chained = call(
        lambda *refs: chain_kernel(*refs, width=width),
        in_specs=[SMEM, SMEM, VMEM],
        out_specs=VMEM,
        out_shape=like((count, per_slab, rows, E), bf16),
        scratch_shapes=[pltpu.VMEM((prompt_ends.shape[0] + 1, rows, E), f32)],
        name="chain",
    )(prompt_ends, cand_prompt, parts)
    states = exchange(chained)

    chained, cand_in = lax.optimization_barrier((chained, (cand_q, cand_k, cand_v)))
    inside = call(
        inside_kernel,
        grid=(heads,),
        in_specs=[SMEM] + [cand_block] * 3,
        out_specs=cand_block,
        out_shape=like((cand_width, flat), f32),
        name="inside",
    )(cand_lengths, *hbm(*cand_in))

    near_q = near(cand_in[0])[0]
    slope, raw, slope_far = call(
        lambda *refs: scores_kernel(*refs, scaling=scaling),
        in_specs=[SMEM] + [VMEM] * 4,
        out_specs=[VMEM, VMEM, ANY],
        out_shape=[
            pltpu.VMEM((cand_width, flat), f32),
            like((8, E), f32),
            pltpu.HBM((cand_width, flat), f32),
        ],
        scratch_shapes=[pltpu.SemaphoreType.DMA((heads,))],
        name="scores",
    )(cand_lengths, near_q, inside, readout.reshape(1, flat), states)
    raws = [raw]
    for step in range(1, groups):
        raws.append(lax.ppermute(raw, "head", [(i, (i + step) % groups) for i in range(groups)]))
    grads = call(
        lambda *refs: grads_kernel(*refs, scaling=scaling),
        in_specs=[SMEM] + [VMEM] * (2 + groups),
        out_specs=VMEM,
        out_shape=like((count, per_slab * rows + SCORE_ROWS, E), bf16),
        name="grads",
    )(cand_lengths, near_q, *near(slope), *raws)
    all_grads = exchange(grads)

    right, coef, loss = call(
        lambda *refs: listwise_kernel(*refs, width=width),
        in_specs=[SMEM, SMEM] + [VMEM] * 3,
        out_specs=[VMEM] * 3,
        out_shape=[
            like((count, PIECES, rows, E), bf16),
            like((8, E), f32),
            like((1, E), f32),
        ],
        scratch_shapes=[
            pltpu.VMEM((cands, E), f32),
            pltpu.VMEM((cands, E), f32),
            pltpu.VMEM((prompt_ends.shape[0], rows, E), f32),
        ],
        name="listwise",
    )(
        prompt_ends,
        cand_prompt,
        cand_prompt.reshape(1, cands),
        cand_ranks.reshape(1, cands),
        all_grads,
    )
    rights = exchange(right)

    cand_dq, cand_dk, cand_dv = call(
        lambda *refs: cand_kernel(*refs, scaling=scaling),
        grid=(heads,),
        in_specs=[SMEM, pl.BlockSpec((8, E), lambda h: (0, 0))]
        + [cand_block] * 4
        + [parts_block(per_slab)],
        out_specs=[cand_block] * 3,
        out_shape=[pltpu.HBM((cand_width, flat), bf16)] * 3,
        name="cand",
    )(cand_lengths, coef, *hbm(*cand_in, slope_far), states)
    gathered = [
        pl.BlockSpec((count, 1, 1, E, E), lambda h: (0, 0, h, 0, 0)),
        pl.BlockSpec((count, 1, 1, E, E), lambda h: (0, 1, h, 0, 0)),
    ]
    cand_dq, late_grad, open_sums = lax.optimization_barrier((cand_dq, prompt_grad, open_sums))
    prompt_dq, later = call(
        query_kernel,
        grid=(heads,),
        in_specs=[SMEM, whole, whole] + gathered,
        out_specs=[whole, pl.BlockSpec((1, E, E), lambda h: (h, 0, 0))],
        out_shape=[pltpu.HBM((width, flat), bf16), like((heads, E, E), f32)],
        name="query",
    )(prompt_ends, *hbm(dq_part, late_grad, open_sums, open_sums))
    rights, cand_dk, prompt_dq = lax.optimization_barrier((rights, cand_dk, prompt_dq))

    prompt_dk, prompt_dv = call(
        right_kernel,
        in_specs=[SMEM, ANY, ANY] + [VMEM] * 4,
        out_specs=[ANY] * 2,
        out_shape=[pltpu.HBM((width, flat), bf16)] * 2,
        scratch_shapes=[pltpu.VMEM((width, flat), f32)] * 2
        + [pltpu.VMEM((width, flat), bf16)] * 2
        + [
            pltpu.VMEM((heads, PIECES, 2 * E, 2 * E), bf16),
            pltpu.VMEM((STRIP, 2 * E), f32),
            pltpu.SemaphoreType.DMA((heads, 4)),
        ],
        name="right",
    )(prompt_ends, *hbm(dk_part, dv_part), *near(prompt_k, prompt_v), later, rights)
    return (
        prompt_dq,
        prompt_dk,
        prompt_dv,
        cand_dq,
        cand_dk,
        cand_dv,
        loss[0, 0],
    )


def solution(mesh):
    tile = P("seq", "head")
    return jax.shard_map(
        per_device,
        mesh=mesh,
        in_specs=(tile,) * 7 + (P("head"), P(), P("seq", None), P(), P()),
        out_specs=(tile,) * 6 + (P(),),
        check_vma=False,
    )
```

```python
import math

import jax
import jax.numpy as jnp
from jax import lax
from jax.experimental import pallas as pl
from jax.experimental.pallas import tpu as pltpu
from jax.sharding import PartitionSpec as P

E = 128
ENDS = 2
PIECES = ENDS + 1
STRIP = 256
grad_scale = 1048576.0
f32 = jnp.float32
bf16 = jnp.bfloat16
SMEM = pl.BlockSpec(memory_space=pltpu.SMEM)
VMEM = pl.BlockSpec(memory_space=pltpu.VMEM)
ANY = pl.BlockSpec(memory_space=pl.ANY)
SCORE_ROWS = 16
SCORE_PARTS = 3


def dot(a, b, ca, cb):
    return lax.dot_general(a, b, (((ca,), (cb,)), ((), ())), preferred_element_type=f32)


def call(body, **kw):
    return pl.pallas_call(
        body,
        compiler_params=pltpu.CompilerParams(vmem_limit_bytes=24 * 1024 * 1024),
        **kw,
    )


def count_ends(ends, limit):
    total = jnp.int32(0)
    for p in range(ends.shape[0]):
        total += (ends[p] <= limit).astype(jnp.int32)
    return total


def end_of(ends, pid, none):
    last = ends.shape[0] - 1
    return jnp.where(pid <= last, ends[jnp.minimum(pid, last)], none)


def slab_bounds(ends, slab, width):
    start = slab * width
    first = count_ends(ends, start)
    far = start + width
    return [jnp.minimum(end_of(ends, first + m, far) - start, width) for m in range(ENDS)]


def pick_rows(rows, bounds, options):
    out = options[-1]
    for b, o in zip(reversed(bounds), reversed(options[:-1])):
        out = jnp.where(rows < b, o, out)
    return out


def rows_of(shape, start=0):
    return lax.broadcasted_iota(jnp.int32, shape, 0) + start


def strip_mask(lo, size, width, bounds):
    s = rows_of((size, 1), lo)
    t = lax.broadcasted_iota(jnp.int32, (size, width - lo), 1) + lo
    stop = pick_rows(s, bounds, [jnp.full((size, 1), b, jnp.int32) for b in bounds] + [width])
    return jnp.logical_and(t >= s, t < stop)


def store_parts(out, place, mat):
    parts, rows = out.shape[0], out.shape[2]
    for o in range(parts):
        out[o, place] = mat[o * rows : (o + 1) * rows].astype(bf16)


def load_matrix(ref, place, h=0, share=None):
    share = ref.shape[0] if share is None else share
    return jnp.concatenate([ref[h * share + o, place] for o in range(share)], axis=0)


def sums_kernel(ends_in, k_in, v_in, out, ends, k, v, sems):
    width, flat = k.shape
    heads = flat // E
    share = out.shape[0] // heads
    columns = [pl.ds(h * E, E) for h in range(heads)]
    fetch_ends = pltpu.make_async_copy(ends_in, ends, sems.at[heads, 0])
    fetch_ends.start()
    copies = [
        [
            pltpu.make_async_copy(a.at[:, columns[h]], b.at[:, columns[h]], sems.at[h, i])
            for i, (a, b) in enumerate(((k_in, k), (v_in, v)))
        ]
        for h in range(heads)
    ]
    for group in copies:
        for c in group:
            c.start()
    fetch_ends.wait()
    bounds = slab_bounds(ends, lax.axis_index("seq"), width)
    rows = rows_of((width, E))
    zero = jnp.zeros((width, E), f32)
    for h in range(heads):
        for c in copies[h]:
            c.wait()
        at = slice(h * E, (h + 1) * E)
        values = v[:, at].astype(f32)
        pieces = []
        low = 0
        for b in bounds + [width]:
            inside = jnp.logical_and(rows >= low, rows < b)
            pieces.append(jnp.where(inside, values, zero).astype(bf16))
            low = b
        sums = dot(k[:, at], jnp.concatenate(pieces, axis=1), 0, 0)
        mine = out.at[pl.ds(h * share, share)]
        for m in range(PIECES):
            store_parts(mine, m, sums[:, m * E : (m + 1) * E])


def chain_kernel(ends, cand_prompt, parts, out, held, *, width):
    count = parts.shape[0]
    per_slab = cand_prompt.shape[0] // count
    running = jnp.zeros(parts.shape[2:], f32)
    for e in range(count):
        start = e * width
        first = count_ends(ends, start)
        last = count_ends(ends, start + width - 1)
        begins = jnp.bool_(True) if e == 0 else ends[jnp.maximum(first - 1, 0)] == start
        if e > 0:
            begins = jnp.logical_and(first > 0, begins)
        incoming = jnp.where(begins, 0.0, running)
        out[e, per_slab] = incoming.astype(bf16)
        firsts = parts[e, 0].astype(f32) + incoming
        second = parts[e, 1].astype(f32)
        third = parts[e, 2].astype(f32)
        spare = ends.shape[0]
        for m, piece in enumerate((firsts, second)):
            ended = end_of(ends, first + m, start + width + 1) <= start + width
            held[jnp.where(ended, first + m, spare)] = piece
        running = jnp.where(last == first, firsts, jnp.where(last == first + 1, second, third))
    for c in range(cand_prompt.shape[0]):
        out[c // per_slab, c % per_slab] = held[cand_prompt[c]].astype(bf16)


def inside_kernel(lengths, q, k, v, out):
    width = q.shape[0]
    bounds = cand_bounds(lengths)
    for lo in range(0, width, STRIP):
        hi = lo + STRIP
        scores = dot(q[lo:hi], k[:hi], 1, 1)
        t = rows_of((STRIP, hi), lo)
        s = lax.broadcasted_iota(jnp.int32, (STRIP, hi), 1)
        begin = pick_rows(t[:, :1], bounds, [0] + [jnp.full((STRIP, 1), b, jnp.int32) for b in bounds])
        keep = jnp.logical_and(s <= t, s >= begin)
        out[lo:hi] = dot(jnp.where(keep, scores, 0.0).astype(bf16), v[:hi], 1, 0)


def cand_bounds(lengths):
    bounds = []
    total = jnp.int32(0)
    for j in range(lengths.shape[1] - 1):
        total += lengths[0, j]
        bounds.append(total)
    return bounds


def scores_kernel(lengths, q, inside, readout, states, slope_out, raw_out, slope_far, sems, *, scaling):
    width, flat = q.shape
    heads = flat // E
    per_slab = lengths.shape[1]
    bounds = cand_bounds(lengths)
    rows = rows_of((width, E))
    zero = jnp.zeros((width, E), f32)
    inverse = [1.0 / jnp.full((1, E), lengths[0, j], jnp.int32).astype(f32) for j in range(per_slab)]
    totals = [jnp.zeros((1, E), f32) for j in range(per_slab)]
    copies = []
    for h in range(heads):
        at = slice(h * E, (h + 1) * E)
        wide = [load_matrix(states, j, h, states.shape[0] // heads) for j in range(per_slab)]
        crossed = dot(q[:, at], jnp.concatenate(wide, axis=1), 1, 0)
        crossed = pick_rows(rows, bounds, [crossed[:, j * E : (j + 1) * E] for j in range(per_slab)])
        out = scaling * (inside[:, at] + crossed)
        weight = pick_rows(rows, bounds, inverse) * readout[:, at]
        sigma = jax.nn.sigmoid(out)
        slope_out[:, at] = weight * sigma * (1.0 + out * (1.0 - sigma))
        columns = pl.ds(h * E, E)
        copies.append(pltpu.make_async_copy(slope_out.at[:, columns], slope_far.at[:, columns], sems.at[h]))
        copies[-1].start()
        silu = out * sigma * weight
        low = 0
        for j, b in enumerate(bounds + [width]):
            mine = jnp.logical_and(rows >= low, rows < b)
            totals[j] += jnp.sum(jnp.where(mine, silu, zero), axis=0, keepdims=True)
            low = b
    raw_out[...] = jnp.zeros_like(raw_out)
    for j in range(per_slab):
        raw_out[j : j + 1] = jnp.broadcast_to(jnp.sum(totals[j], axis=1, keepdims=True), (1, E))
    for c in copies:
        c.wait()


def grads_kernel(lengths, q, slope, head, out, *, scaling):
    width, flat = q.shape
    heads = flat // E
    count = out.shape[0]
    share = count // heads
    size = flat // count
    per_slab = lengths.shape[1]
    bounds = cand_bounds(lengths)
    rows = rows_of((width, E))
    zero = jnp.zeros((width, E), f32)
    for h in range(heads):
        at = slice(h * E, (h + 1) * E)
        mine = slope[:, at]
        high, low_part = [], []
        low = 0
        for b in bounds + [width]:
            kept = jnp.where(jnp.logical_and(rows >= low, rows < b), mine, zero)
            top = kept.astype(bf16)
            high.append(top)
            low_part.append((kept - top.astype(f32)).astype(bf16))
            low = b
        grads = dot(q[:, at], jnp.concatenate(high + low_part, axis=1), 0, 0)
        for j in range(per_slab):
            grad = grads[:, j * E : (j + 1) * E] + grads[:, (per_slab + j) * E : (per_slab + j + 1) * E]
            grad = (scaling * grad).astype(bf16)
            for o in range(share):
                out[h * share + o, j * size : (j + 1) * size] = grad[o * size : (o + 1) * size]
    for o in range(count):
        out[o, per_slab * size : (per_slab + 1) * size] = head[o, 0]


def append_kernel(payload, *refs, per_slab):
    raws, out, tile, sems = refs[:-3], refs[-3], refs[-2], refs[-1]
    total = raws[0][...]
    for r in raws[1:]:
        total += r[...]
    lines = []
    for j in range(per_slab):
        left = total[j : j + 1]
        for i in range(SCORE_PARTS):
            line = left.astype(bf16).astype(f32)
            lines.append(line)
            left = left - line
    lines.append(jnp.zeros((SCORE_ROWS - len(lines), E), f32))
    tile[...] = jnp.concatenate(lines, axis=0).astype(bf16)
    place = pl.ds(out.shape[1] - SCORE_ROWS, SCORE_ROWS)
    copies = [pltpu.make_async_copy(tile, out.at[o, place], sems.at[o]) for o in range(out.shape[0])]
    for c in copies:
        c.start()
    for c in copies:
        c.wait()


def listwise_kernel(
    ends,
    prompts,
    prompt_row,
    rank_row,
    grads,
    out,
    coef_out,
    loss_out,
    raw_held,
    coef_held,
    held,
    *,
    width,
):
    count = grads.shape[0]
    size = held.shape[1]
    per_slab = prompts.shape[0] // count
    cands = count * per_slab
    prompt_count = ends.shape[0]
    for e in range(count):
        tile = grads[e, (per_slab + 1) * size :].astype(f32)
        for j in range(per_slab):
            total = tile[SCORE_PARTS * j : SCORE_PARTS * j + 1]
            for i in range(1, SCORE_PARTS):
                total = total + tile[SCORE_PARTS * j + i : SCORE_PARTS * j + i + 1]
            raw_held[e * per_slab + j : e * per_slab + j + 1] = total
    raw = raw_held[...]
    square = (cands, cands)
    down = lax.broadcasted_iota(jnp.int32, square, 0)
    across = lax.broadcasted_iota(jnp.int32, square, 1)
    same_spot = down == across
    own = jnp.broadcast_to(prompt_row[...].astype(f32), square)
    own_down = jnp.sum(jnp.where(same_spot, own, 0.0), axis=1, keepdims=True)
    group = own == own_down
    rank_weight = jnp.broadcast_to(jnp.exp(-rank_row[...].astype(f32)), square)
    rank_down = jnp.sum(jnp.where(same_spot, rank_weight, 0.0), axis=1, keepdims=True)
    target = rank_down / jnp.sum(jnp.where(group, rank_weight, 0.0), axis=1, keepdims=True)
    tanh_raw = jnp.tanh(raw)
    squashed = 3.0 * tanh_raw
    exp_scores = jnp.exp(squashed)
    exp_across = jnp.sum(jnp.where(same_spot, exp_scores[:, :cands], 0.0), axis=0, keepdims=True)
    denom = jnp.sum(jnp.where(group, jnp.broadcast_to(exp_across, square), 0.0), axis=1, keepdims=True)
    terms = target * (squashed - jnp.log(denom))
    loss_out[...] = -jnp.sum(terms, axis=0, keepdims=True) / prompt_count
    coef = grad_scale / prompt_count * (exp_scores / denom - target) * 3.0 * (1.0 - tanh_raw * tanh_raw)
    coef_held[...] = coef
    me = lax.axis_index("seq")
    for j in range(per_slab):
        coef_out[j : j + 1] = coef_held[pl.ds(me * per_slab + j, 1)]
    held[...] = jnp.zeros_like(held)
    for c in range(cands):
        j = c % per_slab
        held[prompts[c]] += grads[c // per_slab, j * size : (j + 1) * size].astype(f32) * coef[c : c + 1]
    running = jnp.zeros((size, E), f32)
    for e in reversed(range(count)):
        start = e * width
        far = start + width
        first = count_ends(ends, start)
        last = count_ends(ends, far - 1)
        goes_on = ends[last] != far
        from_right = jnp.where(goes_on, running, 0.0)
        from_right_bf = from_right.astype(bf16)
        for m in range(ENDS):
            pid = first + m
            ended = end_of(ends, pid, far + 1) <= far
            here = held[jnp.minimum(pid, prompt_count - 1)]
            out[e, m] = jnp.where(ended, here, from_right).astype(bf16)
            if m == 0:
                running = grads[e, per_slab * size : (per_slab + 1) * size].astype(f32) + jnp.where(ended, here, running)
        out[e, ENDS] = from_right_bf


def cand_kernel(lengths, coef, q, k, v, slope, states, dq, dk, dv, *, scaling):
    width = q.shape[0]
    per_slab = lengths.shape[1]
    bounds = cand_bounds(lengths)
    rows = rows_of((width, E))
    dout = (pick_rows(rows, bounds, [coef[j : j + 1] for j in range(per_slab)]) * slope[...]).astype(bf16)
    wide = jnp.concatenate([load_matrix(states, j) for j in range(per_slab)], axis=0)
    crossed = dot(dout, wide, 1, 1)
    total = pick_rows(rows, bounds, [crossed[:, j * E : (j + 1) * E] for j in range(per_slab)])
    blocks = []
    for lo in range(0, width, STRIP):
        hi = lo + STRIP
        keep = strip_mask(lo, STRIP, width, bounds)
        keys = k[lo:hi]
        attn = jnp.where(keep, dot(keys, q[lo:], 1, 1), 0.0).astype(bf16)
        gw = jnp.where(keep, dot(v[lo:hi], dout[lo:], 1, 1), 0.0).astype(bf16)
        dk[lo:hi] = (scaling * dot(gw, q[lo:], 1, 0)).astype(bf16)
        dv[lo:hi] = (scaling * dot(attn, dout[lo:], 1, 0)).astype(bf16)
        total = total + dot(gw, keys, 0, 0)
        blocks.append((lo, hi, total[:STRIP]))
        total = total[STRIP:]
    for lo, hi, block in blocks:
        dq[lo:hi] = (scaling * block).astype(bf16)


def prompt_kernel(ends, q, k, v, g, dq, dk, dv, head):
    width = q.shape[0]
    scaling = 1.0 / math.sqrt(E * width)
    bounds = slab_bounds(ends, lax.axis_index("seq"), width)
    for lo in range(0, width, STRIP):
        hi = lo + STRIP
        keep = strip_mask(lo, STRIP, width, bounds)
        keys = k[lo:hi]
        attn = jnp.where(keep, dot(keys, q[lo:], 1, 1), 0.0).astype(bf16)
        gw = jnp.where(keep, dot(v[lo:hi], g[lo:], 1, 1), 0.0).astype(bf16)
        dk[lo:hi] = scaling * dot(gw, q[lo:], 1, 0)
        dv[lo:hi] = scaling * dot(attn, g[lo:], 1, 0)
        part = dot(gw, keys, 0, 0)
        if lo == 0:
            first = jnp.where(rows_of((width, E)) < bounds[0], g[...].astype(f32), 0.0).astype(bf16)
            store_parts(head, 0, scaling * dot(q[...], first, 0, 0))
            dq[...] = part
        else:
            dq[lo:] += part


def query_kernel(ends, part, g, states, dq):
    width = g.shape[0]
    scaling = 1.0 / math.sqrt(E * width)
    bounds = slab_bounds(ends, lax.axis_index("seq"), width)
    carry = load_matrix(states, states.shape[1] - 1)
    crossed = dot(g[...], carry, 1, 1)
    rows = rows_of((width, E))
    dq[...] = (scaling * (part[...] + jnp.where(rows < bounds[0], crossed, 0.0))).astype(bf16)


def fetch(pairs, columns, sems, first):
    copies = []
    for i, (a, b) in enumerate(pairs):
        copies.append(pltpu.make_async_copy(a.at[:, columns], b, sems.at[first + i]))
        copies[-1].start()
    return copies


def stage_kernel(dk_part, dv_part, k, v, partial, both, sems):
    ahead = partial.shape[2] // E
    copies = []
    for h in range(ahead):
        at = pl.ds(h * E, E)
        pairs = [(dk_part, partial.at[0]), (dv_part, partial.at[1]), (k, both.at[0]), (v, both.at[1])]
        copies += fetch([(a, b.at[:, at]) for a, b in pairs], at, sems, h * 4)
    for c in copies:
        c.wait()


def right_kernel(
    ends, partial, both, states, dk_in, dv_in, k_in, v_in, dk_out, dv_out, rest, rest_both, dk, dv, sems
):
    width, flat = dk_out.shape
    heads = flat // E
    ahead = partial.shape[2] // E
    waits = [[]] * ahead
    for h in range(ahead, heads):
        at = pl.ds((h - ahead) * E, E)
        pairs = [(k_in, rest_both.at[0]), (v_in, rest_both.at[1]), (dk_in, rest.at[0]), (dv_in, rest.at[1])]
        waits.append(fetch([(a, b.at[:, at]) for a, b in pairs], pl.ds(h * E, E), sems, h * 4))
    bounds = slab_bounds(ends, lax.axis_index("seq"), width)
    rows = rows_of((width, E))
    cut = lambda a: [a[:, m * E : (m + 1) * E] for m in range(PIECES)]
    copies = []
    for h in range(heads):
        near, kv, place = (partial, both, h) if h < ahead else (rest, rest_both, h - ahead)
        at = slice(place * E, (place + 1) * E)
        mine = slice(h * E, (h + 1) * E)
        for c in waits[h]:
            c.wait()
        mats = [load_matrix(states, m, h, states.shape[0] // heads) for m in range(PIECES)]
        by_v = dot(kv[1, :, at], jnp.concatenate(mats, axis=0), 1, 1)
        dk[:, mine] = (near[0, :, at] + pick_rows(rows, bounds, cut(by_v))).astype(bf16)
        by_k = dot(kv[0, :, at], jnp.concatenate(mats, axis=1), 1, 0)
        dv[:, mine] = (near[1, :, at] + pick_rows(rows, bounds, cut(by_k))).astype(bf16)
        columns = pl.ds(h * E, E)
        for i, (a, b) in enumerate(((dk, dk_out), (dv, dv_out))):
            copies.append(pltpu.make_async_copy(a.at[:, columns], b.at[:, columns], sems.at[(heads + h) * 4 + i]))
            copies[-1].start()
    for c in copies:
        c.wait()


def exchange(a):
    return lax.all_to_all(a, "seq", 0, 0, tiled=True)


def per_device(
    prompt_q,
    prompt_k,
    prompt_v,
    prompt_grad,
    cand_q,
    cand_k,
    cand_v,
    readout,
    prompt_ends,
    cand_lengths,
    cand_prompt,
    cand_ranks,
):
    width = prompt_q.shape[0]
    cand_width = cand_q.shape[0]
    flat = prompt_q.shape[1]
    heads = flat // E
    count = lax.axis_size("seq")
    groups = lax.axis_size("head")
    per_slab = cand_lengths.shape[1]
    cands = cand_prompt.shape[0]
    scaling = 1.0 / math.sqrt(E * width)
    rows = flat // count
    share = count // heads
    whole = pl.BlockSpec((width, E), lambda h: (0, h))
    cand_block = pl.BlockSpec((cand_width, E), lambda h: (0, h))
    like = jax.ShapeDtypeStruct

    def parts_block(n):
        return pl.BlockSpec((share, n, rows, E), lambda h: (h, 0, 0, 0))

    def hbm(*arrays):
        return [pltpu.with_memory_space_constraint(a, pltpu.HBM) for a in arrays]

    def near(*arrays):
        return [pltpu.with_memory_space_constraint(a, pltpu.VMEM) for a in arrays]

    prompt_in = (prompt_q, prompt_k, prompt_v, prompt_grad)
    pieces = call(
        sums_kernel,
        in_specs=[ANY] * 3,
        out_specs=VMEM,
        out_shape=like((count, PIECES, rows, E), bf16),
        scratch_shapes=[pltpu.SMEM(prompt_ends.shape, jnp.int32)]
        + [pltpu.VMEM((width, flat), bf16)] * 2
        + [pltpu.SemaphoreType.DMA((heads + 1, 2))],
        name="sums",
    )(*hbm(prompt_ends, prompt_k, prompt_v))
    parts = exchange(pieces)

    pieces, late_in = lax.optimization_barrier((pieces, prompt_in))
    dq_part, dk_part, dv_part, head_part = call(
        prompt_kernel,
        grid=(heads,),
        in_specs=[SMEM] + [whole] * 4,
        out_specs=[whole] * 3 + [parts_block(1)],
        out_shape=[pltpu.HBM((width, flat), f32)] * 3 + [like((count, 1, rows, E), bf16)],
        name="prompt",
    )(prompt_ends, *hbm(*late_in))
    parts, dq_part, dk_part, dv_part = lax.optimization_barrier((parts, dq_part, dk_part, dv_part))

    chained = call(
        lambda *refs: chain_kernel(*refs, width=width),
        in_specs=[SMEM, SMEM, VMEM],
        out_specs=VMEM,
        out_shape=like((count, per_slab + 1, rows, E), bf16),
        scratch_shapes=[pltpu.VMEM((prompt_ends.shape[0] + 1, rows, E), f32)],
        name="chain",
    )(prompt_ends, cand_prompt, parts)
    states = exchange(chained)

    chained, cand_in = lax.optimization_barrier((chained, (cand_q, cand_k, cand_v)))
    inside = call(
        inside_kernel,
        grid=(heads,),
        in_specs=[SMEM] + [cand_block] * 3,
        out_specs=cand_block,
        out_shape=like((cand_width, flat), f32),
        name="inside",
    )(cand_lengths, *hbm(*cand_in))

    near_q = near(cand_in[0])[0]
    slope, raw, slope_far = call(
        lambda *refs: scores_kernel(*refs, scaling=scaling),
        in_specs=[SMEM] + [VMEM] * 4,
        out_specs=[VMEM, VMEM, ANY],
        out_shape=[
            pltpu.VMEM((cand_width, flat), f32),
            like((8, E), f32),
            pltpu.HBM((cand_width, flat), f32),
        ],
        scratch_shapes=[pltpu.SemaphoreType.DMA((heads,))],
        name="scores",
    )(cand_lengths, near_q, inside, readout.reshape(1, flat), states)
    raws = [raw]
    for step in range(1, groups):
        raws.append(lax.ppermute(raw, "head", [(i, (i + step) % groups) for i in range(groups)]))
    payload_shape = (count, (per_slab + 1) * rows + SCORE_ROWS, E)
    grads = call(
        lambda *refs: grads_kernel(*refs, scaling=scaling),
        in_specs=[SMEM] + [VMEM] * 3,
        out_specs=VMEM,
        out_shape=pltpu.HBM(payload_shape, bf16),
        name="grads",
    )(cand_lengths, near_q, *near(slope), head_part)
    grads = call(
        lambda *refs: append_kernel(*refs, per_slab=per_slab),
        in_specs=[ANY] + [VMEM] * groups,
        out_specs=ANY,
        out_shape=pltpu.HBM(payload_shape, bf16),
        input_output_aliases={0: 0},
        scratch_shapes=[pltpu.VMEM((SCORE_ROWS, E), bf16), pltpu.SemaphoreType.DMA((count,))],
        name="append",
    )(*hbm(grads), *raws)
    all_grads = exchange(grads)

    grads, late_grad = lax.optimization_barrier((grads, prompt_grad))
    prompt_dq = call(
        query_kernel,
        grid=(heads,),
        in_specs=[SMEM, whole, whole, parts_block(per_slab + 1)],
        out_specs=whole,
        out_shape=pltpu.HBM((width, flat), bf16),
        name="query",
    )(prompt_ends, *hbm(dq_part, late_grad), states)
    all_grads, prompt_dq = lax.optimization_barrier((all_grads, prompt_dq))

    right, coef, loss = call(
        lambda *refs: listwise_kernel(*refs, width=width),
        in_specs=[SMEM, SMEM] + [VMEM] * 3,
        out_specs=[VMEM] * 3,
        out_shape=[
            like((count, PIECES, rows, E), bf16),
            like((8, E), f32),
            like((1, E), f32),
        ],
        scratch_shapes=[
            pltpu.VMEM((cands, E), f32),
            pltpu.VMEM((cands, E), f32),
            pltpu.VMEM((prompt_ends.shape[0], rows, E), f32),
        ],
        name="listwise",
    )(
        prompt_ends,
        cand_prompt,
        cand_prompt.reshape(1, cands),
        cand_ranks.reshape(1, cands),
        all_grads,
    )
    rights = exchange(right)

    cand_dq, cand_dk, cand_dv = call(
        lambda *refs: cand_kernel(*refs, scaling=scaling),
        grid=(heads,),
        in_specs=[SMEM, pl.BlockSpec((8, E), lambda h: (0, 0))]
        + [cand_block] * 4
        + [parts_block(per_slab + 1)],
        out_specs=[cand_block] * 3,
        out_shape=[pltpu.HBM((cand_width, flat), bf16)] * 3,
        name="cand",
    )(cand_lengths, coef, *hbm(*cand_in, slope_far), states)
    cand_dq, late = lax.optimization_barrier((cand_dq, (dk_part, dv_part, prompt_k, prompt_v)))
    ahead = flat // 2
    staged = call(
        stage_kernel,
        in_specs=[ANY] * 4,
        out_specs=[VMEM] * 2,
        out_shape=[pltpu.VMEM((2, width, ahead), f32), pltpu.VMEM((2, width, ahead), bf16)],
        scratch_shapes=[pltpu.SemaphoreType.DMA((heads * 4,))],
        name="stage",
    )(*hbm(*late))
    rights, staged = lax.optimization_barrier((rights, staged))

    prompt_dk, prompt_dv = call(
        right_kernel,
        in_specs=[SMEM] + [VMEM] * 3 + [ANY] * 4,
        out_specs=[ANY] * 2,
        out_shape=[pltpu.HBM((width, flat), bf16)] * 2,
        scratch_shapes=[
            pltpu.VMEM((2, width, flat - ahead), f32),
            pltpu.VMEM((2, width, flat - ahead), bf16),
            pltpu.VMEM((width, flat), bf16),
            pltpu.VMEM((width, flat), bf16),
            pltpu.SemaphoreType.DMA((8 * heads,)),
        ],
        name="right",
    )(prompt_ends, *near(*staged), rights, *hbm(*late))
    return (
        prompt_dq,
        prompt_dk,
        prompt_dv,
        cand_dq,
        cand_dk,
        cand_dv,
        loss[0, 0],
    )


def solution(mesh):
    tile = P("seq", "head")
    return jax.shard_map(
        per_device,
        mesh=mesh,
        in_specs=(tile,) * 7 + (P("head"), P(), P("seq", None), P(), P()),
        out_specs=(tile,) * 6 + (P(),),
        check_vma=False,
    )
```

```python
import math

import jax
import jax.numpy as jnp
from jax import lax
from jax.experimental import pallas as pl
from jax.experimental.pallas import tpu as pltpu
from jax.sharding import PartitionSpec as P

E = 128
ENDS = 2
PIECES = ENDS + 1
STRIP = 256
grad_scale = 1048576.0
f32 = jnp.float32
bf16 = jnp.bfloat16
SMEM = pl.BlockSpec(memory_space=pltpu.SMEM)
VMEM = pl.BlockSpec(memory_space=pltpu.VMEM)
ANY = pl.BlockSpec(memory_space=pl.ANY)
SCORE_ROWS = 16
SCORE_PARTS = 3


def dot(a, b, ca, cb):
    return lax.dot_general(a, b, (((ca,), (cb,)), ((), ())), preferred_element_type=f32)


def call(body, **kw):
    return pl.pallas_call(
        body,
        compiler_params=pltpu.CompilerParams(vmem_limit_bytes=24 * 1024 * 1024),
        **kw,
    )


def count_ends(ends, limit):
    total = jnp.int32(0)
    for p in range(ends.shape[0]):
        total += (ends[p] <= limit).astype(jnp.int32)
    return total


def end_of(ends, pid, none):
    last = ends.shape[0] - 1
    return jnp.where(pid <= last, ends[jnp.minimum(pid, last)], none)


def slab_bounds(ends, slab, width):
    start = slab * width
    first = count_ends(ends, start)
    far = start + width
    return [jnp.minimum(end_of(ends, first + m, far) - start, width) for m in range(ENDS)]


def slot_use(ends, slab, width):
    start = slab * width
    first = count_ends(ends, start)
    segments = count_ends(ends, start + width - 1) - first + 1
    begins = jnp.logical_or(start == 0, jnp.logical_and(first > 0, ends[jnp.maximum(first - 1, 0)] == start))
    closed = end_of(ends, first + 1, start) == start + width
    longer = 2 * (end_of(ends, first, start) - start) > width
    of_first = jnp.logical_and(jnp.logical_not(begins), jnp.logical_or(closed, longer))
    return segments, jnp.logical_or(segments == 1, of_first)


def pick_rows(rows, bounds, options):
    out = options[-1]
    for b, o in zip(reversed(bounds), reversed(options[:-1])):
        out = jnp.where(rows < b, o, out)
    return out


def rows_of(shape, start=0):
    return lax.broadcasted_iota(jnp.int32, shape, 0) + start


def strip_mask(lo, size, width, bounds):
    s = rows_of((size, 1), lo)
    t = lax.broadcasted_iota(jnp.int32, (size, width - lo), 1) + lo
    stop = pick_rows(s, bounds, [jnp.full((size, 1), b, jnp.int32) for b in bounds] + [width])
    return jnp.logical_and(t >= s, t < stop)


def store_parts(out, place, mat):
    parts, rows = out.shape[0], out.shape[2]
    for o in range(parts):
        out[o, place] = mat[o * rows : (o + 1) * rows].astype(bf16)


def load_matrix(ref, place, h=0, share=None):
    share = ref.shape[0] if share is None else share
    return jnp.concatenate([ref[h * share + o, place] for o in range(share)], axis=0)


def sums_kernel(ends_in, k_in, v_in, out, ends, k, v, sems):
    width, flat = k.shape
    heads = flat // E
    share = out.shape[0] // heads
    columns = [pl.ds(h * E, E) for h in range(heads)]
    fetch_ends = pltpu.make_async_copy(ends_in, ends, sems.at[heads, 0])
    fetch_ends.start()
    copies = [
        [
            pltpu.make_async_copy(a.at[:, columns[h]], b.at[:, columns[h]], sems.at[h, i])
            for i, (a, b) in enumerate(((k_in, k), (v_in, v)))
        ]
        for h in range(heads)
    ]
    for group in copies:
        for c in group:
            c.start()
    fetch_ends.wait()
    me = lax.axis_index("seq")
    bounds = slab_bounds(ends, me, width)
    segments, of_first = slot_use(ends, me, width)
    rows = rows_of((width, E))
    zero = jnp.zeros((width, E), f32)
    for h in range(heads):
        for c in copies[h]:
            c.wait()
        at = slice(h * E, (h + 1) * E)
        values = v[:, at].astype(f32)
        pieces = []
        low = 0
        for b in bounds + [width]:
            inside = jnp.logical_and(rows >= low, rows < b)
            pieces.append(jnp.where(inside, values, zero).astype(bf16))
            low = b
        sums = dot(k[:, at], jnp.concatenate(pieces, axis=1), 0, 0)
        mine = out.at[pl.ds(h * share, share)]
        cuts = [sums[:, m * E : (m + 1) * E] for m in range(PIECES)]
        source = jnp.where(of_first, cuts[0], cuts[1])
        spare = source - source.astype(bf16).astype(f32)
        store_parts(mine, 0, cuts[0])
        store_parts(mine, 1, jnp.where(segments == 1, spare, cuts[1]))
        store_parts(mine, 2, jnp.where(segments == PIECES, cuts[2], spare))


def chain_kernel(ends, cand_prompt, parts, out, held, *, width):
    count = parts.shape[0]
    per_slab = cand_prompt.shape[0] // count
    running = jnp.zeros(parts.shape[2:], f32)
    for e in range(count):
        start = e * width
        first = count_ends(ends, start)
        last = count_ends(ends, start + width - 1)
        begins = jnp.bool_(True) if e == 0 else ends[jnp.maximum(first - 1, 0)] == start
        if e > 0:
            begins = jnp.logical_and(first > 0, begins)
        incoming = jnp.where(begins, 0.0, running)
        out[e, per_slab] = incoming.astype(bf16)
        segments, of_first = slot_use(ends, jnp.int32(e), width)
        second = parts[e, 1].astype(f32)
        third = parts[e, 2].astype(f32)
        spare = jnp.where(segments == 1, second, jnp.where(segments == PIECES, 0.0, third))
        firsts = incoming + (parts[e, 0].astype(f32) + jnp.where(of_first, spare, 0.0))
        second = second + jnp.where(of_first, 0.0, spare)
        nowhere = ends.shape[0]
        for m, piece in enumerate((firsts, second)):
            ended = end_of(ends, first + m, start + width + 1) <= start + width
            held[jnp.where(ended, first + m, nowhere)] = piece
        running = jnp.where(last == first, firsts, jnp.where(last == first + 1, second, third))
    for c in range(cand_prompt.shape[0]):
        out[c // per_slab, c % per_slab] = held[cand_prompt[c]].astype(bf16)


def inside_kernel(lengths, q, k, v, out):
    width = q.shape[0]
    bounds = cand_bounds(lengths)
    for lo in range(0, width, STRIP):
        hi = lo + STRIP
        scores = dot(q[lo:hi], k[:hi], 1, 1)
        t = rows_of((STRIP, hi), lo)
        s = lax.broadcasted_iota(jnp.int32, (STRIP, hi), 1)
        begin = pick_rows(t[:, :1], bounds, [0] + [jnp.full((STRIP, 1), b, jnp.int32) for b in bounds])
        keep = jnp.logical_and(s <= t, s >= begin)
        out[lo:hi] = dot(jnp.where(keep, scores, 0.0).astype(bf16), v[:hi], 1, 0)


def cand_bounds(lengths):
    bounds = []
    total = jnp.int32(0)
    for j in range(lengths.shape[1] - 1):
        total += lengths[0, j]
        bounds.append(total)
    return bounds


def scores_kernel(lengths, q, inside, readout, states, slope_out, raw_out, *, scaling):
    width, flat = q.shape
    heads = flat // E
    per_slab = lengths.shape[1]
    bounds = cand_bounds(lengths)
    rows = rows_of((width, E))
    zero = jnp.zeros((width, E), f32)
    inverse = [1.0 / jnp.full((1, E), lengths[0, j], jnp.int32).astype(f32) for j in range(per_slab)]
    totals = [jnp.zeros((1, E), f32) for j in range(per_slab)]
    for h in range(heads):
        at = slice(h * E, (h + 1) * E)
        wide = [load_matrix(states, j, h, states.shape[0] // heads) for j in range(per_slab)]
        crossed = dot(q[:, at], jnp.concatenate(wide, axis=1), 1, 0)
        crossed = pick_rows(rows, bounds, [crossed[:, j * E : (j + 1) * E] for j in range(per_slab)])
        out = scaling * (inside[:, at] + crossed)
        weight = pick_rows(rows, bounds, inverse) * readout[:, at]
        sigma = jax.nn.sigmoid(out)
        slope_out[:, at] = weight * sigma * (1.0 + out * (1.0 - sigma))
        silu = out * sigma * weight
        low = 0
        for j, b in enumerate(bounds + [width]):
            mine = jnp.logical_and(rows >= low, rows < b)
            totals[j] += jnp.sum(jnp.where(mine, silu, zero), axis=0, keepdims=True)
            low = b
    raw_out[...] = jnp.zeros_like(raw_out)
    for j in range(per_slab):
        raw_out[j : j + 1] = jnp.broadcast_to(jnp.sum(totals[j], axis=1, keepdims=True), (1, E))


def save_kernel(near, far, sems):
    size = near.shape[0] // sems.shape[0]
    some = [pl.ds(i * size, size) for i in range(sems.shape[0])]
    copies = [pltpu.make_async_copy(near.at[a], far.at[a], sems.at[i]) for i, a in enumerate(some)]
    for c in copies:
        c.start()
    for c in copies:
        c.wait()


def grads_kernel(lengths, q, slope, head, out, sem, *, scaling):
    width, flat = q.shape
    heads = flat // E
    count = out.shape[0]
    share = count // heads
    size = flat // count
    per_slab = lengths.shape[1]
    bring = pltpu.make_async_copy(head.at[:, 0], out.at[:, pl.ds(per_slab * size, size)], sem)
    bring.start()
    bounds = cand_bounds(lengths)
    rows = rows_of((width, E))
    zero = jnp.zeros((width, E), f32)
    for h in range(heads):
        at = slice(h * E, (h + 1) * E)
        mine = slope[:, at]
        high, low_part = [], []
        low = 0
        for b in bounds + [width]:
            kept = jnp.where(jnp.logical_and(rows >= low, rows < b), mine, zero)
            top = kept.astype(bf16)
            high.append(top)
            low_part.append((kept - top.astype(f32)).astype(bf16))
            low = b
        grads = dot(q[:, at], jnp.concatenate(high + low_part, axis=1), 0, 0)
        for j in range(per_slab):
            grad = grads[:, j * E : (j + 1) * E] + grads[:, (per_slab + j) * E : (per_slab + j + 1) * E]
            grad = (scaling * grad).astype(bf16)
            for o in range(share):
                out[h * share + o, j * size : (j + 1) * size] = grad[o * size : (o + 1) * size]
    bring.wait()


def append_kernel(payload, *refs, per_slab):
    raws, out, tile, sems = refs[:-3], refs[-3], refs[-2], refs[-1]
    total = raws[0][...]
    for r in raws[1:]:
        total += r[...]
    lines = []
    for j in range(per_slab):
        left = total[j : j + 1]
        for i in range(SCORE_PARTS):
            line = left.astype(bf16).astype(f32)
            lines.append(line)
            left = left - line
    lines.append(jnp.zeros((SCORE_ROWS - len(lines), E), f32))
    tile[...] = jnp.concatenate(lines, axis=0).astype(bf16)
    place = pl.ds(out.shape[1] - SCORE_ROWS, SCORE_ROWS)
    copies = [pltpu.make_async_copy(tile, out.at[o, place], sems.at[o]) for o in range(out.shape[0])]
    for c in copies:
        c.start()
    for c in copies:
        c.wait()


def listwise_kernel(
    ends,
    prompts,
    prompt_row,
    rank_row,
    grads,
    out,
    coef_out,
    loss_out,
    raw_held,
    coef_held,
    held,
    *,
    width,
):
    count = grads.shape[0]
    size = held.shape[1]
    per_slab = prompts.shape[0] // count
    cands = count * per_slab
    prompt_count = ends.shape[0]
    for e in range(count):
        tile = grads[e, (per_slab + 1) * size :].astype(f32)
        for j in range(per_slab):
            total = tile[SCORE_PARTS * j : SCORE_PARTS * j + 1]
            for i in range(1, SCORE_PARTS):
                total = total + tile[SCORE_PARTS * j + i : SCORE_PARTS * j + i + 1]
            raw_held[e * per_slab + j : e * per_slab + j + 1] = total
    raw = raw_held[...]
    square = (cands, cands)
    down = lax.broadcasted_iota(jnp.int32, square, 0)
    across = lax.broadcasted_iota(jnp.int32, square, 1)
    same_spot = down == across
    own = jnp.broadcast_to(prompt_row[...].astype(f32), square)
    own_down = jnp.sum(jnp.where(same_spot, own, 0.0), axis=1, keepdims=True)
    group = own == own_down
    rank_weight = jnp.broadcast_to(jnp.exp(-rank_row[...].astype(f32)), square)
    rank_down = jnp.sum(jnp.where(same_spot, rank_weight, 0.0), axis=1, keepdims=True)
    target = rank_down / jnp.sum(jnp.where(group, rank_weight, 0.0), axis=1, keepdims=True)
    tanh_raw = jnp.tanh(raw)
    squashed = 3.0 * tanh_raw
    exp_scores = jnp.exp(squashed)
    exp_across = jnp.sum(jnp.where(same_spot, exp_scores[:, :cands], 0.0), axis=0, keepdims=True)
    denom = jnp.sum(jnp.where(group, jnp.broadcast_to(exp_across, square), 0.0), axis=1, keepdims=True)
    terms = target * (squashed - jnp.log(denom))
    loss_out[...] = -jnp.sum(terms, axis=0, keepdims=True) / prompt_count
    coef = grad_scale / prompt_count * (exp_scores / denom - target) * 3.0 * (1.0 - tanh_raw * tanh_raw)
    coef_held[...] = coef
    me = lax.axis_index("seq")
    for j in range(per_slab):
        coef_out[j : j + 1] = coef_held[pl.ds(me * per_slab + j, 1)]
    held[...] = jnp.zeros_like(held)
    for c in range(cands):
        j = c % per_slab
        held[prompts[c]] += grads[c // per_slab, j * size : (j + 1) * size].astype(f32) * coef[c : c + 1]
    running = jnp.zeros((size, E), f32)
    for e in reversed(range(count)):
        start = e * width
        far = start + width
        first = count_ends(ends, start)
        last = count_ends(ends, far - 1)
        goes_on = ends[last] != far
        from_right = jnp.where(goes_on, running, 0.0)
        from_right_bf = from_right.astype(bf16)
        for m in range(ENDS):
            pid = first + m
            ended = end_of(ends, pid, far + 1) <= far
            here = held[jnp.minimum(pid, prompt_count - 1)]
            out[e, m] = jnp.where(ended, here, from_right).astype(bf16)
            if m == 0:
                running = grads[e, per_slab * size : (per_slab + 1) * size].astype(f32) + jnp.where(ended, here, running)
        out[e, ENDS] = from_right_bf


def cand_kernel(lengths, coef, q, k, v, slope, states, dq, dk, dv, *, scaling):
    width = q.shape[0]
    per_slab = lengths.shape[1]
    bounds = cand_bounds(lengths)
    rows = rows_of((width, E))
    dout = (pick_rows(rows, bounds, [coef[j : j + 1] for j in range(per_slab)]) * slope[...]).astype(bf16)
    wide = jnp.concatenate([load_matrix(states, j) for j in range(per_slab)], axis=0)
    crossed = dot(dout, wide, 1, 1)
    total = pick_rows(rows, bounds, [crossed[:, j * E : (j + 1) * E] for j in range(per_slab)])
    blocks = []
    for lo in range(0, width, STRIP):
        hi = lo + STRIP
        keep = strip_mask(lo, STRIP, width, bounds)
        keys = k[lo:hi]
        attn = jnp.where(keep, dot(keys, q[lo:], 1, 1), 0.0).astype(bf16)
        gw = jnp.where(keep, dot(v[lo:hi], dout[lo:], 1, 1), 0.0).astype(bf16)
        dk[lo:hi] = (scaling * dot(gw, q[lo:], 1, 0)).astype(bf16)
        dv[lo:hi] = (scaling * dot(attn, dout[lo:], 1, 0)).astype(bf16)
        total = total + dot(gw, keys, 0, 0)
        blocks.append((lo, hi, total[:STRIP]))
        total = total[STRIP:]
    for lo, hi, block in blocks:
        dq[lo:hi] = (scaling * block).astype(bf16)


def prompt_kernel(ends, q, k, v, g, *refs):
    dq, dk, dv, head = refs[-4:]
    width = q.shape[0]
    scaling = 1.0 / math.sqrt(E * width)
    bounds = slab_bounds(ends, lax.axis_index("seq"), width)
    for lo in range(0, width, STRIP):
        hi = lo + STRIP
        keep = strip_mask(lo, STRIP, width, bounds)
        keys = k[lo:hi]
        attn = jnp.where(keep, dot(keys, q[lo:], 1, 1), 0.0).astype(bf16)
        gw = jnp.where(keep, dot(v[lo:hi], g[lo:], 1, 1), 0.0).astype(bf16)
        dk[lo:hi] = scaling * dot(gw, q[lo:], 1, 0)
        dv[lo:hi] = scaling * dot(attn, g[lo:], 1, 0)
        part = dot(gw, keys, 0, 0)
        if lo == 0:
            first = jnp.where(rows_of((width, E)) < bounds[0], g[...].astype(f32), 0.0).astype(bf16)
            store_parts(head, 0, scaling * dot(q[...], first, 0, 0))
            dq[...] = part
        else:
            dq[lo:] += part


def query_kernel(ends, part, g, states, dq):
    width = g.shape[0]
    scaling = 1.0 / math.sqrt(E * width)
    bounds = slab_bounds(ends, lax.axis_index("seq"), width)
    carry = load_matrix(states, states.shape[1] - 1)
    crossed = dot(g[...], carry, 1, 1)
    rows = rows_of((width, E))
    dq[...] = (scaling * (part[...] + jnp.where(rows < bounds[0], crossed, 0.0))).astype(bf16)


def fetch(pairs, columns, sems, first):
    copies = []
    for i, (a, b) in enumerate(pairs):
        copies.append(pltpu.make_async_copy(a.at[:, columns], b, sems.at[first + i]))
        copies[-1].start()
    return copies


def stage_kernel(dk_part, dv_part, k, v, partial, both, sems):
    ahead = partial.shape[2] // E
    copies = []
    for h in range(ahead):
        at = pl.ds(h * E, E)
        pairs = [(dk_part, partial.at[0]), (dv_part, partial.at[1]), (k, both.at[0]), (v, both.at[1])]
        copies += fetch([(a, b.at[:, at]) for a, b in pairs], at, sems, h * 4)
    for c in copies:
        c.wait()


def right_kernel(
    ends, partial, both, states, dk_in, dv_in, k_in, v_in, dk_out, dv_out, rest, rest_both, dk, dv, sems
):
    width, flat = dk_out.shape
    heads = flat // E
    ahead = partial.shape[2] // E
    waits = [[]] * ahead
    for h in range(ahead, heads):
        at = pl.ds((h - ahead) * E, E)
        pairs = [(k_in, rest_both.at[0]), (v_in, rest_both.at[1]), (dk_in, rest.at[0]), (dv_in, rest.at[1])]
        waits.append(fetch([(a, b.at[:, at]) for a, b in pairs], pl.ds(h * E, E), sems, h * 4))
    bounds = slab_bounds(ends, lax.axis_index("seq"), width)
    rows = rows_of((width, E))
    cut = lambda a: [a[:, m * E : (m + 1) * E] for m in range(PIECES)]
    copies = []
    for h in range(heads):
        near, kv, place = (partial, both, h) if h < ahead else (rest, rest_both, h - ahead)
        at = slice(place * E, (place + 1) * E)
        mine = slice(h * E, (h + 1) * E)
        for c in waits[h]:
            c.wait()
        mats = [load_matrix(states, m, h, states.shape[0] // heads) for m in range(PIECES)]
        by_v = dot(kv[1, :, at], jnp.concatenate(mats, axis=0), 1, 1)
        dk[:, mine] = (near[0, :, at] + pick_rows(rows, bounds, cut(by_v))).astype(bf16)
        by_k = dot(kv[0, :, at], jnp.concatenate(mats, axis=1), 1, 0)
        dv[:, mine] = (near[1, :, at] + pick_rows(rows, bounds, cut(by_k))).astype(bf16)
        columns = pl.ds(h * E, E)
        for i, (a, b) in enumerate(((dk, dk_out), (dv, dv_out))):
            copies.append(pltpu.make_async_copy(a.at[:, columns], b.at[:, columns], sems.at[(heads + h) * 4 + i]))
            copies[-1].start()
    for c in copies:
        c.wait()


def exchange(a):
    return lax.all_to_all(a, "seq", 0, 0, tiled=True)


def per_device(
    prompt_q,
    prompt_k,
    prompt_v,
    prompt_grad,
    cand_q,
    cand_k,
    cand_v,
    readout,
    prompt_ends,
    cand_lengths,
    cand_prompt,
    cand_ranks,
):
    width = prompt_q.shape[0]
    cand_width = cand_q.shape[0]
    flat = prompt_q.shape[1]
    heads = flat // E
    count = lax.axis_size("seq")
    groups = lax.axis_size("head")
    per_slab = cand_lengths.shape[1]
    cands = cand_prompt.shape[0]
    scaling = 1.0 / math.sqrt(E * width)
    rows = flat // count
    share = count // heads
    whole = pl.BlockSpec((width, E), lambda h: (0, h))
    cand_block = pl.BlockSpec((cand_width, E), lambda h: (0, h))
    like = jax.ShapeDtypeStruct

    def parts_block(n):
        return pl.BlockSpec((share, n, rows, E), lambda h: (h, 0, 0, 0))

    def hbm(*arrays):
        return [pltpu.with_memory_space_constraint(a, pltpu.HBM) for a in arrays]

    def near(*arrays):
        return [pltpu.with_memory_space_constraint(a, pltpu.VMEM) for a in arrays]

    prompt_in = (prompt_q, prompt_k, prompt_v, prompt_grad)
    pieces = call(
        sums_kernel,
        in_specs=[ANY] * 3,
        out_specs=VMEM,
        out_shape=like((count, PIECES, rows, E), bf16),
        scratch_shapes=[pltpu.SMEM(prompt_ends.shape, jnp.int32)]
        + [pltpu.VMEM((width, flat), bf16)] * 2
        + [pltpu.SemaphoreType.DMA((heads + 1, 2))],
        name="sums",
    )(*hbm(prompt_ends, prompt_k, prompt_v))
    parts = exchange(pieces)

    pieces, late_in = lax.optimization_barrier((pieces, prompt_in))
    late = max(1, heads // 4)
    partial_shapes = [pltpu.HBM((width, flat), f32)] * 3 + [pltpu.HBM((count, 1, rows, E), bf16)]

    def some_heads(from_head, how_many, arrays, held):
        columns = pl.BlockSpec((width, E), lambda h: (0, h + from_head))
        return call(
            prompt_kernel,
            grid=(how_many,),
            in_specs=[SMEM] + [columns] * 4 + [ANY] * len(held),
            out_specs=[columns] * 3
            + [pl.BlockSpec((share, 1, rows, E), lambda h: (h + from_head, 0, 0, 0))],
            out_shape=partial_shapes,
            input_output_aliases={5 + i: i for i in range(len(held))},
            name="prompt",
        )(prompt_ends, *hbm(*arrays), *hbm(*held))

    partials = some_heads(0, heads - late, late_in, [])
    parts, partials = lax.optimization_barrier((parts, partials))

    chained = call(
        lambda *refs: chain_kernel(*refs, width=width),
        in_specs=[SMEM, SMEM, VMEM],
        out_specs=VMEM,
        out_shape=like((count, per_slab + 1, rows, E), bf16),
        scratch_shapes=[pltpu.VMEM((prompt_ends.shape[0] + 1, rows, E), f32)],
        name="chain",
    )(prompt_ends, cand_prompt, parts)
    states = exchange(chained)

    chained, cand_in = lax.optimization_barrier((chained, (cand_q, cand_k, cand_v)))
    inside = call(
        inside_kernel,
        grid=(heads,),
        in_specs=[SMEM] + [cand_block] * 3,
        out_specs=cand_block,
        out_shape=like((cand_width, flat), f32),
        name="inside",
    )(cand_lengths, *hbm(*cand_in))

    inside, partials, late_in = lax.optimization_barrier((inside, partials, late_in))
    dq_part, dk_part, dv_part, head_part = some_heads(heads - late, late, late_in, partials)
    states, head_part = lax.optimization_barrier((states, head_part))
    near_q = near(cand_in[0])[0]
    slope, raw = call(
        lambda *refs: scores_kernel(*refs, scaling=scaling),
        in_specs=[SMEM] + [VMEM] * 4,
        out_specs=[VMEM, VMEM],
        out_shape=[pltpu.VMEM((cand_width, flat), f32), like((8, E), f32)],
        name="scores",
    )(cand_lengths, near_q, inside, readout.reshape(1, flat), states)
    raws = [raw]
    for step in range(1, groups):
        raws.append(lax.ppermute(raw, "head", [(i, (i + step) % groups) for i in range(groups)]))
    payload_shape = (count, (per_slab + 1) * rows + SCORE_ROWS, E)
    grads = call(
        lambda *refs: grads_kernel(*refs, scaling=scaling),
        in_specs=[SMEM, VMEM, VMEM, ANY],
        out_specs=VMEM,
        out_shape=pltpu.HBM(payload_shape, bf16),
        scratch_shapes=[pltpu.SemaphoreType.DMA],
        name="grads",
    )(cand_lengths, near_q, *near(slope), *hbm(head_part))
    grads = call(
        lambda *refs: append_kernel(*refs, per_slab=per_slab),
        in_specs=[ANY] + [VMEM] * groups,
        out_specs=ANY,
        out_shape=pltpu.HBM(payload_shape, bf16),
        input_output_aliases={0: 0},
        scratch_shapes=[pltpu.VMEM((SCORE_ROWS, E), bf16), pltpu.SemaphoreType.DMA((count,))],
        name="append",
    )(*hbm(grads), *raws)
    all_grads = exchange(grads)

    grads, late_grad, slope = lax.optimization_barrier((grads, prompt_grad, slope))
    slope_far = call(
        save_kernel,
        in_specs=[VMEM],
        out_specs=ANY,
        out_shape=pltpu.HBM((cand_width, flat), f32),
        scratch_shapes=[pltpu.SemaphoreType.DMA((4,))],
        name="save",
    )(*near(slope))
    prompt_dq = call(
        query_kernel,
        grid=(heads,),
        in_specs=[SMEM, whole, whole, parts_block(per_slab + 1)],
        out_specs=whole,
        out_shape=pltpu.HBM((width, flat), bf16),
        name="query",
    )(prompt_ends, *hbm(dq_part, late_grad), states)
    all_grads, prompt_dq, slope_far = lax.optimization_barrier((all_grads, prompt_dq, slope_far))

    right, coef, loss = call(
        lambda *refs: listwise_kernel(*refs, width=width),
        in_specs=[SMEM, SMEM] + [VMEM] * 3,
        out_specs=[VMEM] * 3,
        out_shape=[
            like((count, PIECES, rows, E), bf16),
            like((8, E), f32),
            like((1, E), f32),
        ],
        scratch_shapes=[
            pltpu.VMEM((cands, E), f32),
            pltpu.VMEM((cands, E), f32),
            pltpu.VMEM((prompt_ends.shape[0], rows, E), f32),
        ],
        name="listwise",
    )(
        prompt_ends,
        cand_prompt,
        cand_prompt.reshape(1, cands),
        cand_ranks.reshape(1, cands),
        all_grads,
    )
    rights = exchange(right)

    cand_dq, cand_dk, cand_dv = call(
        lambda *refs: cand_kernel(*refs, scaling=scaling),
        grid=(heads,),
        in_specs=[SMEM, pl.BlockSpec((8, E), lambda h: (0, 0))]
        + [cand_block] * 4
        + [parts_block(per_slab + 1)],
        out_specs=[cand_block] * 3,
        out_shape=[pltpu.HBM((cand_width, flat), bf16)] * 3,
        name="cand",
    )(cand_lengths, coef, *hbm(*cand_in, slope_far), states)
    cand_dq, late = lax.optimization_barrier((cand_dq, (dk_part, dv_part, prompt_k, prompt_v)))
    ahead = flat // 2
    staged = call(
        stage_kernel,
        in_specs=[ANY] * 4,
        out_specs=[VMEM] * 2,
        out_shape=[pltpu.VMEM((2, width, ahead), f32), pltpu.VMEM((2, width, ahead), bf16)],
        scratch_shapes=[pltpu.SemaphoreType.DMA((heads * 4,))],
        name="stage",
    )(*hbm(*late))
    rights, staged = lax.optimization_barrier((rights, staged))

    prompt_dk, prompt_dv = call(
        right_kernel,
        in_specs=[SMEM] + [VMEM] * 3 + [ANY] * 4,
        out_specs=[ANY] * 2,
        out_shape=[pltpu.HBM((width, flat), bf16)] * 2,
        scratch_shapes=[
            pltpu.VMEM((2, width, flat - ahead), f32),
            pltpu.VMEM((2, width, flat - ahead), bf16),
            pltpu.VMEM((width, flat), bf16),
            pltpu.VMEM((width, flat), bf16),
            pltpu.SemaphoreType.DMA((8 * heads,)),
        ],
        name="right",
    )(prompt_ends, *near(*staged), rights, *hbm(*late))
    return (
        prompt_dq,
        prompt_dk,
        prompt_dv,
        cand_dq,
        cand_dk,
        cand_dv,
        loss[0, 0],
    )


def solution(mesh):
    tile = P("seq", "head")
    return jax.shard_map(
        per_device,
        mesh=mesh,
        in_specs=(tile,) * 7 + (P("head"), P(), P("seq", None), P(), P()),
        out_specs=(tile,) * 6 + (P(),),
        check_vma=False,
    )
```

```python
import math

import jax
import jax.numpy as jnp
from jax import lax
from jax.experimental import pallas as pl
from jax.experimental.pallas import tpu as pltpu
from jax.sharding import PartitionSpec as P

E = 128
ENDS = 2
PIECES = ENDS + 1
STRIP = 256
grad_scale = 1048576.0
f32 = jnp.float32
bf16 = jnp.bfloat16
SMEM = pl.BlockSpec(memory_space=pltpu.SMEM)
VMEM = pl.BlockSpec(memory_space=pltpu.VMEM)
ANY = pl.BlockSpec(memory_space=pl.ANY)
SCORE_ROWS = 16
SCORE_PARTS = 3


def dot(a, b, ca, cb):
    return lax.dot_general(a, b, (((ca,), (cb,)), ((), ())), preferred_element_type=f32)


def call(body, **kw):
    return pl.pallas_call(
        body,
        compiler_params=pltpu.CompilerParams(vmem_limit_bytes=24 * 1024 * 1024),
        **kw,
    )


def count_ends(ends, limit):
    total = jnp.int32(0)
    for p in range(ends.shape[0]):
        total += (ends[p] <= limit).astype(jnp.int32)
    return total


def end_of(ends, pid, none):
    last = ends.shape[0] - 1
    return jnp.where(pid <= last, ends[jnp.minimum(pid, last)], none)


def slab_bounds(ends, slab, width):
    start = slab * width
    first = count_ends(ends, start)
    far = start + width
    return [jnp.minimum(end_of(ends, first + m, far) - start, width) for m in range(ENDS)]


def slot_use(ends, slab, width):
    start = slab * width
    first = count_ends(ends, start)
    segments = count_ends(ends, start + width - 1) - first + 1
    begins = jnp.logical_or(start == 0, jnp.logical_and(first > 0, ends[jnp.maximum(first - 1, 0)] == start))
    closed = end_of(ends, first + 1, start) == start + width
    longer = 2 * (end_of(ends, first, start) - start) > width
    of_first = jnp.logical_and(jnp.logical_not(begins), jnp.logical_or(closed, longer))
    return segments, jnp.logical_or(segments == 1, of_first)


def pick_rows(rows, bounds, options):
    out = options[-1]
    for b, o in zip(reversed(bounds), reversed(options[:-1])):
        out = jnp.where(rows < b, o, out)
    return out


def rows_of(shape, start=0):
    return lax.broadcasted_iota(jnp.int32, shape, 0) + start


def strip_mask(lo, size, width, bounds):
    s = rows_of((size, 1), lo)
    t = lax.broadcasted_iota(jnp.int32, (size, width - lo), 1) + lo
    stop = pick_rows(s, bounds, [jnp.full((size, 1), b, jnp.int32) for b in bounds] + [width])
    return jnp.logical_and(t >= s, t < stop)


def store_parts(out, place, mat):
    parts, rows = out.shape[0], out.shape[2]
    for o in range(parts):
        out[o, place] = mat[o * rows : (o + 1) * rows].astype(bf16)


def load_matrix(ref, place, h=0, share=None):
    share = ref.shape[0] if share is None else share
    return jnp.concatenate([ref[h * share + o, place] for o in range(share)], axis=0)


def sums_kernel(ends_in, k_in, v_in, out, ends, k, v, sems):
    width, flat = k.shape
    heads = flat // E
    share = out.shape[0] // heads
    columns = [pl.ds(h * E, E) for h in range(heads)]
    fetch_ends = pltpu.make_async_copy(ends_in, ends, sems.at[heads, 0])
    fetch_ends.start()
    copies = [
        [
            pltpu.make_async_copy(a.at[:, columns[h]], b.at[:, columns[h]], sems.at[h, i])
            for i, (a, b) in enumerate(((k_in, k), (v_in, v)))
        ]
        for h in range(heads)
    ]
    for group in copies:
        for c in group:
            c.start()
    fetch_ends.wait()
    me = lax.axis_index("seq")
    bounds = slab_bounds(ends, me, width)
    segments, of_first = slot_use(ends, me, width)
    rows = rows_of((width, E))
    zero = jnp.zeros((width, E), f32)
    for h in range(heads):
        for c in copies[h]:
            c.wait()
        at = slice(h * E, (h + 1) * E)
        values = v[:, at].astype(f32)
        pieces = []
        low = 0
        for b in bounds + [width]:
            inside = jnp.logical_and(rows >= low, rows < b)
            pieces.append(jnp.where(inside, values, zero).astype(bf16))
            low = b
        sums = dot(k[:, at], jnp.concatenate(pieces, axis=1), 0, 0)
        mine = out.at[pl.ds(h * share, share)]
        cuts = [sums[:, m * E : (m + 1) * E] for m in range(PIECES)]
        source = jnp.where(of_first, cuts[0], cuts[1])
        spare = source - source.astype(bf16).astype(f32)
        store_parts(mine, 0, cuts[0])
        store_parts(mine, 1, jnp.where(segments == 1, spare, cuts[1]))
        store_parts(mine, 2, jnp.where(segments == PIECES, cuts[2], spare))


def chain_kernel(ends, cand_prompt, parts, out, held, *, width):
    count = parts.shape[0]
    per_slab = cand_prompt.shape[0] // count
    running = jnp.zeros(parts.shape[2:], f32)
    for e in range(count):
        start = e * width
        first = count_ends(ends, start)
        last = count_ends(ends, start + width - 1)
        begins = jnp.bool_(True) if e == 0 else ends[jnp.maximum(first - 1, 0)] == start
        if e > 0:
            begins = jnp.logical_and(first > 0, begins)
        incoming = jnp.where(begins, 0.0, running)
        out[e, per_slab] = incoming.astype(bf16)
        segments, of_first = slot_use(ends, jnp.int32(e), width)
        second = parts[e, 1].astype(f32)
        third = parts[e, 2].astype(f32)
        spare = jnp.where(segments == 1, second, jnp.where(segments == PIECES, 0.0, third))
        firsts = incoming + (parts[e, 0].astype(f32) + jnp.where(of_first, spare, 0.0))
        second = second + jnp.where(of_first, 0.0, spare)
        nowhere = ends.shape[0]
        for m, piece in enumerate((firsts, second)):
            ended = end_of(ends, first + m, start + width + 1) <= start + width
            held[jnp.where(ended, first + m, nowhere)] = piece
        running = jnp.where(last == first, firsts, jnp.where(last == first + 1, second, third))
    for c in range(cand_prompt.shape[0]):
        out[c // per_slab, c % per_slab] = held[cand_prompt[c]].astype(bf16)


def inside_kernel(lengths, q, k, v, out):
    width = q.shape[0]
    bounds = cand_bounds(lengths)
    for lo in range(0, width, STRIP):
        hi = lo + STRIP
        scores = dot(q[lo:hi], k[:hi], 1, 1)
        t = rows_of((STRIP, hi), lo)
        s = lax.broadcasted_iota(jnp.int32, (STRIP, hi), 1)
        begin = pick_rows(t[:, :1], bounds, [0] + [jnp.full((STRIP, 1), b, jnp.int32) for b in bounds])
        keep = jnp.logical_and(s <= t, s >= begin)
        out[lo:hi] = dot(jnp.where(keep, scores, 0.0).astype(bf16), v[:hi], 1, 0)


def cand_bounds(lengths):
    bounds = []
    total = jnp.int32(0)
    for j in range(lengths.shape[1] - 1):
        total += lengths[0, j]
        bounds.append(total)
    return bounds


def scores_kernel(lengths, q, inside, readout, states, slope_out, raw_out, *, scaling):
    width, flat = q.shape
    heads = flat // E
    per_slab = lengths.shape[1]
    bounds = cand_bounds(lengths)
    rows = rows_of((width, E))
    zero = jnp.zeros((width, E), f32)
    inverse = [1.0 / jnp.full((1, E), lengths[0, j], jnp.int32).astype(f32) for j in range(per_slab)]
    totals = [jnp.zeros((1, E), f32) for j in range(per_slab)]
    for h in range(heads):
        at = slice(h * E, (h + 1) * E)
        wide = [load_matrix(states, j, h, states.shape[0] // heads) for j in range(per_slab)]
        crossed = dot(q[:, at], jnp.concatenate(wide, axis=1), 1, 0)
        crossed = pick_rows(rows, bounds, [crossed[:, j * E : (j + 1) * E] for j in range(per_slab)])
        out = scaling * (inside[:, at] + crossed)
        weight = pick_rows(rows, bounds, inverse) * readout[:, at]
        sigma = jax.nn.sigmoid(out)
        slope_out[:, at] = weight * sigma * (1.0 + out * (1.0 - sigma))
        silu = out * sigma * weight
        low = 0
        for j, b in enumerate(bounds + [width]):
            mine = jnp.logical_and(rows >= low, rows < b)
            totals[j] += jnp.sum(jnp.where(mine, silu, zero), axis=0, keepdims=True)
            low = b
    raw_out[...] = jnp.zeros_like(raw_out)
    for j in range(per_slab):
        raw_out[j : j + 1] = jnp.broadcast_to(jnp.sum(totals[j], axis=1, keepdims=True), (1, E))


def save_kernel(near, far, sems):
    size = near.shape[0] // sems.shape[0]
    some = [pl.ds(i * size, size) for i in range(sems.shape[0])]
    copies = [pltpu.make_async_copy(near.at[a], far.at[a], sems.at[i]) for i, a in enumerate(some)]
    for c in copies:
        c.start()
    for c in copies:
        c.wait()


def grads_kernel(lengths, q, slope, head, out, made, sems, *, scaling):
    width, flat = q.shape
    heads = flat // E
    count = out.shape[0]
    share = count // heads
    size = flat // count
    per_slab = lengths.shape[1]
    copies = [pltpu.make_async_copy(head.at[:, 0], out.at[:, pl.ds(per_slab * size, size)], sems.at[heads])]
    copies[0].start()
    bounds = cand_bounds(lengths)
    rows = rows_of((width, E))
    for h in range(heads):
        at = slice(h * E, (h + 1) * E)
        mine = slope[:, at]
        high = mine.astype(bf16)
        low_part = (mine - high.astype(f32)).astype(bf16)
        queries = q[:, at].astype(f32)
        masked = []
        low = 0
        for b in bounds + [width]:
            masked.append(jnp.where(jnp.logical_and(rows >= low, rows < b), queries, 0.0).astype(bf16))
            low = b
        grads = dot(jnp.concatenate(masked, axis=1), jnp.concatenate([high, low_part], axis=1), 0, 0)
        grads = (scaling * (grads[:, :E] + grads[:, E:])).astype(bf16)
        for j in range(per_slab):
            for o in range(share):
                start = j * E + o * size
                made[h * share + o, j * size : (j + 1) * size] = grads[start : start + size]
        some = pl.ds(h * share, share)
        copies.append(
            pltpu.make_async_copy(made.at[some], out.at[some, pl.ds(0, per_slab * size)], sems.at[h])
        )
        copies[-1].start()
    for c in copies:
        c.wait()


def append_kernel(payload, *refs, per_slab):
    raws, out, tile, sems = refs[:-3], refs[-3], refs[-2], refs[-1]
    total = raws[0][...]
    for r in raws[1:]:
        total += r[...]
    lines = []
    for j in range(per_slab):
        left = total[j : j + 1]
        for i in range(SCORE_PARTS):
            line = left.astype(bf16).astype(f32)
            lines.append(line)
            left = left - line
    lines.append(jnp.zeros((SCORE_ROWS - len(lines), E), f32))
    tile[...] = jnp.concatenate(lines, axis=0).astype(bf16)
    place = pl.ds(out.shape[1] - SCORE_ROWS, SCORE_ROWS)
    copies = [pltpu.make_async_copy(tile, out.at[o, place], sems.at[o]) for o in range(out.shape[0])]
    for c in copies:
        c.start()
    for c in copies:
        c.wait()


def listwise_kernel(
    ends,
    prompts,
    prompt_row,
    rank_row,
    grads,
    out,
    coef_out,
    loss_out,
    raw_held,
    coef_held,
    held,
    made,
    sems,
    *,
    width,
):
    count = grads.shape[0]
    size = held.shape[1]
    per_slab = prompts.shape[0] // count
    cands = count * per_slab
    prompt_count = ends.shape[0]
    for e in range(count):
        tile = grads[e, (per_slab + 1) * size :].astype(f32)
        for j in range(per_slab):
            total = tile[SCORE_PARTS * j : SCORE_PARTS * j + 1]
            for i in range(1, SCORE_PARTS):
                total = total + tile[SCORE_PARTS * j + i : SCORE_PARTS * j + i + 1]
            raw_held[e * per_slab + j : e * per_slab + j + 1] = total
    raw = raw_held[...]
    square = (cands, cands)
    down = lax.broadcasted_iota(jnp.int32, square, 0)
    across = lax.broadcasted_iota(jnp.int32, square, 1)
    same_spot = down == across
    own = jnp.broadcast_to(prompt_row[...].astype(f32), square)
    own_down = jnp.sum(jnp.where(same_spot, own, 0.0), axis=1, keepdims=True)
    group = own == own_down
    rank_weight = jnp.broadcast_to(jnp.exp(-rank_row[...].astype(f32)), square)
    rank_down = jnp.sum(jnp.where(same_spot, rank_weight, 0.0), axis=1, keepdims=True)
    target = rank_down / jnp.sum(jnp.where(group, rank_weight, 0.0), axis=1, keepdims=True)
    tanh_raw = jnp.tanh(raw)
    squashed = 3.0 * tanh_raw
    exp_scores = jnp.exp(squashed)
    exp_across = jnp.sum(jnp.where(same_spot, exp_scores[:, :cands], 0.0), axis=0, keepdims=True)
    denom = jnp.sum(jnp.where(group, jnp.broadcast_to(exp_across, square), 0.0), axis=1, keepdims=True)
    terms = target * (squashed - jnp.log(denom))
    loss_out[...] = -jnp.sum(terms, axis=0, keepdims=True) / prompt_count
    coef = grad_scale / prompt_count * (exp_scores / denom - target) * 3.0 * (1.0 - tanh_raw * tanh_raw)
    coef_held[...] = coef
    me = lax.axis_index("seq")
    for j in range(per_slab):
        coef_out[j : j + 1] = coef_held[pl.ds(me * per_slab + j, 1)]
    held[...] = jnp.zeros_like(held)
    for c in range(cands):
        j = c % per_slab
        held[prompts[c]] += grads[c // per_slab, j * size : (j + 1) * size].astype(f32) * coef[c : c + 1]
    running = jnp.zeros((size, E), f32)
    copies = []
    for e in reversed(range(count)):
        start = e * width
        far = start + width
        first = count_ends(ends, start)
        last = count_ends(ends, far - 1)
        goes_on = ends[last] != far
        from_right = jnp.where(goes_on, running, 0.0)
        from_right_bf = from_right.astype(bf16)
        for m in range(ENDS):
            pid = first + m
            ended = end_of(ends, pid, far + 1) <= far
            here = held[jnp.minimum(pid, prompt_count - 1)]
            made[e, m] = jnp.where(ended, here, from_right).astype(bf16)
            if m == 0:
                running = grads[e, per_slab * size : (per_slab + 1) * size].astype(f32) + jnp.where(ended, here, running)
        made[e, ENDS] = from_right_bf
        copies.append(pltpu.make_async_copy(made.at[e], out.at[e], sems.at[e]))
        copies[-1].start()
    for c in copies:
        c.wait()


def cand_kernel(lengths, coef, q, k, v, slope, states, dq, dk, dv, *, scaling):
    width = q.shape[0]
    per_slab = lengths.shape[1]
    bounds = cand_bounds(lengths)
    rows = rows_of((width, E))
    dout = (pick_rows(rows, bounds, [coef[j : j + 1] for j in range(per_slab)]) * slope[...]).astype(bf16)
    wide = jnp.concatenate([load_matrix(states, j) for j in range(per_slab)], axis=0)
    crossed = dot(dout, wide, 1, 1)
    total = pick_rows(rows, bounds, [crossed[:, j * E : (j + 1) * E] for j in range(per_slab)])
    blocks = []
    for lo in range(0, width, STRIP):
        hi = lo + STRIP
        keep = strip_mask(lo, STRIP, width, bounds)
        keys = k[lo:hi]
        attn = jnp.where(keep, dot(keys, q[lo:], 1, 1), 0.0).astype(bf16)
        gw = jnp.where(keep, dot(v[lo:hi], dout[lo:], 1, 1), 0.0).astype(bf16)
        dk[lo:hi] = (scaling * dot(gw, q[lo:], 1, 0)).astype(bf16)
        dv[lo:hi] = (scaling * dot(attn, dout[lo:], 1, 0)).astype(bf16)
        total = total + dot(gw, keys, 0, 0)
        blocks.append((lo, hi, total[:STRIP]))
        total = total[STRIP:]
    for lo, hi, block in blocks:
        dq[lo:hi] = (scaling * block).astype(bf16)


def prompt_kernel(ends, q, k, v, g, *refs):
    dq, dk, dv, head = refs[-4:]
    width = q.shape[0]
    scaling = 1.0 / math.sqrt(E * width)
    bounds = slab_bounds(ends, lax.axis_index("seq"), width)
    for lo in range(0, width, STRIP):
        hi = lo + STRIP
        keep = strip_mask(lo, STRIP, width, bounds)
        keys = k[lo:hi]
        attn = jnp.where(keep, dot(keys, q[lo:], 1, 1), 0.0).astype(bf16)
        gw = jnp.where(keep, dot(v[lo:hi], g[lo:], 1, 1), 0.0).astype(bf16)
        dk[lo:hi] = scaling * dot(gw, q[lo:], 1, 0)
        dv[lo:hi] = scaling * dot(attn, g[lo:], 1, 0)
        part = dot(gw, keys, 0, 0)
        if lo == 0:
            first = jnp.where(rows_of((width, E)) < bounds[0], g[...].astype(f32), 0.0).astype(bf16)
            store_parts(head, 0, scaling * dot(q[...], first, 0, 0))
            dq[...] = part
        else:
            dq[lo:] += part


def query_kernel(ends, part, g, states, dq):
    width = g.shape[0]
    scaling = 1.0 / math.sqrt(E * width)
    bounds = slab_bounds(ends, lax.axis_index("seq"), width)
    carry = load_matrix(states, states.shape[1] - 1)
    crossed = dot(g[...], carry, 1, 1)
    rows = rows_of((width, E))
    dq[...] = (scaling * (part[...] + jnp.where(rows < bounds[0], crossed, 0.0))).astype(bf16)


def fetch(pairs, columns, sems, first):
    copies = []
    for i, (a, b) in enumerate(pairs):
        copies.append(pltpu.make_async_copy(a.at[:, columns], b, sems.at[first + i]))
        copies[-1].start()
    return copies


def stage_kernel(dk_part, dv_part, k, v, partial, both, sems):
    ahead = partial.shape[2] // E
    copies = []
    for h in range(ahead):
        at = pl.ds(h * E, E)
        pairs = [(dk_part, partial.at[0]), (dv_part, partial.at[1]), (k, both.at[0]), (v, both.at[1])]
        copies += fetch([(a, b.at[:, at]) for a, b in pairs], at, sems, h * 4)
    for c in copies:
        c.wait()


def right_kernel(
    ends, partial, both, states, dk_in, dv_in, k_in, v_in, dk_out, dv_out, rest, rest_both, dk, dv, sems
):
    width, flat = dk_out.shape
    heads = flat // E
    ahead = partial.shape[2] // E
    waits = [[]] * ahead
    for h in range(ahead, heads):
        at = pl.ds((h - ahead) * E, E)
        pairs = [(k_in, rest_both.at[0]), (v_in, rest_both.at[1]), (dk_in, rest.at[0]), (dv_in, rest.at[1])]
        waits.append(fetch([(a, b.at[:, at]) for a, b in pairs], pl.ds(h * E, E), sems, h * 4))
    bounds = slab_bounds(ends, lax.axis_index("seq"), width)
    rows = rows_of((width, E))
    copies = []
    for h in range(heads):
        near, kv, place = (partial, both, h) if h < ahead else (rest, rest_both, h - ahead)
        at = slice(place * E, (place + 1) * E)
        mine = slice(h * E, (h + 1) * E)
        for c in waits[h]:
            c.wait()

        def finish(pieces):
            mats = [load_matrix(states, m, h, states.shape[0] // heads) for m in range(pieces)]
            cut = lambda a: [a[:, m * E : (m + 1) * E] for m in range(pieces)]
            some = bounds[: pieces - 1]
            by_v = dot(kv[1, :, at], jnp.concatenate(mats, axis=0), 1, 1)
            dk[:, mine] = (near[0, :, at] + pick_rows(rows, some, cut(by_v))).astype(bf16)
            by_k = dot(kv[0, :, at], jnp.concatenate(mats, axis=1), 1, 0)
            dv[:, mine] = (near[1, :, at] + pick_rows(rows, some, cut(by_k))).astype(bf16)

        pl.when(bounds[-1] < width)(lambda: finish(PIECES))
        pl.when(bounds[-1] >= width)(lambda: finish(PIECES - 1))
        columns = pl.ds(h * E, E)
        for i, (a, b) in enumerate(((dk, dk_out), (dv, dv_out))):
            copies.append(pltpu.make_async_copy(a.at[:, columns], b.at[:, columns], sems.at[(heads + h) * 4 + i]))
            copies[-1].start()
    for c in copies:
        c.wait()


def exchange(a):
    return lax.all_to_all(a, "seq", 0, 0, tiled=True)


def per_device(
    prompt_q,
    prompt_k,
    prompt_v,
    prompt_grad,
    cand_q,
    cand_k,
    cand_v,
    readout,
    prompt_ends,
    cand_lengths,
    cand_prompt,
    cand_ranks,
):
    width = prompt_q.shape[0]
    cand_width = cand_q.shape[0]
    flat = prompt_q.shape[1]
    heads = flat // E
    count = lax.axis_size("seq")
    groups = lax.axis_size("head")
    per_slab = cand_lengths.shape[1]
    cands = cand_prompt.shape[0]
    scaling = 1.0 / math.sqrt(E * width)
    rows = flat // count
    share = count // heads
    whole = pl.BlockSpec((width, E), lambda h: (0, h))
    cand_block = pl.BlockSpec((cand_width, E), lambda h: (0, h))
    like = jax.ShapeDtypeStruct

    def parts_block(n):
        return pl.BlockSpec((share, n, rows, E), lambda h: (h, 0, 0, 0))

    def hbm(*arrays):
        return [pltpu.with_memory_space_constraint(a, pltpu.HBM) for a in arrays]

    def near(*arrays):
        return [pltpu.with_memory_space_constraint(a, pltpu.VMEM) for a in arrays]

    prompt_in = (prompt_q, prompt_k, prompt_v, prompt_grad)
    pieces = call(
        sums_kernel,
        in_specs=[ANY] * 3,
        out_specs=VMEM,
        out_shape=like((count, PIECES, rows, E), bf16),
        scratch_shapes=[pltpu.SMEM(prompt_ends.shape, jnp.int32)]
        + [pltpu.VMEM((width, flat), bf16)] * 2
        + [pltpu.SemaphoreType.DMA((heads + 1, 2))],
        name="sums",
    )(*hbm(prompt_ends, prompt_k, prompt_v))
    parts = exchange(pieces)

    pieces, late_in = lax.optimization_barrier((pieces, prompt_in))
    late = max(1, heads // 4)
    partial_shapes = [pltpu.HBM((width, flat), f32)] * 3 + [pltpu.HBM((count, 1, rows, E), bf16)]

    def some_heads(from_head, how_many, arrays, held):
        columns = pl.BlockSpec((width, E), lambda h: (0, h + from_head))
        return call(
            prompt_kernel,
            grid=(how_many,),
            in_specs=[SMEM] + [columns] * 4 + [ANY] * len(held),
            out_specs=[columns] * 3
            + [pl.BlockSpec((share, 1, rows, E), lambda h: (h + from_head, 0, 0, 0))],
            out_shape=partial_shapes,
            input_output_aliases={5 + i: i for i in range(len(held))},
            name="prompt",
        )(prompt_ends, *hbm(*arrays), *hbm(*held))

    partials = some_heads(0, heads - late, late_in, [])
    parts, partials = lax.optimization_barrier((parts, partials))

    chained = call(
        lambda *refs: chain_kernel(*refs, width=width),
        in_specs=[SMEM, SMEM, VMEM],
        out_specs=VMEM,
        out_shape=like((count, per_slab + 1, rows, E), bf16),
        scratch_shapes=[pltpu.VMEM((prompt_ends.shape[0] + 1, rows, E), f32)],
        name="chain",
    )(prompt_ends, cand_prompt, parts)
    states = exchange(chained)

    chained, cand_in = lax.optimization_barrier((chained, (cand_q, cand_k, cand_v)))
    inside = call(
        inside_kernel,
        grid=(heads,),
        in_specs=[SMEM] + [cand_block] * 3,
        out_specs=cand_block,
        out_shape=like((cand_width, flat), f32),
        name="inside",
    )(cand_lengths, *hbm(*cand_in))

    inside, partials, late_in = lax.optimization_barrier((inside, partials, late_in))
    dq_part, dk_part, dv_part, head_part = some_heads(heads - late, late, late_in, partials)
    states, head_part = lax.optimization_barrier((states, head_part))
    near_q = near(cand_in[0])[0]
    slope, raw = call(
        lambda *refs: scores_kernel(*refs, scaling=scaling),
        in_specs=[SMEM] + [VMEM] * 4,
        out_specs=[VMEM, VMEM],
        out_shape=[pltpu.VMEM((cand_width, flat), f32), like((8, E), f32)],
        name="scores",
    )(cand_lengths, near_q, inside, readout.reshape(1, flat), states)
    raws = [raw]
    for step in range(1, groups):
        raws.append(lax.ppermute(raw, "head", [(i, (i + step) % groups) for i in range(groups)]))
    payload_shape = (count, (per_slab + 1) * rows + SCORE_ROWS, E)
    grads = call(
        lambda *refs: grads_kernel(*refs, scaling=scaling),
        in_specs=[SMEM, VMEM, VMEM, ANY],
        out_specs=ANY,
        out_shape=pltpu.HBM(payload_shape, bf16),
        scratch_shapes=[
            pltpu.VMEM((count, per_slab * rows, E), bf16),
            pltpu.SemaphoreType.DMA((heads + 1,)),
        ],
        name="grads",
    )(cand_lengths, near_q, *near(slope), *hbm(head_part))
    grads = call(
        lambda *refs: append_kernel(*refs, per_slab=per_slab),
        in_specs=[ANY] + [VMEM] * groups,
        out_specs=ANY,
        out_shape=pltpu.HBM(payload_shape, bf16),
        input_output_aliases={0: 0},
        scratch_shapes=[pltpu.VMEM((SCORE_ROWS, E), bf16), pltpu.SemaphoreType.DMA((count,))],
        name="append",
    )(*hbm(grads), *raws)
    all_grads = exchange(grads)

    grads, late_grad, slope = lax.optimization_barrier((grads, prompt_grad, slope))
    slope_far = call(
        save_kernel,
        in_specs=[VMEM],
        out_specs=ANY,
        out_shape=pltpu.HBM((cand_width, flat), f32),
        scratch_shapes=[pltpu.SemaphoreType.DMA((4,))],
        name="save",
    )(*near(slope))
    prompt_dq = call(
        query_kernel,
        grid=(heads,),
        in_specs=[SMEM, whole, whole, parts_block(per_slab + 1)],
        out_specs=whole,
        out_shape=pltpu.HBM((width, flat), bf16),
        name="query",
    )(prompt_ends, *hbm(dq_part, late_grad), states)
    all_grads, prompt_dq, slope_far = lax.optimization_barrier((all_grads, prompt_dq, slope_far))

    right, coef, loss = call(
        lambda *refs: listwise_kernel(*refs, width=width),
        in_specs=[SMEM, SMEM] + [VMEM] * 3,
        out_specs=[ANY, VMEM, VMEM],
        out_shape=[
            pltpu.HBM((count, PIECES, rows, E), bf16),
            like((8, E), f32),
            like((1, E), f32),
        ],
        scratch_shapes=[
            pltpu.VMEM((cands, E), f32),
            pltpu.VMEM((cands, E), f32),
            pltpu.VMEM((prompt_ends.shape[0], rows, E), f32),
            pltpu.VMEM((count, PIECES, rows, E), bf16),
            pltpu.SemaphoreType.DMA((count,)),
        ],
        name="listwise",
    )(
        prompt_ends,
        cand_prompt,
        cand_prompt.reshape(1, cands),
        cand_ranks.reshape(1, cands),
        all_grads,
    )
    rights = exchange(right)

    cand_dq, cand_dk, cand_dv = call(
        lambda *refs: cand_kernel(*refs, scaling=scaling),
        grid=(heads,),
        in_specs=[SMEM, pl.BlockSpec((8, E), lambda h: (0, 0))]
        + [cand_block] * 4
        + [parts_block(per_slab + 1)],
        out_specs=[cand_block] * 3,
        out_shape=[pltpu.HBM((cand_width, flat), bf16)] * 3,
        name="cand",
    )(cand_lengths, coef, *hbm(*cand_in, slope_far), states)
    cand_dq, late = lax.optimization_barrier((cand_dq, (dk_part, dv_part, prompt_k, prompt_v)))
    ahead = flat // 2
    staged = call(
        stage_kernel,
        in_specs=[ANY] * 4,
        out_specs=[VMEM] * 2,
        out_shape=[pltpu.VMEM((2, width, ahead), f32), pltpu.VMEM((2, width, ahead), bf16)],
        scratch_shapes=[pltpu.SemaphoreType.DMA((heads * 4,))],
        name="stage",
    )(*hbm(*late))
    rights, staged = lax.optimization_barrier((rights, staged))

    prompt_dk, prompt_dv = call(
        right_kernel,
        in_specs=[SMEM] + [VMEM] * 3 + [ANY] * 4,
        out_specs=[ANY] * 2,
        out_shape=[pltpu.HBM((width, flat), bf16)] * 2,
        scratch_shapes=[
            pltpu.VMEM((2, width, flat - ahead), f32),
            pltpu.VMEM((2, width, flat - ahead), bf16),
            pltpu.VMEM((width, flat), bf16),
            pltpu.VMEM((width, flat), bf16),
            pltpu.SemaphoreType.DMA((8 * heads,)),
        ],
        name="right",
    )(prompt_ends, *near(*staged), rights, *hbm(*late))
    return (
        prompt_dq,
        prompt_dk,
        prompt_dv,
        cand_dq,
        cand_dk,
        cand_dv,
        loss[0, 0],
    )


def solution(mesh):
    tile = P("seq", "head")
    return jax.shard_map(
        per_device,
        mesh=mesh,
        in_specs=(tile,) * 7 + (P("head"), P(), P("seq", None), P(), P()),
        out_specs=(tile,) * 6 + (P(),),
        check_vma=False,
    )
```

```python
import math

import jax
import jax.numpy as jnp
from jax import lax
from jax.experimental import pallas as pl
from jax.experimental.pallas import tpu as pltpu
from jax.sharding import PartitionSpec as P

E = 128
ENDS = 2
PIECES = ENDS + 1
STRIP = 256
grad_scale = 1048576.0
f32 = jnp.float32
bf16 = jnp.bfloat16
SMEM = pl.BlockSpec(memory_space=pltpu.SMEM)
VMEM = pl.BlockSpec(memory_space=pltpu.VMEM)
ANY = pl.BlockSpec(memory_space=pl.ANY)
SCORE_ROWS = 16
SCORE_PARTS = 3


def dot(a, b, ca, cb):
    return lax.dot_general(a, b, (((ca,), (cb,)), ((), ())), preferred_element_type=f32)


def call(body, **kw):
    return pl.pallas_call(
        body,
        compiler_params=pltpu.CompilerParams(vmem_limit_bytes=24 * 1024 * 1024),
        **kw,
    )


def count_ends(ends, limit):
    total = jnp.int32(0)
    for p in range(ends.shape[0]):
        total += (ends[p] <= limit).astype(jnp.int32)
    return total


def end_of(ends, pid, none):
    last = ends.shape[0] - 1
    return jnp.where(pid <= last, ends[jnp.minimum(pid, last)], none)


def slab_bounds(ends, slab, width):
    start = slab * width
    first = count_ends(ends, start)
    far = start + width
    return [jnp.minimum(end_of(ends, first + m, far) - start, width) for m in range(ENDS)]


def slot_use(ends, slab, width):
    start = slab * width
    first = count_ends(ends, start)
    segments = count_ends(ends, start + width - 1) - first + 1
    begins = jnp.logical_or(start == 0, jnp.logical_and(first > 0, ends[jnp.maximum(first - 1, 0)] == start))
    closed = end_of(ends, first + 1, start) == start + width
    longer = 2 * (end_of(ends, first, start) - start) > width
    of_first = jnp.logical_and(jnp.logical_not(begins), jnp.logical_or(closed, longer))
    return segments, jnp.logical_or(segments == 1, of_first)


def pick_rows(rows, bounds, options):
    out = options[-1]
    for b, o in zip(reversed(bounds), reversed(options[:-1])):
        out = jnp.where(rows < b, o, out)
    return out


def rows_of(shape, start=0):
    return lax.broadcasted_iota(jnp.int32, shape, 0) + start


def strip_mask(lo, size, width, bounds):
    s = rows_of((size, 1), lo)
    t = lax.broadcasted_iota(jnp.int32, (size, width - lo), 1) + lo
    stop = pick_rows(s, bounds, [jnp.full((size, 1), b, jnp.int32) for b in bounds] + [width])
    return jnp.logical_and(t >= s, t < stop)


def store_parts(out, place, mat):
    parts, rows = out.shape[0], out.shape[2]
    for o in range(parts):
        out[o, place] = mat[o * rows : (o + 1) * rows].astype(bf16)


def load_matrix(ref, place, h=0, share=None):
    share = ref.shape[0] if share is None else share
    return jnp.concatenate([ref[h * share + o, place] for o in range(share)], axis=0)


def sums_kernel(ends_in, k_in, v_in, out, ends, k, v, sems):
    width, flat = k.shape
    heads = flat // E
    share = out.shape[0] // heads
    columns = [pl.ds(h * E, E) for h in range(heads)]
    fetch_ends = pltpu.make_async_copy(ends_in, ends, sems.at[heads, 0])
    fetch_ends.start()
    copies = [
        [
            pltpu.make_async_copy(a.at[:, columns[h]], b.at[:, columns[h]], sems.at[h, i])
            for i, (a, b) in enumerate(((k_in, k), (v_in, v)))
        ]
        for h in range(heads)
    ]
    for group in copies:
        for c in group:
            c.start()
    fetch_ends.wait()
    me = lax.axis_index("seq")
    bounds = slab_bounds(ends, me, width)
    segments, of_first = slot_use(ends, me, width)
    rows = rows_of((width, E))
    zero = jnp.zeros((width, E), f32)
    for h in range(heads):
        for c in copies[h]:
            c.wait()
        at = slice(h * E, (h + 1) * E)
        values = v[:, at].astype(f32)
        pieces = []
        low = 0
        for b in bounds + [width]:
            inside = jnp.logical_and(rows >= low, rows < b)
            pieces.append(jnp.where(inside, values, zero).astype(bf16))
            low = b
        sums = dot(k[:, at], jnp.concatenate(pieces, axis=1), 0, 0)
        mine = out.at[pl.ds(h * share, share)]
        cuts = [sums[:, m * E : (m + 1) * E] for m in range(PIECES)]
        source = jnp.where(of_first, cuts[0], cuts[1])
        spare = source - source.astype(bf16).astype(f32)
        store_parts(mine, 0, cuts[0])
        store_parts(mine, 1, jnp.where(segments == 1, spare, cuts[1]))
        store_parts(mine, 2, jnp.where(segments == PIECES, cuts[2], spare))


def chain_kernel(ends, cand_prompt, parts, out, held, *, width):
    count = parts.shape[0]
    per_slab = cand_prompt.shape[0] // count
    running = jnp.zeros(parts.shape[2:], f32)
    for e in range(count):
        start = e * width
        first = count_ends(ends, start)
        last = count_ends(ends, start + width - 1)
        begins = jnp.bool_(True) if e == 0 else ends[jnp.maximum(first - 1, 0)] == start
        if e > 0:
            begins = jnp.logical_and(first > 0, begins)
        incoming = jnp.where(begins, 0.0, running)
        out[e, per_slab] = incoming.astype(bf16)
        segments, of_first = slot_use(ends, jnp.int32(e), width)
        second = parts[e, 1].astype(f32)
        third = parts[e, 2].astype(f32)
        spare = jnp.where(segments == 1, second, jnp.where(segments == PIECES, 0.0, third))
        firsts = incoming + (parts[e, 0].astype(f32) + jnp.where(of_first, spare, 0.0))
        second = second + jnp.where(of_first, 0.0, spare)
        nowhere = ends.shape[0]
        for m, piece in enumerate((firsts, second)):
            ended = end_of(ends, first + m, start + width + 1) <= start + width
            held[jnp.where(ended, first + m, nowhere)] = piece
        running = jnp.where(last == first, firsts, jnp.where(last == first + 1, second, third))
    for c in range(cand_prompt.shape[0]):
        out[c // per_slab, c % per_slab] = held[cand_prompt[c]].astype(bf16)


def inside_kernel(lengths, q, k, v, out):
    width = q.shape[0]
    bounds = cand_bounds(lengths)
    for lo in range(0, width, STRIP):
        hi = lo + STRIP
        scores = dot(q[lo:hi], k[:hi], 1, 1)
        t = rows_of((STRIP, hi), lo)
        s = lax.broadcasted_iota(jnp.int32, (STRIP, hi), 1)
        begin = pick_rows(t[:, :1], bounds, [0] + [jnp.full((STRIP, 1), b, jnp.int32) for b in bounds])
        keep = jnp.logical_and(s <= t, s >= begin)
        out[lo:hi] = dot(jnp.where(keep, scores, 0.0).astype(bf16), v[:hi], 1, 0)


def cand_bounds(lengths):
    bounds = []
    total = jnp.int32(0)
    for j in range(lengths.shape[1] - 1):
        total += lengths[0, j]
        bounds.append(total)
    return bounds


def scores_kernel(lengths, q, inside, readout, states, slope_out, raw_out, *, scaling):
    width, flat = q.shape
    heads = flat // E
    per_slab = lengths.shape[1]
    bounds = cand_bounds(lengths)
    rows = rows_of((width, E))
    zero = jnp.zeros((width, E), f32)
    inverse = [1.0 / jnp.full((1, E), lengths[0, j], jnp.int32).astype(f32) for j in range(per_slab)]
    totals = [jnp.zeros((1, E), f32) for j in range(per_slab)]
    for h in range(heads):
        at = slice(h * E, (h + 1) * E)
        wide = [load_matrix(states, j, h, states.shape[0] // heads) for j in range(per_slab)]
        crossed = dot(q[:, at], jnp.concatenate(wide, axis=1), 1, 0)
        crossed = pick_rows(rows, bounds, [crossed[:, j * E : (j + 1) * E] for j in range(per_slab)])
        out = scaling * (inside[:, at] + crossed)
        weight = pick_rows(rows, bounds, inverse) * readout[:, at]
        sigma = jax.nn.sigmoid(out)
        slope_out[:, at] = weight * sigma * (1.0 + out * (1.0 - sigma))
        silu = out * sigma * weight
        low = 0
        for j, b in enumerate(bounds + [width]):
            mine = jnp.logical_and(rows >= low, rows < b)
            totals[j] += jnp.sum(jnp.where(mine, silu, zero), axis=0, keepdims=True)
            low = b
    raw_out[...] = jnp.zeros_like(raw_out)
    for j in range(per_slab):
        raw_out[j : j + 1] = jnp.broadcast_to(jnp.sum(totals[j], axis=1, keepdims=True), (1, E))


def save_kernel(near, far, sems):
    size = near.shape[0] // sems.shape[0]
    some = [pl.ds(i * size, size) for i in range(sems.shape[0])]
    copies = [pltpu.make_async_copy(near.at[a], far.at[a], sems.at[i]) for i, a in enumerate(some)]
    for c in copies:
        c.start()
    for c in copies:
        c.wait()


def grads_kernel(lengths, q, slope, head, out, sem, *, scaling):
    width, flat = q.shape
    heads = flat // E
    count = out.shape[0]
    share = count // heads
    size = flat // count
    per_slab = lengths.shape[1]
    bring = pltpu.make_async_copy(head.at[:, 0], out.at[:, pl.ds(per_slab * size, size)], sem)
    bring.start()
    bounds = cand_bounds(lengths)
    rows = rows_of((width, E))
    for h in range(heads):
        at = slice(h * E, (h + 1) * E)
        mine = slope[:, at]
        high = mine.astype(bf16)
        low_part = (mine - high.astype(f32)).astype(bf16)
        queries = q[:, at].astype(f32)
        masked = []
        low = 0
        for b in bounds + [width]:
            masked.append(jnp.where(jnp.logical_and(rows >= low, rows < b), queries, 0.0).astype(bf16))
            low = b
        grads = dot(jnp.concatenate(masked, axis=1), jnp.concatenate([high, low_part], axis=1), 0, 0)
        grads = (scaling * (grads[:, :E] + grads[:, E:])).astype(bf16)
        for j in range(per_slab):
            for o in range(share):
                start = j * E + o * size
                out[h * share + o, j * size : (j + 1) * size] = grads[start : start + size]
    bring.wait()


def append_kernel(payload, *refs, per_slab):
    raws, out, tile, sems = refs[:-3], refs[-3], refs[-2], refs[-1]
    total = raws[0][...]
    for r in raws[1:]:
        total += r[...]
    lines = []
    for j in range(per_slab):
        left = total[j : j + 1]
        for i in range(SCORE_PARTS):
            line = left.astype(bf16).astype(f32)
            lines.append(line)
            left = left - line
    lines.append(jnp.zeros((SCORE_ROWS - len(lines), E), f32))
    tile[...] = jnp.concatenate(lines, axis=0).astype(bf16)
    place = pl.ds(out.shape[1] - SCORE_ROWS, SCORE_ROWS)
    copies = [pltpu.make_async_copy(tile, out.at[o, place], sems.at[o]) for o in range(out.shape[0])]
    for c in copies:
        c.start()
    for c in copies:
        c.wait()


def listwise_kernel(
    ends,
    prompts,
    prompt_row,
    rank_row,
    grads,
    out,
    coef_out,
    loss_out,
    raw_held,
    coef_held,
    held,
    *,
    width,
):
    count = grads.shape[0]
    size = held.shape[1]
    per_slab = prompts.shape[0] // count
    cands = count * per_slab
    prompt_count = ends.shape[0]
    for e in range(count):
        tile = grads[e, (per_slab + 1) * size :].astype(f32)
        for j in range(per_slab):
            total = tile[SCORE_PARTS * j : SCORE_PARTS * j + 1]
            for i in range(1, SCORE_PARTS):
                total = total + tile[SCORE_PARTS * j + i : SCORE_PARTS * j + i + 1]
            raw_held[e * per_slab + j : e * per_slab + j + 1] = total
    raw = raw_held[...]
    square = (cands, cands)
    down = lax.broadcasted_iota(jnp.int32, square, 0)
    across = lax.broadcasted_iota(jnp.int32, square, 1)
    same_spot = down == across
    own = jnp.broadcast_to(prompt_row[...].astype(f32), square)
    own_down = jnp.sum(jnp.where(same_spot, own, 0.0), axis=1, keepdims=True)
    group = own == own_down
    rank_weight = jnp.broadcast_to(jnp.exp(-rank_row[...].astype(f32)), square)
    rank_down = jnp.sum(jnp.where(same_spot, rank_weight, 0.0), axis=1, keepdims=True)
    target = rank_down / jnp.sum(jnp.where(group, rank_weight, 0.0), axis=1, keepdims=True)
    tanh_raw = jnp.tanh(raw)
    squashed = 3.0 * tanh_raw
    exp_scores = jnp.exp(squashed)
    exp_across = jnp.sum(jnp.where(same_spot, exp_scores[:, :cands], 0.0), axis=0, keepdims=True)
    denom = jnp.sum(jnp.where(group, jnp.broadcast_to(exp_across, square), 0.0), axis=1, keepdims=True)
    terms = target * (squashed - jnp.log(denom))
    loss_out[...] = -jnp.sum(terms, axis=0, keepdims=True) / prompt_count
    coef = grad_scale / prompt_count * (exp_scores / denom - target) * 3.0 * (1.0 - tanh_raw * tanh_raw)
    coef_held[...] = coef
    me = lax.axis_index("seq")
    for j in range(per_slab):
        coef_out[j : j + 1] = coef_held[pl.ds(me * per_slab + j, 1)]
    held[...] = jnp.zeros_like(held)
    for c in range(cands):
        j = c % per_slab
        held[prompts[c]] += grads[c // per_slab, j * size : (j + 1) * size].astype(f32) * coef[c : c + 1]
    running = jnp.zeros((size, E), f32)
    for e in reversed(range(count)):
        start = e * width
        far = start + width
        first = count_ends(ends, start)
        last = count_ends(ends, far - 1)
        goes_on = ends[last] != far
        from_right = jnp.where(goes_on, running, 0.0)
        from_right_bf = from_right.astype(bf16)
        for m in range(ENDS):
            pid = first + m
            ended = end_of(ends, pid, far + 1) <= far
            here = held[jnp.minimum(pid, prompt_count - 1)]
            out[e, m] = jnp.where(ended, here, from_right).astype(bf16)
            if m == 0:
                running = grads[e, per_slab * size : (per_slab + 1) * size].astype(f32) + jnp.where(ended, here, running)
        out[e, ENDS] = from_right_bf


def cand_kernel(lengths, coef, q, k, v, slope, states, dq, dk, dv, *, scaling):
    width = q.shape[0]
    per_slab = lengths.shape[1]
    bounds = cand_bounds(lengths)
    rows = rows_of((width, E))
    dout = (pick_rows(rows, bounds, [coef[j : j + 1] for j in range(per_slab)]) * slope[...]).astype(bf16)
    wide = jnp.concatenate([load_matrix(states, j) for j in range(per_slab)], axis=0)
    crossed = dot(dout, wide, 1, 1)
    total = pick_rows(rows, bounds, [crossed[:, j * E : (j + 1) * E] for j in range(per_slab)])
    blocks = []
    for lo in range(0, width, STRIP):
        hi = lo + STRIP
        keep = strip_mask(lo, STRIP, width, bounds)
        keys = k[lo:hi]
        attn = jnp.where(keep, dot(keys, q[lo:], 1, 1), 0.0).astype(bf16)
        gw = jnp.where(keep, dot(v[lo:hi], dout[lo:], 1, 1), 0.0).astype(bf16)
        dk[lo:hi] = (scaling * dot(gw, q[lo:], 1, 0)).astype(bf16)
        dv[lo:hi] = (scaling * dot(attn, dout[lo:], 1, 0)).astype(bf16)
        total = total + dot(gw, keys, 0, 0)
        blocks.append((lo, hi, total[:STRIP]))
        total = total[STRIP:]
    for lo, hi, block in blocks:
        dq[lo:hi] = (scaling * block).astype(bf16)


def prompt_kernel(ends, q, k, v, g, *refs):
    dq, dk, dv, head = refs[-4:]
    width = q.shape[0]
    scaling = 1.0 / math.sqrt(E * width)
    bounds = slab_bounds(ends, lax.axis_index("seq"), width)
    for lo in range(0, width, STRIP):
        hi = lo + STRIP
        keep = strip_mask(lo, STRIP, width, bounds)
        keys = k[lo:hi]
        attn = jnp.where(keep, dot(keys, q[lo:], 1, 1), 0.0).astype(bf16)
        gw = jnp.where(keep, dot(v[lo:hi], g[lo:], 1, 1), 0.0).astype(bf16)
        dk[lo:hi] = scaling * dot(gw, q[lo:], 1, 0)
        dv[lo:hi] = scaling * dot(attn, g[lo:], 1, 0)
        part = dot(gw, keys, 0, 0)
        if lo == 0:
            first = jnp.where(rows_of((width, E)) < bounds[0], g[...].astype(f32), 0.0).astype(bf16)
            store_parts(head, 0, scaling * dot(q[...], first, 0, 0))
            dq[...] = part
        else:
            dq[lo:] += part


def query_kernel(ends, part, g, states, dq):
    width = g.shape[0]
    scaling = 1.0 / math.sqrt(E * width)
    bounds = slab_bounds(ends, lax.axis_index("seq"), width)
    carry = load_matrix(states, states.shape[1] - 1)
    crossed = dot(g[...], carry, 1, 1)
    rows = rows_of((width, E))
    dq[...] = (scaling * (part[...] + jnp.where(rows < bounds[0], crossed, 0.0))).astype(bf16)


def fetch(pairs, columns, sems, first):
    copies = []
    for i, (a, b) in enumerate(pairs):
        copies.append(pltpu.make_async_copy(a.at[:, columns], b, sems.at[first + i]))
        copies[-1].start()
    return copies


def stage_kernel(dk_part, dv_part, k, v, partial, both, sems):
    ahead = partial.shape[2] // E
    copies = []
    for h in range(ahead):
        at = pl.ds(h * E, E)
        pairs = [(dk_part, partial.at[0]), (dv_part, partial.at[1]), (k, both.at[0]), (v, both.at[1])]
        copies += fetch([(a, b.at[:, at]) for a, b in pairs], at, sems, h * 4)
    for c in copies:
        c.wait()


def right_kernel(
    ends, partial, both, states, dk_in, dv_in, k_in, v_in, dk_out, dv_out, rest, rest_both, dk, dv, sems
):
    width, flat = dk_out.shape
    heads = flat // E
    ahead = partial.shape[2] // E
    waits = [[]] * ahead
    for h in range(ahead, heads):
        at = pl.ds((h - ahead) * E, E)
        pairs = [(k_in, rest_both.at[0]), (v_in, rest_both.at[1]), (dk_in, rest.at[0]), (dv_in, rest.at[1])]
        waits.append(fetch([(a, b.at[:, at]) for a, b in pairs], pl.ds(h * E, E), sems, h * 4))
    bounds = slab_bounds(ends, lax.axis_index("seq"), width)
    rows = rows_of((width, E))
    copies = []
    for h in range(heads):
        near, kv, place = (partial, both, h) if h < ahead else (rest, rest_both, h - ahead)
        at = slice(place * E, (place + 1) * E)
        mine = slice(h * E, (h + 1) * E)
        for c in waits[h]:
            c.wait()

        def finish(pieces):
            mats = [load_matrix(states, m, h, states.shape[0] // heads) for m in range(pieces)]
            cut = lambda a: [a[:, m * E : (m + 1) * E] for m in range(pieces)]
            some = bounds[: pieces - 1]
            by_v = dot(kv[1, :, at], jnp.concatenate(mats, axis=0), 1, 1)
            dk[:, mine] = (near[0, :, at] + pick_rows(rows, some, cut(by_v))).astype(bf16)
            by_k = dot(kv[0, :, at], jnp.concatenate(mats, axis=1), 1, 0)
            dv[:, mine] = (near[1, :, at] + pick_rows(rows, some, cut(by_k))).astype(bf16)

        pl.when(bounds[-1] < width)(lambda: finish(PIECES))
        pl.when(bounds[-1] >= width)(lambda: finish(PIECES - 1))
        columns = pl.ds(h * E, E)
        for i, (a, b) in enumerate(((dk, dk_out), (dv, dv_out))):
            copies.append(pltpu.make_async_copy(a.at[:, columns], b.at[:, columns], sems.at[(heads + h) * 4 + i]))
            copies[-1].start()
    for c in copies:
        c.wait()


def exchange(a):
    return lax.all_to_all(a, "seq", 0, 0, tiled=True)


def per_device(
    prompt_q,
    prompt_k,
    prompt_v,
    prompt_grad,
    cand_q,
    cand_k,
    cand_v,
    readout,
    prompt_ends,
    cand_lengths,
    cand_prompt,
    cand_ranks,
):
    width = prompt_q.shape[0]
    cand_width = cand_q.shape[0]
    flat = prompt_q.shape[1]
    heads = flat // E
    count = lax.axis_size("seq")
    groups = lax.axis_size("head")
    per_slab = cand_lengths.shape[1]
    cands = cand_prompt.shape[0]
    scaling = 1.0 / math.sqrt(E * width)
    rows = flat // count
    share = count // heads
    whole = pl.BlockSpec((width, E), lambda h: (0, h))
    cand_block = pl.BlockSpec((cand_width, E), lambda h: (0, h))
    like = jax.ShapeDtypeStruct

    def parts_block(n):
        return pl.BlockSpec((share, n, rows, E), lambda h: (h, 0, 0, 0))

    def hbm(*arrays):
        return [pltpu.with_memory_space_constraint(a, pltpu.HBM) for a in arrays]

    def near(*arrays):
        return [pltpu.with_memory_space_constraint(a, pltpu.VMEM) for a in arrays]

    prompt_in = (prompt_q, prompt_k, prompt_v, prompt_grad)
    pieces = call(
        sums_kernel,
        in_specs=[ANY] * 3,
        out_specs=VMEM,
        out_shape=like((count, PIECES, rows, E), bf16),
        scratch_shapes=[pltpu.SMEM(prompt_ends.shape, jnp.int32)]
        + [pltpu.VMEM((width, flat), bf16)] * 2
        + [pltpu.SemaphoreType.DMA((heads + 1, 2))],
        name="sums",
    )(*hbm(prompt_ends, prompt_k, prompt_v))
    parts = exchange(pieces)

    pieces, late_in = lax.optimization_barrier((pieces, prompt_in))
    late = max(1, heads // 4)
    partial_shapes = [pltpu.HBM((width, flat), f32)] * 3 + [pltpu.HBM((count, 1, rows, E), bf16)]

    def some_heads(from_head, how_many, arrays, held):
        columns = pl.BlockSpec((width, E), lambda h: (0, h + from_head))
        return call(
            prompt_kernel,
            grid=(how_many,),
            in_specs=[SMEM] + [columns] * 4 + [ANY] * len(held),
            out_specs=[columns] * 3
            + [pl.BlockSpec((share, 1, rows, E), lambda h: (h + from_head, 0, 0, 0))],
            out_shape=partial_shapes,
            input_output_aliases={5 + i: i for i in range(len(held))},
            name="prompt",
        )(prompt_ends, *hbm(*arrays), *hbm(*held))

    partials = some_heads(0, heads - late, late_in, [])
    parts, partials = lax.optimization_barrier((parts, partials))

    chained = call(
        lambda *refs: chain_kernel(*refs, width=width),
        in_specs=[SMEM, SMEM, VMEM],
        out_specs=VMEM,
        out_shape=like((count, per_slab + 1, rows, E), bf16),
        scratch_shapes=[pltpu.VMEM((prompt_ends.shape[0] + 1, rows, E), f32)],
        name="chain",
    )(prompt_ends, cand_prompt, parts)
    states = exchange(chained)

    chained, cand_in = lax.optimization_barrier((chained, (cand_q, cand_k, cand_v)))
    inside = call(
        inside_kernel,
        grid=(heads,),
        in_specs=[SMEM] + [cand_block] * 3,
        out_specs=cand_block,
        out_shape=like((cand_width, flat), f32),
        name="inside",
    )(cand_lengths, *hbm(*cand_in))

    inside, partials, late_in = lax.optimization_barrier((inside, partials, late_in))
    dq_part, dk_part, dv_part, head_part = some_heads(heads - late, late, late_in, partials)
    states, head_part = lax.optimization_barrier((states, head_part))
    near_q = near(cand_in[0])[0]
    slope, raw = call(
        lambda *refs: scores_kernel(*refs, scaling=scaling),
        in_specs=[SMEM] + [VMEM] * 4,
        out_specs=[VMEM, VMEM],
        out_shape=[pltpu.VMEM((cand_width, flat), f32), like((8, E), f32)],
        name="scores",
    )(cand_lengths, near_q, inside, readout.reshape(1, flat), states)
    raws = [raw]
    for step in range(1, groups):
        raws.append(lax.ppermute(raw, "head", [(i, (i + step) % groups) for i in range(groups)]))
    payload_shape = (count, (per_slab + 1) * rows + SCORE_ROWS, E)
    grads = call(
        lambda *refs: grads_kernel(*refs, scaling=scaling),
        in_specs=[SMEM, VMEM, VMEM, ANY],
        out_specs=VMEM,
        out_shape=pltpu.HBM(payload_shape, bf16),
        scratch_shapes=[pltpu.SemaphoreType.DMA],
        name="grads",
    )(cand_lengths, near_q, *near(slope), *hbm(head_part))
    grads = call(
        lambda *refs: append_kernel(*refs, per_slab=per_slab),
        in_specs=[ANY] + [VMEM] * groups,
        out_specs=ANY,
        out_shape=pltpu.HBM(payload_shape, bf16),
        input_output_aliases={0: 0},
        scratch_shapes=[pltpu.VMEM((SCORE_ROWS, E), bf16), pltpu.SemaphoreType.DMA((count,))],
        name="append",
    )(*hbm(grads), *raws)
    all_grads = exchange(grads)

    grads, late_grad, slope = lax.optimization_barrier((grads, prompt_grad, slope))
    slope_far = call(
        save_kernel,
        in_specs=[VMEM],
        out_specs=ANY,
        out_shape=pltpu.HBM((cand_width, flat), f32),
        scratch_shapes=[pltpu.SemaphoreType.DMA((4,))],
        name="save",
    )(*near(slope))
    prompt_dq = call(
        query_kernel,
        grid=(heads,),
        in_specs=[SMEM, whole, whole, parts_block(per_slab + 1)],
        out_specs=whole,
        out_shape=pltpu.HBM((width, flat), bf16),
        name="query",
    )(prompt_ends, *hbm(dq_part, late_grad), states)
    all_grads, prompt_dq, slope_far = lax.optimization_barrier((all_grads, prompt_dq, slope_far))

    right, coef, loss = call(
        lambda *refs: listwise_kernel(*refs, width=width),
        in_specs=[SMEM, SMEM] + [VMEM] * 3,
        out_specs=[VMEM] * 3,
        out_shape=[
            like((count, PIECES, rows, E), bf16),
            like((8, E), f32),
            like((1, E), f32),
        ],
        scratch_shapes=[
            pltpu.VMEM((cands, E), f32),
            pltpu.VMEM((cands, E), f32),
            pltpu.VMEM((prompt_ends.shape[0], rows, E), f32),
        ],
        name="listwise",
    )(
        prompt_ends,
        cand_prompt,
        cand_prompt.reshape(1, cands),
        cand_ranks.reshape(1, cands),
        all_grads,
    )
    rights = exchange(right)

    cand_dq, cand_dk, cand_dv = call(
        lambda *refs: cand_kernel(*refs, scaling=scaling),
        grid=(heads,),
        in_specs=[SMEM, pl.BlockSpec((8, E), lambda h: (0, 0))]
        + [cand_block] * 4
        + [parts_block(per_slab + 1)],
        out_specs=[cand_block] * 3,
        out_shape=[pltpu.HBM((cand_width, flat), bf16)] * 3,
        name="cand",
    )(cand_lengths, coef, *hbm(*cand_in, slope_far), states)
    cand_dq, late = lax.optimization_barrier((cand_dq, (dk_part, dv_part, prompt_k, prompt_v)))
    ahead = flat // 2
    staged = call(
        stage_kernel,
        in_specs=[ANY] * 4,
        out_specs=[VMEM] * 2,
        out_shape=[pltpu.VMEM((2, width, ahead), f32), pltpu.VMEM((2, width, ahead), bf16)],
        scratch_shapes=[pltpu.SemaphoreType.DMA((heads * 4,))],
        name="stage",
    )(*hbm(*late))
    rights, staged = lax.optimization_barrier((rights, staged))

    prompt_dk, prompt_dv = call(
        right_kernel,
        in_specs=[SMEM] + [VMEM] * 3 + [ANY] * 4,
        out_specs=[ANY] * 2,
        out_shape=[pltpu.HBM((width, flat), bf16)] * 2,
        scratch_shapes=[
            pltpu.VMEM((2, width, flat - ahead), f32),
            pltpu.VMEM((2, width, flat - ahead), bf16),
            pltpu.VMEM((width, flat), bf16),
            pltpu.VMEM((width, flat), bf16),
            pltpu.SemaphoreType.DMA((8 * heads,)),
        ],
        name="right",
    )(prompt_ends, *near(*staged), rights, *hbm(*late))
    return (
        prompt_dq,
        prompt_dk,
        prompt_dv,
        cand_dq,
        cand_dk,
        cand_dv,
        loss[0, 0],
    )


def solution(mesh):
    tile = P("seq", "head")
    return jax.shard_map(
        per_device,
        mesh=mesh,
        in_specs=(tile,) * 7 + (P("head"), P(), P("seq", None), P(), P()),
        out_specs=(tile,) * 6 + (P(),),
        check_vma=False,
    )
```

```python
import math

import jax
import jax.numpy as jnp
from jax import lax
from jax.experimental import pallas as pl
from jax.experimental.pallas import tpu as pltpu
from jax.sharding import PartitionSpec as P

E = 128
ENDS = 2
PIECES = ENDS + 1
STRIP = 256
grad_scale = 1048576.0
f32 = jnp.float32
bf16 = jnp.bfloat16
SMEM = pl.BlockSpec(memory_space=pltpu.SMEM)
VMEM = pl.BlockSpec(memory_space=pltpu.VMEM)
ANY = pl.BlockSpec(memory_space=pl.ANY)
SCORE_ROWS = 16
SCORE_PARTS = 3


def dot(a, b, ca, cb):
    return lax.dot_general(a, b, (((ca,), (cb,)), ((), ())), preferred_element_type=f32)


def call(body, **kw):
    return pl.pallas_call(
        body,
        compiler_params=pltpu.CompilerParams(vmem_limit_bytes=24 * 1024 * 1024),
        **kw,
    )


def small_first(body, arrays):
    n = len(arrays)

    def wrapped(*refs):
        held, sems = refs[-n - 1 : -1], refs[-1]
        copies = [pltpu.make_async_copy(refs[i], held[i], sems.at[i]) for i in range(n)]
        for c in copies:
            c.start()
        for c in copies:
            c.wait()
        body(*held, *refs[n : -n - 1])

    scratch = [pltpu.SMEM(a.shape, a.dtype) for a in arrays] + [pltpu.SemaphoreType.DMA((n,))]
    return wrapped, scratch


def count_ends(ends, limit):
    total = jnp.int32(0)
    for p in range(ends.shape[0]):
        total += (ends[p] <= limit).astype(jnp.int32)
    return total


def end_of(ends, pid, none):
    last = ends.shape[0] - 1
    return jnp.where(pid <= last, ends[jnp.minimum(pid, last)], none)


def slab_bounds(ends, slab, width):
    start = slab * width
    first = count_ends(ends, start)
    far = start + width
    return [jnp.minimum(end_of(ends, first + m, far) - start, width) for m in range(ENDS)]


def slot_use(ends, slab, width):
    start = slab * width
    first = count_ends(ends, start)
    segments = count_ends(ends, start + width - 1) - first + 1
    begins = jnp.logical_or(start == 0, jnp.logical_and(first > 0, ends[jnp.maximum(first - 1, 0)] == start))
    closed = end_of(ends, first + 1, start) == start + width
    longer = 2 * (end_of(ends, first, start) - start) > width
    of_first = jnp.logical_and(jnp.logical_not(begins), jnp.logical_or(closed, longer))
    return segments, jnp.logical_or(segments == 1, of_first)


def pick_rows(rows, bounds, options):
    out = options[-1]
    for b, o in zip(reversed(bounds), reversed(options[:-1])):
        out = jnp.where(rows < b, o, out)
    return out


def rows_of(shape, start=0):
    return lax.broadcasted_iota(jnp.int32, shape, 0) + start


def strip_mask(lo, size, width, bounds):
    s = rows_of((size, 1), lo)
    t = lax.broadcasted_iota(jnp.int32, (size, width - lo), 1) + lo
    stop = pick_rows(s, bounds, [jnp.full((size, 1), b, jnp.int32) for b in bounds] + [width])
    return jnp.logical_and(t >= s, t < stop)


def store_parts(out, place, mat):
    parts, rows = out.shape[0], out.shape[2]
    for o in range(parts):
        out[o, place] = mat[o * rows : (o + 1) * rows].astype(bf16)


def load_matrix(ref, place, h=0, share=None):
    share = ref.shape[0] if share is None else share
    return jnp.concatenate([ref[h * share + o, place] for o in range(share)], axis=0)


def sums_kernel(ends_in, k_in, v_in, out, ends, k, v, sems):
    width, flat = k.shape
    heads = flat // E
    share = out.shape[0] // heads
    columns = [pl.ds(h * E, E) for h in range(heads)]
    fetch_ends = pltpu.make_async_copy(ends_in, ends, sems.at[heads, 0])
    fetch_ends.start()
    copies = [
        [
            pltpu.make_async_copy(a.at[:, columns[h]], b.at[:, columns[h]], sems.at[h, i])
            for i, (a, b) in enumerate(((k_in, k), (v_in, v)))
        ]
        for h in range(heads)
    ]
    for group in copies:
        for c in group:
            c.start()
    fetch_ends.wait()
    me = lax.axis_index("seq")
    bounds = slab_bounds(ends, me, width)
    segments, of_first = slot_use(ends, me, width)
    rows = rows_of((width, E))
    zero = jnp.zeros((width, E), f32)
    for h in range(heads):
        for c in copies[h]:
            c.wait()
        at = slice(h * E, (h + 1) * E)
        values = v[:, at].astype(f32)
        pieces = []
        low = 0
        for b in bounds + [width]:
            inside = jnp.logical_and(rows >= low, rows < b)
            pieces.append(jnp.where(inside, values, zero).astype(bf16))
            low = b
        sums = dot(k[:, at], jnp.concatenate(pieces, axis=1), 0, 0)
        mine = out.at[pl.ds(h * share, share)]
        cuts = [sums[:, m * E : (m + 1) * E] for m in range(PIECES)]
        source = jnp.where(of_first, cuts[0], cuts[1])
        spare = source - source.astype(bf16).astype(f32)
        store_parts(mine, 0, cuts[0])
        store_parts(mine, 1, jnp.where(segments == 1, spare, cuts[1]))
        store_parts(mine, 2, jnp.where(segments == PIECES, cuts[2], spare))


def chain_kernel(ends, cand_prompt, parts, out, held, *, width):
    count = parts.shape[0]
    per_slab = cand_prompt.shape[0] // count
    running = jnp.zeros(parts.shape[2:], f32)
    for e in range(count):
        start = e * width
        first = count_ends(ends, start)
        last = count_ends(ends, start + width - 1)
        begins = jnp.bool_(True) if e == 0 else ends[jnp.maximum(first - 1, 0)] == start
        if e > 0:
            begins = jnp.logical_and(first > 0, begins)
        incoming = jnp.where(begins, 0.0, running)
        out[e, per_slab] = incoming.astype(bf16)
        segments, of_first = slot_use(ends, jnp.int32(e), width)
        second = parts[e, 1].astype(f32)
        third = parts[e, 2].astype(f32)
        spare = jnp.where(segments == 1, second, jnp.where(segments == PIECES, 0.0, third))
        firsts = incoming + (parts[e, 0].astype(f32) + jnp.where(of_first, spare, 0.0))
        second = second + jnp.where(of_first, 0.0, spare)
        nowhere = ends.shape[0]
        for m, piece in enumerate((firsts, second)):
            ended = end_of(ends, first + m, start + width + 1) <= start + width
            held[jnp.where(ended, first + m, nowhere)] = piece
        running = jnp.where(last == first, firsts, jnp.where(last == first + 1, second, third))
    for c in range(cand_prompt.shape[0]):
        out[c // per_slab, c % per_slab] = held[cand_prompt[c]].astype(bf16)


def inside_kernel(lengths, q, k, v, out):
    width = q.shape[0]
    bounds = cand_bounds(lengths)
    for lo in range(0, width, STRIP):
        hi = lo + STRIP
        scores = dot(q[lo:hi], k[:hi], 1, 1)
        t = rows_of((STRIP, hi), lo)
        s = lax.broadcasted_iota(jnp.int32, (STRIP, hi), 1)
        begin = pick_rows(t[:, :1], bounds, [0] + [jnp.full((STRIP, 1), b, jnp.int32) for b in bounds])
        keep = jnp.logical_and(s <= t, s >= begin)
        out[lo:hi] = dot(jnp.where(keep, scores, 0.0).astype(bf16), v[:hi], 1, 0)


def cand_bounds(lengths):
    bounds = []
    total = jnp.int32(0)
    for j in range(lengths.shape[1] - 1):
        total += lengths[0, j]
        bounds.append(total)
    return bounds


def scores_kernel(lengths, q, inside, readout, states, slope_out, raw_out, *, scaling):
    width, flat = q.shape
    heads = flat // E
    per_slab = lengths.shape[1]
    bounds = cand_bounds(lengths)
    rows = rows_of((width, E))
    zero = jnp.zeros((width, E), f32)
    inverse = [1.0 / jnp.full((1, E), lengths[0, j], jnp.int32).astype(f32) for j in range(per_slab)]
    totals = [jnp.zeros((1, E), f32) for j in range(per_slab)]
    for h in range(heads):
        at = slice(h * E, (h + 1) * E)
        wide = [load_matrix(states, j, h, states.shape[0] // heads) for j in range(per_slab)]
        crossed = dot(q[:, at], jnp.concatenate(wide, axis=1), 1, 0)
        crossed = pick_rows(rows, bounds, [crossed[:, j * E : (j + 1) * E] for j in range(per_slab)])
        out = scaling * (inside[:, at] + crossed)
        weight = pick_rows(rows, bounds, inverse) * readout[:, at]
        sigma = jax.nn.sigmoid(out)
        slope_out[:, at] = weight * sigma * (1.0 + out * (1.0 - sigma))
        silu = out * sigma * weight
        low = 0
        for j, b in enumerate(bounds + [width]):
            mine = jnp.logical_and(rows >= low, rows < b)
            totals[j] += jnp.sum(jnp.where(mine, silu, zero), axis=0, keepdims=True)
            low = b
    raw_out[...] = jnp.zeros_like(raw_out)
    for j in range(per_slab):
        raw_out[j : j + 1] = jnp.broadcast_to(jnp.sum(totals[j], axis=1, keepdims=True), (1, E))


def save_kernel(near, far, sems):
    size = near.shape[0] // sems.shape[0]
    some = [pl.ds(i * size, size) for i in range(sems.shape[0])]
    copies = [pltpu.make_async_copy(near.at[a], far.at[a], sems.at[i]) for i, a in enumerate(some)]
    for c in copies:
        c.start()
    for c in copies:
        c.wait()


def grads_kernel(lengths, q, slope, head, out, sem, *, scaling):
    width, flat = q.shape
    heads = flat // E
    count = out.shape[0]
    share = count // heads
    size = flat // count
    per_slab = lengths.shape[1]
    bring = pltpu.make_async_copy(head.at[:, 0], out.at[:, pl.ds(per_slab * size, size)], sem)
    bring.start()
    bounds = cand_bounds(lengths)
    rows = rows_of((width, E))
    for h in range(heads):
        at = slice(h * E, (h + 1) * E)
        mine = slope[:, at]
        high = mine.astype(bf16)
        low_part = (mine - high.astype(f32)).astype(bf16)
        queries = q[:, at].astype(f32)
        masked = []
        low = 0
        for b in bounds + [width]:
            masked.append(jnp.where(jnp.logical_and(rows >= low, rows < b), queries, 0.0).astype(bf16))
            low = b
        grads = dot(jnp.concatenate(masked, axis=1), jnp.concatenate([high, low_part], axis=1), 0, 0)
        grads = (scaling * (grads[:, :E] + grads[:, E:])).astype(bf16)
        for j in range(per_slab):
            for o in range(share):
                start = j * E + o * size
                out[h * share + o, j * size : (j + 1) * size] = grads[start : start + size]
    bring.wait()


def append_kernel(payload, *refs, per_slab):
    raws, out, tile, sems = refs[:-3], refs[-3], refs[-2], refs[-1]
    total = raws[0][...]
    for r in raws[1:]:
        total += r[...]
    lines = []
    for j in range(per_slab):
        left = total[j : j + 1]
        for i in range(SCORE_PARTS):
            line = left.astype(bf16).astype(f32)
            lines.append(line)
            left = left - line
    lines.append(jnp.zeros((SCORE_ROWS - len(lines), E), f32))
    tile[...] = jnp.concatenate(lines, axis=0).astype(bf16)
    place = pl.ds(out.shape[1] - SCORE_ROWS, SCORE_ROWS)
    copies = [pltpu.make_async_copy(tile, out.at[o, place], sems.at[o]) for o in range(out.shape[0])]
    for c in copies:
        c.start()
    for c in copies:
        c.wait()


def listwise_kernel(
    ends,
    prompts,
    prompt_row,
    rank_row,
    grads,
    out,
    coef_out,
    loss_out,
    raw_held,
    coef_held,
    held,
    *,
    width,
):
    count = grads.shape[0]
    size = held.shape[1]
    per_slab = prompts.shape[0] // count
    cands = count * per_slab
    prompt_count = ends.shape[0]
    for e in range(count):
        tile = grads[e, (per_slab + 1) * size :].astype(f32)
        for j in range(per_slab):
            total = tile[SCORE_PARTS * j : SCORE_PARTS * j + 1]
            for i in range(1, SCORE_PARTS):
                total = total + tile[SCORE_PARTS * j + i : SCORE_PARTS * j + i + 1]
            raw_held[e * per_slab + j : e * per_slab + j + 1] = total
    raw = raw_held[...]
    square = (cands, cands)
    down = lax.broadcasted_iota(jnp.int32, square, 0)
    across = lax.broadcasted_iota(jnp.int32, square, 1)
    same_spot = down == across
    own = jnp.broadcast_to(prompt_row[...].astype(f32), square)
    own_down = jnp.sum(jnp.where(same_spot, own, 0.0), axis=1, keepdims=True)
    group = own == own_down
    rank_weight = jnp.broadcast_to(jnp.exp(-rank_row[...].astype(f32)), square)
    rank_down = jnp.sum(jnp.where(same_spot, rank_weight, 0.0), axis=1, keepdims=True)
    target = rank_down / jnp.sum(jnp.where(group, rank_weight, 0.0), axis=1, keepdims=True)
    tanh_raw = jnp.tanh(raw)
    squashed = 3.0 * tanh_raw
    exp_scores = jnp.exp(squashed)
    exp_across = jnp.sum(jnp.where(same_spot, exp_scores[:, :cands], 0.0), axis=0, keepdims=True)
    denom = jnp.sum(jnp.where(group, jnp.broadcast_to(exp_across, square), 0.0), axis=1, keepdims=True)
    terms = target * (squashed - jnp.log(denom))
    loss_out[...] = -jnp.sum(terms, axis=0, keepdims=True) / prompt_count
    coef = grad_scale / prompt_count * (exp_scores / denom - target) * 3.0 * (1.0 - tanh_raw * tanh_raw)
    coef_held[...] = coef
    me = lax.axis_index("seq")
    for j in range(per_slab):
        coef_out[j : j + 1] = coef_held[pl.ds(me * per_slab + j, 1)]
    held[...] = jnp.zeros_like(held)
    for c in range(cands):
        j = c % per_slab
        held[prompts[c]] += grads[c // per_slab, j * size : (j + 1) * size].astype(f32) * coef[c : c + 1]
    running = jnp.zeros((size, E), f32)
    for e in reversed(range(count)):
        start = e * width
        far = start + width
        first = count_ends(ends, start)
        last = count_ends(ends, far - 1)
        goes_on = ends[last] != far
        from_right = jnp.where(goes_on, running, 0.0)
        from_right_bf = from_right.astype(bf16)
        for m in range(ENDS):
            pid = first + m
            ended = end_of(ends, pid, far + 1) <= far
            here = held[jnp.minimum(pid, prompt_count - 1)]
            out[e, m] = jnp.where(ended, here, from_right).astype(bf16)
            if m == 0:
                running = grads[e, per_slab * size : (per_slab + 1) * size].astype(f32) + jnp.where(ended, here, running)
        out[e, ENDS] = from_right_bf


def cand_kernel(lengths, coef, q, k, v, slope, states, dq, dk, dv, *, scaling):
    width = q.shape[0]
    per_slab = lengths.shape[1]
    bounds = cand_bounds(lengths)
    rows = rows_of((width, E))
    dout = (pick_rows(rows, bounds, [coef[j : j + 1] for j in range(per_slab)]) * slope[...]).astype(bf16)
    wide = jnp.concatenate([load_matrix(states, j) for j in range(per_slab)], axis=0)
    crossed = dot(dout, wide, 1, 1)
    total = pick_rows(rows, bounds, [crossed[:, j * E : (j + 1) * E] for j in range(per_slab)])
    blocks = []
    for lo in range(0, width, STRIP):
        hi = lo + STRIP
        keep = strip_mask(lo, STRIP, width, bounds)
        keys = k[lo:hi]
        attn = jnp.where(keep, dot(keys, q[lo:], 1, 1), 0.0).astype(bf16)
        gw = jnp.where(keep, dot(v[lo:hi], dout[lo:], 1, 1), 0.0).astype(bf16)
        dk[lo:hi] = (scaling * dot(gw, q[lo:], 1, 0)).astype(bf16)
        dv[lo:hi] = (scaling * dot(attn, dout[lo:], 1, 0)).astype(bf16)
        total = total + dot(gw, keys, 0, 0)
        blocks.append((lo, hi, total[:STRIP]))
        total = total[STRIP:]
    for lo, hi, block in blocks:
        dq[lo:hi] = (scaling * block).astype(bf16)


def prompt_kernel(ends, q, k, v, g, *refs):
    dq, dk, dv, head = refs[-4:]
    width = q.shape[0]
    scaling = 1.0 / math.sqrt(E * width)
    bounds = slab_bounds(ends, lax.axis_index("seq"), width)
    for lo in range(0, width, STRIP):
        hi = lo + STRIP
        keep = strip_mask(lo, STRIP, width, bounds)
        keys = k[lo:hi]
        attn = jnp.where(keep, dot(keys, q[lo:], 1, 1), 0.0).astype(bf16)
        gw = jnp.where(keep, dot(v[lo:hi], g[lo:], 1, 1), 0.0).astype(bf16)
        dk[lo:hi] = scaling * dot(gw, q[lo:], 1, 0)
        dv[lo:hi] = scaling * dot(attn, g[lo:], 1, 0)
        part = dot(gw, keys, 0, 0)
        if lo == 0:
            first = jnp.where(rows_of((width, E)) < bounds[0], g[...].astype(f32), 0.0).astype(bf16)
            store_parts(head, 0, scaling * dot(q[...], first, 0, 0))
            dq[...] = part
        else:
            dq[lo:] += part


def query_kernel(ends, part, g, states, dq):
    width = g.shape[0]
    scaling = 1.0 / math.sqrt(E * width)
    bounds = slab_bounds(ends, lax.axis_index("seq"), width)
    carry = load_matrix(states, states.shape[1] - 1)
    crossed = dot(g[...], carry, 1, 1)
    rows = rows_of((width, E))
    dq[...] = (scaling * (part[...] + jnp.where(rows < bounds[0], crossed, 0.0))).astype(bf16)


def fetch(pairs, columns, sems, first):
    copies = []
    for i, (a, b) in enumerate(pairs):
        copies.append(pltpu.make_async_copy(a.at[:, columns], b, sems.at[first + i]))
        copies[-1].start()
    return copies


def stage_kernel(dk_part, dv_part, k, v, partial, both, sems):
    ahead = partial.shape[2] // E
    copies = []
    for h in range(ahead):
        at = pl.ds(h * E, E)
        pairs = [(dk_part, partial.at[0]), (dv_part, partial.at[1]), (k, both.at[0]), (v, both.at[1])]
        copies += fetch([(a, b.at[:, at]) for a, b in pairs], at, sems, h * 4)
    for c in copies:
        c.wait()


def right_kernel(
    ends_in, partial, both, states, dk_in, dv_in, k_in, v_in, dk_out, dv_out, rest, rest_both, dk, dv, ends, sems
):
    width, flat = dk_out.shape
    heads = flat // E
    ahead = partial.shape[2] // E
    bring = pltpu.make_async_copy(ends_in, ends, sems.at[0])
    bring.start()
    waits = [[]] * ahead
    for h in range(ahead, heads):
        at = pl.ds((h - ahead) * E, E)
        pairs = [(k_in, rest_both.at[0]), (v_in, rest_both.at[1]), (dk_in, rest.at[0]), (dv_in, rest.at[1])]
        waits.append(fetch([(a, b.at[:, at]) for a, b in pairs], pl.ds(h * E, E), sems, h * 4))
    bring.wait()
    bounds = slab_bounds(ends, lax.axis_index("seq"), width)
    rows = rows_of((width, E))
    copies = []
    for h in range(heads):
        near, kv, place = (partial, both, h) if h < ahead else (rest, rest_both, h - ahead)
        at = slice(place * E, (place + 1) * E)
        mine = slice(h * E, (h + 1) * E)
        for c in waits[h]:
            c.wait()

        def finish(pieces):
            mats = [load_matrix(states, m, h, states.shape[0] // heads) for m in range(pieces)]
            cut = lambda a: [a[:, m * E : (m + 1) * E] for m in range(pieces)]
            some = bounds[: pieces - 1]
            by_v = dot(kv[1, :, at], jnp.concatenate(mats, axis=0), 1, 1)
            dk[:, mine] = (near[0, :, at] + pick_rows(rows, some, cut(by_v))).astype(bf16)
            by_k = dot(kv[0, :, at], jnp.concatenate(mats, axis=1), 1, 0)
            dv[:, mine] = (near[1, :, at] + pick_rows(rows, some, cut(by_k))).astype(bf16)

        pl.when(bounds[-1] < width)(lambda: finish(PIECES))
        pl.when(bounds[-1] >= width)(lambda: finish(PIECES - 1))
        columns = pl.ds(h * E, E)
        for i, (a, b) in enumerate(((dk, dk_out), (dv, dv_out))):
            copies.append(pltpu.make_async_copy(a.at[:, columns], b.at[:, columns], sems.at[(heads + h) * 4 + i]))
            copies[-1].start()
    for c in copies:
        c.wait()


def exchange(a):
    return lax.all_to_all(a, "seq", 0, 0, tiled=True)


def per_device(
    prompt_q,
    prompt_k,
    prompt_v,
    prompt_grad,
    cand_q,
    cand_k,
    cand_v,
    readout,
    prompt_ends,
    cand_lengths,
    cand_prompt,
    cand_ranks,
):
    width = prompt_q.shape[0]
    cand_width = cand_q.shape[0]
    flat = prompt_q.shape[1]
    heads = flat // E
    count = lax.axis_size("seq")
    groups = lax.axis_size("head")
    per_slab = cand_lengths.shape[1]
    cands = cand_prompt.shape[0]
    scaling = 1.0 / math.sqrt(E * width)
    rows = flat // count
    share = count // heads
    whole = pl.BlockSpec((width, E), lambda h: (0, h))
    cand_block = pl.BlockSpec((cand_width, E), lambda h: (0, h))
    like = jax.ShapeDtypeStruct

    def parts_block(n):
        return pl.BlockSpec((share, n, rows, E), lambda h: (h, 0, 0, 0))

    def hbm(*arrays):
        return [pltpu.with_memory_space_constraint(a, pltpu.HBM) for a in arrays]

    def near(*arrays):
        return [pltpu.with_memory_space_constraint(a, pltpu.VMEM) for a in arrays]

    prompt_in = (prompt_q, prompt_k, prompt_v, prompt_grad)
    pieces = call(
        sums_kernel,
        in_specs=[ANY] * 3,
        out_specs=VMEM,
        out_shape=like((count, PIECES, rows, E), bf16),
        scratch_shapes=[pltpu.SMEM(prompt_ends.shape, jnp.int32)]
        + [pltpu.VMEM((width, flat), bf16)] * 2
        + [pltpu.SemaphoreType.DMA((heads + 1, 2))],
        name="sums",
    )(*hbm(prompt_ends, prompt_k, prompt_v))
    parts = exchange(pieces)

    pieces, late_in = lax.optimization_barrier((pieces, prompt_in))
    late = max(1, heads // 4)
    partial_shapes = [pltpu.HBM((width, flat), f32)] * 3 + [pltpu.HBM((count, 1, rows, E), bf16)]

    def some_heads(from_head, how_many, arrays, held):
        columns = pl.BlockSpec((width, E), lambda h: (0, h + from_head))
        return call(
            prompt_kernel,
            grid=(how_many,),
            in_specs=[SMEM] + [columns] * 4 + [ANY] * len(held),
            out_specs=[columns] * 3
            + [pl.BlockSpec((share, 1, rows, E), lambda h: (h + from_head, 0, 0, 0))],
            out_shape=partial_shapes,
            input_output_aliases={5 + i: i for i in range(len(held))},
            name="prompt",
        )(prompt_ends, *hbm(*arrays), *hbm(*held))

    partials = some_heads(0, heads - late, late_in, [])
    parts, partials = lax.optimization_barrier((parts, partials))

    body, small = small_first(lambda *refs: chain_kernel(*refs, width=width), (prompt_ends, cand_prompt))
    chained = call(
        body,
        in_specs=[ANY, ANY, VMEM],
        out_specs=VMEM,
        out_shape=like((count, per_slab + 1, rows, E), bf16),
        scratch_shapes=[pltpu.VMEM((prompt_ends.shape[0] + 1, rows, E), f32)] + small,
        name="chain",
    )(prompt_ends, cand_prompt, parts)
    states = exchange(chained)

    chained, cand_in = lax.optimization_barrier((chained, (cand_q, cand_k, cand_v)))
    inside = call(
        inside_kernel,
        grid=(heads,),
        in_specs=[SMEM] + [cand_block] * 3,
        out_specs=cand_block,
        out_shape=like((cand_width, flat), f32),
        name="inside",
    )(cand_lengths, *hbm(*cand_in))

    inside, partials, late_in = lax.optimization_barrier((inside, partials, late_in))
    dq_part, dk_part, dv_part, head_part = some_heads(heads - late, late, late_in, partials)
    states, head_part = lax.optimization_barrier((states, head_part))
    near_q = near(cand_in[0])[0]
    slope, raw = call(
        lambda *refs: scores_kernel(*refs, scaling=scaling),
        in_specs=[SMEM] + [VMEM] * 4,
        out_specs=[VMEM, VMEM],
        out_shape=[pltpu.VMEM((cand_width, flat), f32), like((8, E), f32)],
        name="scores",
    )(cand_lengths, near_q, inside, readout.reshape(1, flat), states)
    raws = [raw]
    for step in range(1, groups):
        raws.append(lax.ppermute(raw, "head", [(i, (i + step) % groups) for i in range(groups)]))
    payload_shape = (count, (per_slab + 1) * rows + SCORE_ROWS, E)
    grads = call(
        lambda *refs: grads_kernel(*refs, scaling=scaling),
        in_specs=[SMEM, VMEM, VMEM, ANY],
        out_specs=VMEM,
        out_shape=pltpu.HBM(payload_shape, bf16),
        scratch_shapes=[pltpu.SemaphoreType.DMA],
        name="grads",
    )(cand_lengths, near_q, *near(slope), *hbm(head_part))
    grads = call(
        lambda *refs: append_kernel(*refs, per_slab=per_slab),
        in_specs=[ANY] + [VMEM] * groups,
        out_specs=ANY,
        out_shape=pltpu.HBM(payload_shape, bf16),
        input_output_aliases={0: 0},
        scratch_shapes=[pltpu.VMEM((SCORE_ROWS, E), bf16), pltpu.SemaphoreType.DMA((count,))],
        name="append",
    )(*hbm(grads), *raws)
    all_grads = exchange(grads)

    grads, late_grad, slope = lax.optimization_barrier((grads, prompt_grad, slope))
    slope_far = call(
        save_kernel,
        in_specs=[VMEM],
        out_specs=ANY,
        out_shape=pltpu.HBM((cand_width, flat), f32),
        scratch_shapes=[pltpu.SemaphoreType.DMA((4,))],
        name="save",
    )(*near(slope))
    prompt_dq = call(
        query_kernel,
        grid=(heads,),
        in_specs=[SMEM, whole, whole, parts_block(per_slab + 1)],
        out_specs=whole,
        out_shape=pltpu.HBM((width, flat), bf16),
        name="query",
    )(prompt_ends, *hbm(dq_part, late_grad), states)
    all_grads, prompt_dq, slope_far = lax.optimization_barrier((all_grads, prompt_dq, slope_far))

    body, small = small_first(lambda *refs: listwise_kernel(*refs, width=width), (prompt_ends, cand_prompt))
    right, coef, loss = call(
        body,
        in_specs=[ANY, ANY] + [VMEM] * 3,
        out_specs=[VMEM] * 3,
        out_shape=[
            like((count, PIECES, rows, E), bf16),
            like((8, E), f32),
            like((1, E), f32),
        ],
        scratch_shapes=[
            pltpu.VMEM((cands, E), f32),
            pltpu.VMEM((cands, E), f32),
            pltpu.VMEM((prompt_ends.shape[0], rows, E), f32),
        ]
        + small,
        name="listwise",
    )(
        prompt_ends,
        cand_prompt,
        cand_prompt.reshape(1, cands),
        cand_ranks.reshape(1, cands),
        all_grads,
    )
    rights = exchange(right)

    cand_dq, cand_dk, cand_dv = call(
        lambda *refs: cand_kernel(*refs, scaling=scaling),
        grid=(heads,),
        in_specs=[SMEM, pl.BlockSpec((8, E), lambda h: (0, 0))]
        + [cand_block] * 4
        + [parts_block(per_slab + 1)],
        out_specs=[cand_block] * 3,
        out_shape=[pltpu.HBM((cand_width, flat), bf16)] * 3,
        name="cand",
    )(cand_lengths, coef, *hbm(*cand_in, slope_far), states)
    cand_dq, late = lax.optimization_barrier((cand_dq, (dk_part, dv_part, prompt_k, prompt_v)))
    ahead = flat // 2
    staged = call(
        stage_kernel,
        in_specs=[ANY] * 4,
        out_specs=[VMEM] * 2,
        out_shape=[pltpu.VMEM((2, width, ahead), f32), pltpu.VMEM((2, width, ahead), bf16)],
        scratch_shapes=[pltpu.SemaphoreType.DMA((heads * 4,))],
        name="stage",
    )(*hbm(*late))
    rights, staged = lax.optimization_barrier((rights, staged))

    prompt_dk, prompt_dv = call(
        right_kernel,
        in_specs=[ANY] + [VMEM] * 3 + [ANY] * 4,
        out_specs=[ANY] * 2,
        out_shape=[pltpu.HBM((width, flat), bf16)] * 2,
        scratch_shapes=[
            pltpu.VMEM((2, width, flat - ahead), f32),
            pltpu.VMEM((2, width, flat - ahead), bf16),
            pltpu.VMEM((width, flat), bf16),
            pltpu.VMEM((width, flat), bf16),
            pltpu.SMEM(prompt_ends.shape, jnp.int32),
            pltpu.SemaphoreType.DMA((8 * heads,)),
        ],
        name="right",
    )(prompt_ends, *near(*staged), rights, *hbm(*late))
    return (
        prompt_dq,
        prompt_dk,
        prompt_dv,
        cand_dq,
        cand_dk,
        cand_dv,
        loss[0, 0],
    )


def solution(mesh):
    tile = P("seq", "head")
    return jax.shard_map(
        per_device,
        mesh=mesh,
        in_specs=(tile,) * 7 + (P("head"), P(), P("seq", None), P(), P()),
        out_specs=(tile,) * 6 + (P(),),
        check_vma=False,
    )
```

```python
import math

import jax
import jax.numpy as jnp
from jax import lax
from jax.experimental import pallas as pl
from jax.experimental.pallas import tpu as pltpu
from jax.sharding import PartitionSpec as P

E = 128
ENDS = 2
PIECES = ENDS + 1
STRIP = 256
grad_scale = 1048576.0
f32 = jnp.float32
bf16 = jnp.bfloat16
SMEM = pl.BlockSpec(memory_space=pltpu.SMEM)
VMEM = pl.BlockSpec(memory_space=pltpu.VMEM)
ANY = pl.BlockSpec(memory_space=pl.ANY)
SCORE_ROWS = 16
SCORE_PARTS = 3


def dot(a, b, ca, cb):
    return lax.dot_general(a, b, (((ca,), (cb,)), ((), ())), preferred_element_type=f32)


def call(body, **kw):
    return pl.pallas_call(
        body,
        compiler_params=pltpu.CompilerParams(vmem_limit_bytes=24 * 1024 * 1024),
        **kw,
    )


def small_first(body, arrays):
    n = len(arrays)

    def wrapped(*refs):
        held, sems = refs[-n - 1 : -1], refs[-1]
        copies = [pltpu.make_async_copy(refs[i], held[i], sems.at[i]) for i in range(n)]
        for c in copies:
            c.start()
        for c in copies:
            c.wait()
        body(*held, *refs[n : -n - 1])

    scratch = [pltpu.SMEM(a.shape, a.dtype) for a in arrays] + [pltpu.SemaphoreType.DMA((n,))]
    return wrapped, scratch


def count_ends(ends, limit):
    total = jnp.int32(0)
    for p in range(ends.shape[0]):
        total += (ends[p] <= limit).astype(jnp.int32)
    return total


def end_of(ends, pid, none):
    last = ends.shape[0] - 1
    return jnp.where(pid <= last, ends[jnp.minimum(pid, last)], none)


def slab_bounds(ends, slab, width):
    start = slab * width
    first = count_ends(ends, start)
    far = start + width
    return [jnp.minimum(end_of(ends, first + m, far) - start, width) for m in range(ENDS)]


def slot_use(ends, slab, width):
    start = slab * width
    first = count_ends(ends, start)
    segments = count_ends(ends, start + width - 1) - first + 1
    begins = jnp.logical_or(start == 0, jnp.logical_and(first > 0, ends[jnp.maximum(first - 1, 0)] == start))
    closed = end_of(ends, first + 1, start) == start + width
    longer = 2 * (end_of(ends, first, start) - start) > width
    of_first = jnp.logical_and(jnp.logical_not(begins), jnp.logical_or(closed, longer))
    return segments, jnp.logical_or(segments == 1, of_first)


def pick_rows(rows, bounds, options):
    out = options[-1]
    for b, o in zip(reversed(bounds), reversed(options[:-1])):
        out = jnp.where(rows < b, o, out)
    return out


def rows_of(shape, start=0):
    return lax.broadcasted_iota(jnp.int32, shape, 0) + start


def strip_mask(lo, size, width, bounds):
    s = rows_of((size, 1), lo)
    t = lax.broadcasted_iota(jnp.int32, (size, width - lo), 1) + lo
    stop = pick_rows(s, bounds, [jnp.full((size, 1), b, jnp.int32) for b in bounds] + [width])
    return jnp.logical_and(t >= s, t < stop)


def store_parts(out, place, mat):
    parts, rows = out.shape[0], out.shape[2]
    for o in range(parts):
        out[o, place] = mat[o * rows : (o + 1) * rows].astype(bf16)


def load_matrix(ref, place, h=0, share=None):
    share = ref.shape[0] if share is None else share
    return jnp.concatenate([ref[h * share + o, place] for o in range(share)], axis=0)


def sums_kernel(ends_in, k_in, v_in, out, ends, k, v, made, sems):
    width, flat = k.shape
    heads = flat // E
    share = out.shape[0] // heads
    columns = [pl.ds(h * E, E) for h in range(heads)]
    fetch_ends = pltpu.make_async_copy(ends_in, ends, sems.at[heads, 0])
    fetch_ends.start()
    copies = [
        [
            pltpu.make_async_copy(a.at[:, columns[h]], b.at[:, columns[h]], sems.at[h, i])
            for i, (a, b) in enumerate(((k_in, k), (v_in, v)))
        ]
        for h in range(heads)
    ]
    for group in copies:
        for c in group:
            c.start()
    fetch_ends.wait()
    me = lax.axis_index("seq")
    bounds = slab_bounds(ends, me, width)
    segments, of_first = slot_use(ends, me, width)
    rows = rows_of((width, E))
    zero = jnp.zeros((width, E), f32)
    results = []
    for h in range(heads):
        for c in copies[h]:
            c.wait()
        at = slice(h * E, (h + 1) * E)
        values = v[:, at].astype(f32)
        pieces = []
        low = 0
        for b in bounds + [width]:
            inside = jnp.logical_and(rows >= low, rows < b)
            pieces.append(jnp.where(inside, values, zero).astype(bf16))
            low = b
        sums = dot(k[:, at], jnp.concatenate(pieces, axis=1), 0, 0)
        some = pl.ds(h * share, share)
        mine = made.at[some]
        cuts = [sums[:, m * E : (m + 1) * E] for m in range(PIECES)]
        source = jnp.where(of_first, cuts[0], cuts[1])
        spare = source - source.astype(bf16).astype(f32)
        store_parts(mine, 0, cuts[0])
        store_parts(mine, 1, jnp.where(segments == 1, spare, cuts[1]))
        store_parts(mine, 2, jnp.where(segments == PIECES, cuts[2], spare))
        results.append(pltpu.make_async_copy(mine, out.at[some], sems.at[h, 2]))
        results[-1].start()
    for c in results:
        c.wait()


def chain_kernel(ends, cand_prompt, parts, out, held, *, width):
    count = parts.shape[0]
    per_slab = cand_prompt.shape[0] // count
    running = jnp.zeros(parts.shape[2:], f32)
    for e in range(count):
        start = e * width
        first = count_ends(ends, start)
        last = count_ends(ends, start + width - 1)
        begins = jnp.bool_(True) if e == 0 else ends[jnp.maximum(first - 1, 0)] == start
        if e > 0:
            begins = jnp.logical_and(first > 0, begins)
        incoming = jnp.where(begins, 0.0, running)
        out[e, per_slab] = incoming.astype(bf16)
        segments, of_first = slot_use(ends, jnp.int32(e), width)
        second = parts[e, 1].astype(f32)
        third = parts[e, 2].astype(f32)
        spare = jnp.where(segments == 1, second, jnp.where(segments == PIECES, 0.0, third))
        firsts = incoming + (parts[e, 0].astype(f32) + jnp.where(of_first, spare, 0.0))
        second = second + jnp.where(of_first, 0.0, spare)
        nowhere = ends.shape[0]
        for m, piece in enumerate((firsts, second)):
            ended = end_of(ends, first + m, start + width + 1) <= start + width
            held[jnp.where(ended, first + m, nowhere)] = piece
        running = jnp.where(last == first, firsts, jnp.where(last == first + 1, second, third))
    for c in range(cand_prompt.shape[0]):
        out[c // per_slab, c % per_slab] = held[cand_prompt[c]].astype(bf16)


def inside_kernel(lengths, q, k, v, out):
    width = q.shape[0]
    bounds = cand_bounds(lengths)
    for lo in range(0, width, STRIP):
        hi = lo + STRIP
        scores = dot(q[lo:hi], k[:hi], 1, 1)
        t = rows_of((STRIP, hi), lo)
        s = lax.broadcasted_iota(jnp.int32, (STRIP, hi), 1)
        begin = pick_rows(t[:, :1], bounds, [0] + [jnp.full((STRIP, 1), b, jnp.int32) for b in bounds])
        keep = jnp.logical_and(s <= t, s >= begin)
        out[lo:hi] = dot(jnp.where(keep, scores, 0.0).astype(bf16), v[:hi], 1, 0)


def cand_bounds(lengths):
    bounds = []
    total = jnp.int32(0)
    for j in range(lengths.shape[1] - 1):
        total += lengths[0, j]
        bounds.append(total)
    return bounds


def scores_kernel(lengths, q, inside, readout, states, slope_out, raw_out, *, scaling):
    width, flat = q.shape
    heads = flat // E
    per_slab = lengths.shape[1]
    bounds = cand_bounds(lengths)
    rows = rows_of((width, E))
    zero = jnp.zeros((width, E), f32)
    inverse = [1.0 / jnp.full((1, E), lengths[0, j], jnp.int32).astype(f32) for j in range(per_slab)]
    totals = [jnp.zeros((1, E), f32) for j in range(per_slab)]
    for h in range(heads):
        at = slice(h * E, (h + 1) * E)
        wide = [load_matrix(states, j, h, states.shape[0] // heads) for j in range(per_slab)]
        crossed = dot(q[:, at], jnp.concatenate(wide, axis=1), 1, 0)
        crossed = pick_rows(rows, bounds, [crossed[:, j * E : (j + 1) * E] for j in range(per_slab)])
        out = scaling * (inside[:, at] + crossed)
        weight = pick_rows(rows, bounds, inverse) * readout[:, at]
        sigma = jax.nn.sigmoid(out)
        slope_out[:, at] = weight * sigma * (1.0 + out * (1.0 - sigma))
        silu = out * sigma * weight
        low = 0
        for j, b in enumerate(bounds + [width]):
            mine = jnp.logical_and(rows >= low, rows < b)
            totals[j] += jnp.sum(jnp.where(mine, silu, zero), axis=0, keepdims=True)
            low = b
    raw_out[...] = jnp.zeros_like(raw_out)
    for j in range(per_slab):
        raw_out[j : j + 1] = jnp.broadcast_to(jnp.sum(totals[j], axis=1, keepdims=True), (1, E))


def save_kernel(near, far, sems):
    size = near.shape[0] // sems.shape[0]
    some = [pl.ds(i * size, size) for i in range(sems.shape[0])]
    copies = [pltpu.make_async_copy(near.at[a], far.at[a], sems.at[i]) for i, a in enumerate(some)]
    for c in copies:
        c.start()
    for c in copies:
        c.wait()


def grads_kernel(lengths, q, slope, head, out, made, passed, sems, *, scaling):
    width, flat = q.shape
    heads = flat // E
    count = out.shape[0]
    share = count // heads
    size = flat // count
    per_slab = lengths.shape[1]
    bring = pltpu.make_async_copy(head.at[:, 0], passed, sems.at[heads])
    bring.start()
    pass_on = pltpu.make_async_copy(passed, out.at[:, pl.ds(per_slab * size, size)], sems.at[heads + 1])
    results = [pass_on]
    bounds = cand_bounds(lengths)
    rows = rows_of((width, E))
    for h in range(heads):
        at = slice(h * E, (h + 1) * E)
        mine = slope[:, at]
        high = mine.astype(bf16)
        low_part = (mine - high.astype(f32)).astype(bf16)
        queries = q[:, at].astype(f32)
        masked = []
        low = 0
        for b in bounds + [width]:
            masked.append(jnp.where(jnp.logical_and(rows >= low, rows < b), queries, 0.0).astype(bf16))
            low = b
        grads = dot(jnp.concatenate(masked, axis=1), jnp.concatenate([high, low_part], axis=1), 0, 0)
        grads = (scaling * (grads[:, :E] + grads[:, E:])).astype(bf16)
        for j in range(per_slab):
            for o in range(share):
                start = j * E + o * size
                made[h * share + o, j * size : (j + 1) * size] = grads[start : start + size]
        if h == 0:
            bring.wait()
            pass_on.start()
        some = pl.ds(h * share, share)
        results.append(
            pltpu.make_async_copy(made.at[some], out.at[some, pl.ds(0, per_slab * size)], sems.at[h])
        )
        results[-1].start()
    for c in results:
        c.wait()


def append_kernel(payload, *refs, per_slab):
    raws, out, tile, sems = refs[:-3], refs[-3], refs[-2], refs[-1]
    total = raws[0][...]
    for r in raws[1:]:
        total += r[...]
    lines = []
    for j in range(per_slab):
        left = total[j : j + 1]
        for i in range(SCORE_PARTS):
            line = left.astype(bf16).astype(f32)
            lines.append(line)
            left = left - line
    lines.append(jnp.zeros((SCORE_ROWS - len(lines), E), f32))
    tile[...] = jnp.concatenate(lines, axis=0).astype(bf16)
    place = pl.ds(out.shape[1] - SCORE_ROWS, SCORE_ROWS)
    copies = [pltpu.make_async_copy(tile, out.at[o, place], sems.at[o]) for o in range(out.shape[0])]
    for c in copies:
        c.start()
    for c in copies:
        c.wait()


def listwise_kernel(
    ends,
    prompts,
    prompt_row,
    rank_row,
    grads,
    out,
    coef_out,
    loss_out,
    raw_held,
    coef_held,
    held,
    *,
    width,
):
    count = grads.shape[0]
    size = held.shape[1]
    per_slab = prompts.shape[0] // count
    cands = count * per_slab
    prompt_count = ends.shape[0]
    for e in range(count):
        tile = grads[e, (per_slab + 1) * size :].astype(f32)
        for j in range(per_slab):
            total = tile[SCORE_PARTS * j : SCORE_PARTS * j + 1]
            for i in range(1, SCORE_PARTS):
                total = total + tile[SCORE_PARTS * j + i : SCORE_PARTS * j + i + 1]
            raw_held[e * per_slab + j : e * per_slab + j + 1] = total
    raw = raw_held[...]
    square = (cands, cands)
    down = lax.broadcasted_iota(jnp.int32, square, 0)
    across = lax.broadcasted_iota(jnp.int32, square, 1)
    same_spot = down == across
    own = jnp.broadcast_to(prompt_row[...].astype(f32), square)
    own_down = jnp.sum(jnp.where(same_spot, own, 0.0), axis=1, keepdims=True)
    group = own == own_down
    rank_weight = jnp.broadcast_to(jnp.exp(-rank_row[...].astype(f32)), square)
    rank_down = jnp.sum(jnp.where(same_spot, rank_weight, 0.0), axis=1, keepdims=True)
    target = rank_down / jnp.sum(jnp.where(group, rank_weight, 0.0), axis=1, keepdims=True)
    tanh_raw = jnp.tanh(raw)
    squashed = 3.0 * tanh_raw
    exp_scores = jnp.exp(squashed)
    exp_across = jnp.sum(jnp.where(same_spot, exp_scores[:, :cands], 0.0), axis=0, keepdims=True)
    denom = jnp.sum(jnp.where(group, jnp.broadcast_to(exp_across, square), 0.0), axis=1, keepdims=True)
    terms = target * (squashed - jnp.log(denom))
    loss_out[...] = -jnp.sum(terms, axis=0, keepdims=True) / prompt_count
    coef = grad_scale / prompt_count * (exp_scores / denom - target) * 3.0 * (1.0 - tanh_raw * tanh_raw)
    coef_held[...] = coef
    me = lax.axis_index("seq")
    for j in range(per_slab):
        coef_out[j : j + 1] = coef_held[pl.ds(me * per_slab + j, 1)]
    held[...] = jnp.zeros_like(held)
    for c in range(cands):
        j = c % per_slab
        held[prompts[c]] += grads[c // per_slab, j * size : (j + 1) * size].astype(f32) * coef[c : c + 1]
    running = jnp.zeros((size, E), f32)
    for e in reversed(range(count)):
        start = e * width
        far = start + width
        first = count_ends(ends, start)
        last = count_ends(ends, far - 1)
        goes_on = ends[last] != far
        from_right = jnp.where(goes_on, running, 0.0)
        from_right_bf = from_right.astype(bf16)
        for m in range(ENDS):
            pid = first + m
            ended = end_of(ends, pid, far + 1) <= far
            here = held[jnp.minimum(pid, prompt_count - 1)]
            out[e, m] = jnp.where(ended, here, from_right).astype(bf16)
            if m == 0:
                running = grads[e, per_slab * size : (per_slab + 1) * size].astype(f32) + jnp.where(ended, here, running)
        out[e, ENDS] = from_right_bf


def cand_kernel(lengths, coef, q, k, v, slope, states, dq, dk, dv, *, scaling):
    width = q.shape[0]
    per_slab = lengths.shape[1]
    bounds = cand_bounds(lengths)
    rows = rows_of((width, E))
    dout = (pick_rows(rows, bounds, [coef[j : j + 1] for j in range(per_slab)]) * slope[...]).astype(bf16)
    wide = jnp.concatenate([load_matrix(states, j) for j in range(per_slab)], axis=0)
    crossed = dot(dout, wide, 1, 1)
    total = pick_rows(rows, bounds, [crossed[:, j * E : (j + 1) * E] for j in range(per_slab)])
    blocks = []
    for lo in range(0, width, STRIP):
        hi = lo + STRIP
        keep = strip_mask(lo, STRIP, width, bounds)
        keys = k[lo:hi]
        attn = jnp.where(keep, dot(keys, q[lo:], 1, 1), 0.0).astype(bf16)
        gw = jnp.where(keep, dot(v[lo:hi], dout[lo:], 1, 1), 0.0).astype(bf16)
        dk[lo:hi] = (scaling * dot(gw, q[lo:], 1, 0)).astype(bf16)
        dv[lo:hi] = (scaling * dot(attn, dout[lo:], 1, 0)).astype(bf16)
        total = total + dot(gw, keys, 0, 0)
        blocks.append((lo, hi, total[:STRIP]))
        total = total[STRIP:]
    for lo, hi, block in blocks:
        dq[lo:hi] = (scaling * block).astype(bf16)


def prompt_kernel(ends, q, k, v, g, *refs):
    dq, dk, dv, head = refs[-4:]
    width = q.shape[0]
    scaling = 1.0 / math.sqrt(E * width)
    bounds = slab_bounds(ends, lax.axis_index("seq"), width)
    for lo in range(0, width, STRIP):
        hi = lo + STRIP
        keep = strip_mask(lo, STRIP, width, bounds)
        keys = k[lo:hi]
        attn = jnp.where(keep, dot(keys, q[lo:], 1, 1), 0.0).astype(bf16)
        gw = jnp.where(keep, dot(v[lo:hi], g[lo:], 1, 1), 0.0).astype(bf16)
        dk[lo:hi] = scaling * dot(gw, q[lo:], 1, 0)
        dv[lo:hi] = scaling * dot(attn, g[lo:], 1, 0)
        part = dot(gw, keys, 0, 0)
        if lo == 0:
            first = jnp.where(rows_of((width, E)) < bounds[0], g[...].astype(f32), 0.0).astype(bf16)
            store_parts(head, 0, scaling * dot(q[...], first, 0, 0))
            dq[...] = part
        else:
            dq[lo:] += part


def query_kernel(ends, part, g, states, dq):
    width = g.shape[0]
    scaling = 1.0 / math.sqrt(E * width)
    bounds = slab_bounds(ends, lax.axis_index("seq"), width)
    carry = load_matrix(states, states.shape[1] - 1)
    crossed = dot(g[...], carry, 1, 1)
    rows = rows_of((width, E))
    dq[...] = (scaling * (part[...] + jnp.where(rows < bounds[0], crossed, 0.0))).astype(bf16)


def fetch(pairs, columns, sems, first):
    copies = []
    for i, (a, b) in enumerate(pairs):
        copies.append(pltpu.make_async_copy(a.at[:, columns], b, sems.at[first + i]))
        copies[-1].start()
    return copies


def stage_kernel(dk_part, dv_part, k, v, partial, both, sems):
    ahead = partial.shape[2] // E
    copies = []
    for h in range(ahead):
        at = pl.ds(h * E, E)
        pairs = [(dk_part, partial.at[0]), (dv_part, partial.at[1]), (k, both.at[0]), (v, both.at[1])]
        copies += fetch([(a, b.at[:, at]) for a, b in pairs], at, sems, h * 4)
    for c in copies:
        c.wait()


def right_kernel(
    ends_in, partial, both, states, dk_in, dv_in, k_in, v_in, dk_out, dv_out, rest, rest_both, dk, dv, ends, sems
):
    width, flat = dk_out.shape
    heads = flat // E
    ahead = partial.shape[2] // E
    bring = pltpu.make_async_copy(ends_in, ends, sems.at[0])
    bring.start()
    waits = [[]] * ahead
    for h in range(ahead, heads):
        at = pl.ds((h - ahead) * E, E)
        pairs = [(k_in, rest_both.at[0]), (v_in, rest_both.at[1]), (dk_in, rest.at[0]), (dv_in, rest.at[1])]
        waits.append(fetch([(a, b.at[:, at]) for a, b in pairs], pl.ds(h * E, E), sems, h * 4))
    bring.wait()
    bounds = slab_bounds(ends, lax.axis_index("seq"), width)
    rows = rows_of((width, E))
    copies = []
    for h in range(heads):
        near, kv, place = (partial, both, h) if h < ahead else (rest, rest_both, h - ahead)
        at = slice(place * E, (place + 1) * E)
        mine = slice(h * E, (h + 1) * E)
        for c in waits[h]:
            c.wait()

        def finish(pieces):
            mats = [load_matrix(states, m, h, states.shape[0] // heads) for m in range(pieces)]
            cut = lambda a: [a[:, m * E : (m + 1) * E] for m in range(pieces)]
            some = bounds[: pieces - 1]
            by_v = dot(kv[1, :, at], jnp.concatenate(mats, axis=0), 1, 1)
            dk[:, mine] = (near[0, :, at] + pick_rows(rows, some, cut(by_v))).astype(bf16)
            by_k = dot(kv[0, :, at], jnp.concatenate(mats, axis=1), 1, 0)
            dv[:, mine] = (near[1, :, at] + pick_rows(rows, some, cut(by_k))).astype(bf16)

        pl.when(bounds[-1] < width)(lambda: finish(PIECES))
        pl.when(bounds[-1] >= width)(lambda: finish(PIECES - 1))
        columns = pl.ds(h * E, E)
        for i, (a, b) in enumerate(((dk, dk_out), (dv, dv_out))):
            copies.append(pltpu.make_async_copy(a.at[:, columns], b.at[:, columns], sems.at[(heads + h) * 4 + i]))
            copies[-1].start()
    for c in copies:
        c.wait()


def exchange(a):
    return lax.all_to_all(a, "seq", 0, 0, tiled=True)


def per_device(
    prompt_q,
    prompt_k,
    prompt_v,
    prompt_grad,
    cand_q,
    cand_k,
    cand_v,
    readout,
    prompt_ends,
    cand_lengths,
    cand_prompt,
    cand_ranks,
):
    width = prompt_q.shape[0]
    cand_width = cand_q.shape[0]
    flat = prompt_q.shape[1]
    heads = flat // E
    count = lax.axis_size("seq")
    groups = lax.axis_size("head")
    per_slab = cand_lengths.shape[1]
    cands = cand_prompt.shape[0]
    scaling = 1.0 / math.sqrt(E * width)
    rows = flat // count
    share = count // heads
    whole = pl.BlockSpec((width, E), lambda h: (0, h))
    cand_block = pl.BlockSpec((cand_width, E), lambda h: (0, h))
    like = jax.ShapeDtypeStruct

    def parts_block(n):
        return pl.BlockSpec((share, n, rows, E), lambda h: (h, 0, 0, 0))

    def hbm(*arrays):
        return [pltpu.with_memory_space_constraint(a, pltpu.HBM) for a in arrays]

    def near(*arrays):
        return [pltpu.with_memory_space_constraint(a, pltpu.VMEM) for a in arrays]

    prompt_in = (prompt_q, prompt_k, prompt_v, prompt_grad)
    pieces = call(
        sums_kernel,
        in_specs=[ANY] * 3,
        out_specs=ANY,
        out_shape=pltpu.HBM((count, PIECES, rows, E), bf16),
        scratch_shapes=[pltpu.SMEM(prompt_ends.shape, jnp.int32)]
        + [pltpu.VMEM((width, flat), bf16)] * 2
        + [pltpu.VMEM((count, PIECES, rows, E), bf16), pltpu.SemaphoreType.DMA((heads + 1, 3))],
        name="sums",
    )(*hbm(prompt_ends, prompt_k, prompt_v))
    parts = exchange(pieces)

    pieces, late_in = lax.optimization_barrier((pieces, prompt_in))
    late = max(1, heads // 4)
    partial_shapes = [pltpu.HBM((width, flat), f32)] * 3 + [pltpu.HBM((count, 1, rows, E), bf16)]

    def some_heads(from_head, how_many, arrays, held):
        columns = pl.BlockSpec((width, E), lambda h: (0, h + from_head))
        return call(
            prompt_kernel,
            grid=(how_many,),
            in_specs=[SMEM] + [columns] * 4 + [ANY] * len(held),
            out_specs=[columns] * 3
            + [pl.BlockSpec((share, 1, rows, E), lambda h: (h + from_head, 0, 0, 0))],
            out_shape=partial_shapes,
            input_output_aliases={5 + i: i for i in range(len(held))},
            name="prompt",
        )(prompt_ends, *hbm(*arrays), *hbm(*held))

    partials = some_heads(0, heads - late, late_in, [])
    parts, partials = lax.optimization_barrier((parts, partials))

    body, small = small_first(lambda *refs: chain_kernel(*refs, width=width), (prompt_ends, cand_prompt))
    chained = call(
        body,
        in_specs=[ANY, ANY, VMEM],
        out_specs=VMEM,
        out_shape=like((count, per_slab + 1, rows, E), bf16),
        scratch_shapes=[pltpu.VMEM((prompt_ends.shape[0] + 1, rows, E), f32)] + small,
        name="chain",
    )(prompt_ends, cand_prompt, parts)
    states = exchange(chained)

    chained, cand_in = lax.optimization_barrier((chained, (cand_q, cand_k, cand_v)))
    inside = call(
        inside_kernel,
        grid=(heads,),
        in_specs=[SMEM] + [cand_block] * 3,
        out_specs=cand_block,
        out_shape=like((cand_width, flat), f32),
        name="inside",
    )(cand_lengths, *hbm(*cand_in))

    inside, partials, late_in = lax.optimization_barrier((inside, partials, late_in))
    dq_part, dk_part, dv_part, head_part = some_heads(heads - late, late, late_in, partials)
    states, head_part = lax.optimization_barrier((states, head_part))
    near_q = near(cand_in[0])[0]
    slope, raw = call(
        lambda *refs: scores_kernel(*refs, scaling=scaling),
        in_specs=[SMEM] + [VMEM] * 4,
        out_specs=[VMEM, VMEM],
        out_shape=[pltpu.VMEM((cand_width, flat), f32), like((8, E), f32)],
        name="scores",
    )(cand_lengths, near_q, inside, readout.reshape(1, flat), states)
    raws = [raw]
    for step in range(1, groups):
        raws.append(lax.ppermute(raw, "head", [(i, (i + step) % groups) for i in range(groups)]))
    payload_shape = (count, (per_slab + 1) * rows + SCORE_ROWS, E)
    grads = call(
        lambda *refs: grads_kernel(*refs, scaling=scaling),
        in_specs=[SMEM, VMEM, VMEM, ANY],
        out_specs=ANY,
        out_shape=pltpu.HBM(payload_shape, bf16),
        scratch_shapes=[
            pltpu.VMEM((count, per_slab * rows, E), bf16),
            pltpu.VMEM((count, rows, E), bf16),
            pltpu.SemaphoreType.DMA((heads + 2,)),
        ],
        name="grads",
    )(cand_lengths, near_q, *near(slope), *hbm(head_part))
    grads = call(
        lambda *refs: append_kernel(*refs, per_slab=per_slab),
        in_specs=[ANY] + [VMEM] * groups,
        out_specs=ANY,
        out_shape=pltpu.HBM(payload_shape, bf16),
        input_output_aliases={0: 0},
        scratch_shapes=[pltpu.VMEM((SCORE_ROWS, E), bf16), pltpu.SemaphoreType.DMA((count,))],
        name="append",
    )(*hbm(grads), *raws)
    all_grads = exchange(grads)

    grads, late_grad, slope = lax.optimization_barrier((grads, prompt_grad, slope))
    slope_far = call(
        save_kernel,
        in_specs=[VMEM],
        out_specs=ANY,
        out_shape=pltpu.HBM((cand_width, flat), f32),
        scratch_shapes=[pltpu.SemaphoreType.DMA((4,))],
        name="save",
    )(*near(slope))
    prompt_dq = call(
        query_kernel,
        grid=(heads,),
        in_specs=[SMEM, whole, whole, parts_block(per_slab + 1)],
        out_specs=whole,
        out_shape=pltpu.HBM((width, flat), bf16),
        name="query",
    )(prompt_ends, *hbm(dq_part, late_grad), states)
    all_grads, prompt_dq, slope_far = lax.optimization_barrier((all_grads, prompt_dq, slope_far))

    body, small = small_first(lambda *refs: listwise_kernel(*refs, width=width), (prompt_ends, cand_prompt))
    right, coef, loss = call(
        body,
        in_specs=[ANY, ANY] + [VMEM] * 3,
        out_specs=[VMEM] * 3,
        out_shape=[
            like((count, PIECES, rows, E), bf16),
            like((8, E), f32),
            like((1, E), f32),
        ],
        scratch_shapes=[
            pltpu.VMEM((cands, E), f32),
            pltpu.VMEM((cands, E), f32),
            pltpu.VMEM((prompt_ends.shape[0], rows, E), f32),
        ]
        + small,
        name="listwise",
    )(
        prompt_ends,
        cand_prompt,
        cand_prompt.reshape(1, cands),
        cand_ranks.reshape(1, cands),
        all_grads,
    )
    rights = exchange(right)

    cand_dq, cand_dk, cand_dv = call(
        lambda *refs: cand_kernel(*refs, scaling=scaling),
        grid=(heads,),
        in_specs=[SMEM, pl.BlockSpec((8, E), lambda h: (0, 0))]
        + [cand_block] * 4
        + [parts_block(per_slab + 1)],
        out_specs=[cand_block] * 3,
        out_shape=[pltpu.HBM((cand_width, flat), bf16)] * 3,
        name="cand",
    )(cand_lengths, coef, *hbm(*cand_in, slope_far), states)
    cand_dq, late = lax.optimization_barrier((cand_dq, (dk_part, dv_part, prompt_k, prompt_v)))
    ahead = flat // 2
    staged = call(
        stage_kernel,
        in_specs=[ANY] * 4,
        out_specs=[VMEM] * 2,
        out_shape=[pltpu.VMEM((2, width, ahead), f32), pltpu.VMEM((2, width, ahead), bf16)],
        scratch_shapes=[pltpu.SemaphoreType.DMA((heads * 4,))],
        name="stage",
    )(*hbm(*late))
    rights, staged = lax.optimization_barrier((rights, staged))

    prompt_dk, prompt_dv = call(
        right_kernel,
        in_specs=[ANY] + [VMEM] * 3 + [ANY] * 4,
        out_specs=[ANY] * 2,
        out_shape=[pltpu.HBM((width, flat), bf16)] * 2,
        scratch_shapes=[
            pltpu.VMEM((2, width, flat - ahead), f32),
            pltpu.VMEM((2, width, flat - ahead), bf16),
            pltpu.VMEM((width, flat), bf16),
            pltpu.VMEM((width, flat), bf16),
            pltpu.SMEM(prompt_ends.shape, jnp.int32),
            pltpu.SemaphoreType.DMA((8 * heads,)),
        ],
        name="right",
    )(prompt_ends, *near(*staged), rights, *hbm(*late))
    return (
        prompt_dq,
        prompt_dk,
        prompt_dv,
        cand_dq,
        cand_dk,
        cand_dv,
        loss[0, 0],
    )


def solution(mesh):
    tile = P("seq", "head")
    return jax.shard_map(
        per_device,
        mesh=mesh,
        in_specs=(tile,) * 7 + (P("head"), P(), P("seq", None), P(), P()),
        out_specs=(tile,) * 6 + (P(),),
        check_vma=False,
    )
```

```python
import math

import jax
import jax.numpy as jnp
from jax import lax
from jax.experimental import pallas as pl
from jax.experimental.pallas import tpu as pltpu
from jax.sharding import PartitionSpec as P

E = 128
ENDS = 2
PIECES = ENDS + 1
STRIP = 256
grad_scale = 1048576.0
f32 = jnp.float32
bf16 = jnp.bfloat16
SMEM = pl.BlockSpec(memory_space=pltpu.SMEM)
VMEM = pl.BlockSpec(memory_space=pltpu.VMEM)
ANY = pl.BlockSpec(memory_space=pl.ANY)
SCORE_ROWS = 16
SCORE_PARTS = 3


def dot(a, b, ca, cb):
    return lax.dot_general(a, b, (((ca,), (cb,)), ((), ())), preferred_element_type=f32)


def call(body, **kw):
    return pl.pallas_call(
        body,
        compiler_params=pltpu.CompilerParams(vmem_limit_bytes=24 * 1024 * 1024),
        **kw,
    )


def small_first(body, arrays):
    n = len(arrays)

    def wrapped(*refs):
        held, sems = refs[-n - 1 : -1], refs[-1]
        copies = [pltpu.make_async_copy(refs[i], held[i], sems.at[i]) for i in range(n)]
        for c in copies:
            c.start()
        for c in copies:
            c.wait()
        body(*held, *refs[n : -n - 1])

    scratch = [pltpu.SMEM(a.shape, a.dtype) for a in arrays] + [pltpu.SemaphoreType.DMA((n,))]
    return wrapped, scratch


def count_ends(ends, limit):
    total = jnp.int32(0)
    for p in range(ends.shape[0]):
        total += (ends[p] <= limit).astype(jnp.int32)
    return total


def end_of(ends, pid, none):
    last = ends.shape[0] - 1
    return jnp.where(pid <= last, ends[jnp.minimum(pid, last)], none)


def slab_bounds(ends, slab, width):
    start = slab * width
    first = count_ends(ends, start)
    far = start + width
    return [jnp.minimum(end_of(ends, first + m, far) - start, width) for m in range(ENDS)]


def slot_use(ends, slab, width):
    start = slab * width
    first = count_ends(ends, start)
    segments = count_ends(ends, start + width - 1) - first + 1
    begins = jnp.logical_or(start == 0, jnp.logical_and(first > 0, ends[jnp.maximum(first - 1, 0)] == start))
    closed = end_of(ends, first + 1, start) == start + width
    longer = 2 * (end_of(ends, first, start) - start) > width
    of_first = jnp.logical_and(jnp.logical_not(begins), jnp.logical_or(closed, longer))
    return segments, jnp.logical_or(segments == 1, of_first)


def pick_rows(rows, bounds, options):
    out = options[-1]
    for b, o in zip(reversed(bounds), reversed(options[:-1])):
        out = jnp.where(rows < b, o, out)
    return out


def rows_of(shape, start=0):
    return lax.broadcasted_iota(jnp.int32, shape, 0) + start


def strip_mask(lo, size, width, bounds):
    s = rows_of((size, 1), lo)
    t = lax.broadcasted_iota(jnp.int32, (size, width - lo), 1) + lo
    stop = pick_rows(s, bounds, [jnp.full((size, 1), b, jnp.int32) for b in bounds] + [width])
    return jnp.logical_and(t >= s, t < stop)


def store_parts(out, place, mat):
    parts, rows = out.shape[0], out.shape[2]
    for o in range(parts):
        out[o, place] = mat[o * rows : (o + 1) * rows].astype(bf16)


def load_matrix(ref, place, h=0, share=None):
    share = ref.shape[0] if share is None else share
    return jnp.concatenate([ref[h * share + o, place] for o in range(share)], axis=0)


def sums_kernel(ends_in, k_in, v_in, out, ends, k, v, sems):
    width, flat = k.shape
    heads = flat // E
    share = out.shape[0] // heads
    columns = [pl.ds(h * E, E) for h in range(heads)]
    fetch_ends = pltpu.make_async_copy(ends_in, ends, sems.at[heads, 0])
    fetch_ends.start()
    copies = [
        [
            pltpu.make_async_copy(a.at[:, columns[h]], b.at[:, columns[h]], sems.at[h, i])
            for i, (a, b) in enumerate(((k_in, k), (v_in, v)))
        ]
        for h in range(heads)
    ]
    for group in copies:
        for c in group:
            c.start()
    fetch_ends.wait()
    me = lax.axis_index("seq")
    bounds = slab_bounds(ends, me, width)
    segments, of_first = slot_use(ends, me, width)
    rows = rows_of((width, E))
    zero = jnp.zeros((width, E), f32)
    for h in range(heads):
        for c in copies[h]:
            c.wait()
        at = slice(h * E, (h + 1) * E)
        values = v[:, at].astype(f32)
        pieces = []
        low = 0
        for b in bounds + [width]:
            inside = jnp.logical_and(rows >= low, rows < b)
            pieces.append(jnp.where(inside, values, zero).astype(bf16))
            low = b
        sums = dot(k[:, at], jnp.concatenate(pieces, axis=1), 0, 0)
        mine = out.at[pl.ds(h * share, share)]
        cuts = [sums[:, m * E : (m + 1) * E] for m in range(PIECES)]
        source = jnp.where(of_first, cuts[0], cuts[1])
        spare = source - source.astype(bf16).astype(f32)
        store_parts(mine, 0, cuts[0])
        store_parts(mine, 1, jnp.where(segments == 1, spare, cuts[1]))
        store_parts(mine, 2, jnp.where(segments == PIECES, cuts[2], spare))


def chain_kernel(ends, cand_prompt, parts, out, held, *, width):
    count = parts.shape[0]
    per_slab = cand_prompt.shape[0] // count
    running = jnp.zeros(parts.shape[2:], f32)
    for e in range(count):
        start = e * width
        first = count_ends(ends, start)
        last = count_ends(ends, start + width - 1)
        begins = jnp.bool_(True) if e == 0 else ends[jnp.maximum(first - 1, 0)] == start
        if e > 0:
            begins = jnp.logical_and(first > 0, begins)
        incoming = jnp.where(begins, 0.0, running)
        out[e, per_slab] = incoming.astype(bf16)
        segments, of_first = slot_use(ends, jnp.int32(e), width)
        second = parts[e, 1].astype(f32)
        third = parts[e, 2].astype(f32)
        spare = jnp.where(segments == 1, second, jnp.where(segments == PIECES, 0.0, third))
        firsts = incoming + (parts[e, 0].astype(f32) + jnp.where(of_first, spare, 0.0))
        second = second + jnp.where(of_first, 0.0, spare)
        nowhere = ends.shape[0]
        for m, piece in enumerate((firsts, second)):
            ended = end_of(ends, first + m, start + width + 1) <= start + width
            held[jnp.where(ended, first + m, nowhere)] = piece
        running = jnp.where(last == first, firsts, jnp.where(last == first + 1, second, third))
    for c in range(cand_prompt.shape[0]):
        out[c // per_slab, c % per_slab] = held[cand_prompt[c]].astype(bf16)


def inside_kernel(lengths, q, k, v, out):
    width = q.shape[0]
    bounds = cand_bounds(lengths)
    for lo in range(0, width, STRIP):
        hi = lo + STRIP
        scores = dot(q[lo:hi], k[:hi], 1, 1)
        t = rows_of((STRIP, hi), lo)
        s = lax.broadcasted_iota(jnp.int32, (STRIP, hi), 1)
        begin = pick_rows(t[:, :1], bounds, [0] + [jnp.full((STRIP, 1), b, jnp.int32) for b in bounds])
        keep = jnp.logical_and(s <= t, s >= begin)
        out[lo:hi] = dot(jnp.where(keep, scores, 0.0).astype(bf16), v[:hi], 1, 0)


def cand_bounds(lengths):
    bounds = []
    total = jnp.int32(0)
    for j in range(lengths.shape[1] - 1):
        total += lengths[0, j]
        bounds.append(total)
    return bounds


def scores_kernel(lengths, q, inside, readout, states, slope_out, raw_out, *, scaling):
    width, flat = q.shape
    heads = flat // E
    per_slab = lengths.shape[1]
    bounds = cand_bounds(lengths)
    rows = rows_of((width, E))
    zero = jnp.zeros((width, E), f32)
    inverse = [1.0 / jnp.full((1, E), lengths[0, j], jnp.int32).astype(f32) for j in range(per_slab)]
    totals = [jnp.zeros((1, E), f32) for j in range(per_slab)]
    for h in range(heads):
        at = slice(h * E, (h + 1) * E)
        wide = [load_matrix(states, j, h, states.shape[0] // heads) for j in range(per_slab)]
        crossed = dot(q[:, at], jnp.concatenate(wide, axis=1), 1, 0)
        crossed = pick_rows(rows, bounds, [crossed[:, j * E : (j + 1) * E] for j in range(per_slab)])
        out = scaling * (inside[:, at] + crossed)
        weight = pick_rows(rows, bounds, inverse) * readout[:, at]
        sigma = jax.nn.sigmoid(out)
        slope_out[:, at] = weight * sigma * (1.0 + out * (1.0 - sigma))
        silu = out * sigma * weight
        low = 0
        for j, b in enumerate(bounds + [width]):
            mine = jnp.logical_and(rows >= low, rows < b)
            totals[j] += jnp.sum(jnp.where(mine, silu, zero), axis=0, keepdims=True)
            low = b
    raw_out[...] = jnp.zeros_like(raw_out)
    for j in range(per_slab):
        raw_out[j : j + 1] = jnp.broadcast_to(jnp.sum(totals[j], axis=1, keepdims=True), (1, E))


def save_kernel(near, far, sems):
    size = near.shape[0] // sems.shape[0]
    some = [pl.ds(i * size, size) for i in range(sems.shape[0])]
    copies = [pltpu.make_async_copy(near.at[a], far.at[a], sems.at[i]) for i, a in enumerate(some)]
    for c in copies:
        c.start()
    for c in copies:
        c.wait()


def grads_kernel(lengths, q, slope, head, out, sem, *, scaling):
    width, flat = q.shape
    heads = flat // E
    count = out.shape[0]
    share = count // heads
    size = flat // count
    per_slab = lengths.shape[1]
    bring = pltpu.make_async_copy(head.at[:, 0], out.at[:, pl.ds(per_slab * size, size)], sem)
    bring.start()
    bounds = cand_bounds(lengths)
    rows = rows_of((width, E))
    for h in range(heads):
        at = slice(h * E, (h + 1) * E)
        mine = slope[:, at]
        high = mine.astype(bf16)
        low_part = (mine - high.astype(f32)).astype(bf16)
        queries = q[:, at].astype(f32)
        masked = []
        low = 0
        for b in bounds + [width]:
            masked.append(jnp.where(jnp.logical_and(rows >= low, rows < b), queries, 0.0).astype(bf16))
            low = b
        grads = dot(jnp.concatenate(masked, axis=1), jnp.concatenate([high, low_part], axis=1), 0, 0)
        grads = (scaling * (grads[:, :E] + grads[:, E:])).astype(bf16)
        for j in range(per_slab):
            for o in range(share):
                start = j * E + o * size
                out[h * share + o, j * size : (j + 1) * size] = grads[start : start + size]
    bring.wait()


def append_kernel(payload, *refs, per_slab):
    raws, out, tile, sems = refs[:-3], refs[-3], refs[-2], refs[-1]
    total = raws[0][...]
    for r in raws[1:]:
        total += r[...]
    lines = []
    for j in range(per_slab):
        left = total[j : j + 1]
        for i in range(SCORE_PARTS):
            line = left.astype(bf16).astype(f32)
            lines.append(line)
            left = left - line
    lines.append(jnp.zeros((SCORE_ROWS - len(lines), E), f32))
    tile[...] = jnp.concatenate(lines, axis=0).astype(bf16)
    place = pl.ds(out.shape[1] - SCORE_ROWS, SCORE_ROWS)
    copies = [pltpu.make_async_copy(tile, out.at[o, place], sems.at[o]) for o in range(out.shape[0])]
    for c in copies:
        c.start()
    for c in copies:
        c.wait()


def listwise_kernel(
    ends,
    prompts,
    prompt_row,
    rank_row,
    grads,
    out,
    coef_out,
    loss_out,
    raw_held,
    coef_held,
    held,
    *,
    width,
):
    count = grads.shape[0]
    size = held.shape[1]
    per_slab = prompts.shape[0] // count
    cands = count * per_slab
    prompt_count = ends.shape[0]
    for e in range(count):
        tile = grads[e, (per_slab + 1) * size :].astype(f32)
        for j in range(per_slab):
            total = tile[SCORE_PARTS * j : SCORE_PARTS * j + 1]
            for i in range(1, SCORE_PARTS):
                total = total + tile[SCORE_PARTS * j + i : SCORE_PARTS * j + i + 1]
            raw_held[e * per_slab + j : e * per_slab + j + 1] = total
    raw = raw_held[...]
    square = (cands, cands)
    down = lax.broadcasted_iota(jnp.int32, square, 0)
    across = lax.broadcasted_iota(jnp.int32, square, 1)
    same_spot = down == across
    own = jnp.broadcast_to(prompt_row[...].astype(f32), square)
    own_down = jnp.sum(jnp.where(same_spot, own, 0.0), axis=1, keepdims=True)
    group = own == own_down
    rank_weight = jnp.broadcast_to(jnp.exp(-rank_row[...].astype(f32)), square)
    rank_down = jnp.sum(jnp.where(same_spot, rank_weight, 0.0), axis=1, keepdims=True)
    target = rank_down / jnp.sum(jnp.where(group, rank_weight, 0.0), axis=1, keepdims=True)
    tanh_raw = jnp.tanh(raw)
    squashed = 3.0 * tanh_raw
    exp_scores = jnp.exp(squashed)
    exp_across = jnp.sum(jnp.where(same_spot, exp_scores[:, :cands], 0.0), axis=0, keepdims=True)
    denom = jnp.sum(jnp.where(group, jnp.broadcast_to(exp_across, square), 0.0), axis=1, keepdims=True)
    terms = target * (squashed - jnp.log(denom))
    loss_out[...] = -jnp.sum(terms, axis=0, keepdims=True) / prompt_count
    coef = grad_scale / prompt_count * (exp_scores / denom - target) * 3.0 * (1.0 - tanh_raw * tanh_raw)
    coef_held[...] = coef
    me = lax.axis_index("seq")
    for j in range(per_slab):
        coef_out[j : j + 1] = coef_held[pl.ds(me * per_slab + j, 1)]
    held[...] = jnp.zeros_like(held)
    for c in range(cands):
        j = c % per_slab
        held[prompts[c]] += grads[c // per_slab, j * size : (j + 1) * size].astype(f32) * coef[c : c + 1]
    running = jnp.zeros((size, E), f32)
    for e in reversed(range(count)):
        start = e * width
        far = start + width
        first = count_ends(ends, start)
        last = count_ends(ends, far - 1)
        goes_on = ends[last] != far
        from_right = jnp.where(goes_on, running, 0.0)
        from_right_bf = from_right.astype(bf16)
        for m in range(ENDS):
            pid = first + m
            ended = end_of(ends, pid, far + 1) <= far
            here = held[jnp.minimum(pid, prompt_count - 1)]
            out[e, m] = jnp.where(ended, here, from_right).astype(bf16)
            if m == 0:
                running = grads[e, per_slab * size : (per_slab + 1) * size].astype(f32) + jnp.where(ended, here, running)
        out[e, ENDS] = from_right_bf


def cand_kernel(lengths, coef, q, k, v, slope, states, dq, dk, dv, *, scaling):
    width = q.shape[0]
    per_slab = lengths.shape[1]
    bounds = cand_bounds(lengths)
    rows = rows_of((width, E))
    dout = (pick_rows(rows, bounds, [coef[j : j + 1] for j in range(per_slab)]) * slope[...]).astype(bf16)
    wide = jnp.concatenate([load_matrix(states, j) for j in range(per_slab)], axis=0)
    crossed = dot(dout, wide, 1, 1)
    total = pick_rows(rows, bounds, [crossed[:, j * E : (j + 1) * E] for j in range(per_slab)])
    blocks = []
    for lo in range(0, width, STRIP):
        hi = lo + STRIP
        keep = strip_mask(lo, STRIP, width, bounds)
        keys = k[lo:hi]
        attn = jnp.where(keep, dot(keys, q[lo:], 1, 1), 0.0).astype(bf16)
        gw = jnp.where(keep, dot(v[lo:hi], dout[lo:], 1, 1), 0.0).astype(bf16)
        dk[lo:hi] = (scaling * dot(gw, q[lo:], 1, 0)).astype(bf16)
        dv[lo:hi] = (scaling * dot(attn, dout[lo:], 1, 0)).astype(bf16)
        total = total + dot(gw, keys, 0, 0)
        blocks.append((lo, hi, total[:STRIP]))
        total = total[STRIP:]
    for lo, hi, block in blocks:
        dq[lo:hi] = (scaling * block).astype(bf16)


def prompt_kernel(ends, q, k, v, g, *refs):
    dq, dk, dv, head = refs[-4:]
    width = q.shape[0]
    scaling = 1.0 / math.sqrt(E * width)
    bounds = slab_bounds(ends, lax.axis_index("seq"), width)
    for lo in range(0, width, STRIP):
        hi = lo + STRIP
        keep = strip_mask(lo, STRIP, width, bounds)
        keys = k[lo:hi]
        attn = jnp.where(keep, dot(keys, q[lo:], 1, 1), 0.0).astype(bf16)
        gw = jnp.where(keep, dot(v[lo:hi], g[lo:], 1, 1), 0.0).astype(bf16)
        dk[lo:hi] = scaling * dot(gw, q[lo:], 1, 0)
        dv[lo:hi] = scaling * dot(attn, g[lo:], 1, 0)
        part = dot(gw, keys, 0, 0)
        if lo == 0:
            first = jnp.where(rows_of((width, E)) < bounds[0], g[...].astype(f32), 0.0).astype(bf16)
            store_parts(head, 0, scaling * dot(q[...], first, 0, 0))
            dq[...] = part
        else:
            dq[lo:] += part


def query_kernel(ends, part, g, states, dq):
    width = g.shape[0]
    scaling = 1.0 / math.sqrt(E * width)
    bounds = slab_bounds(ends, lax.axis_index("seq"), width)
    carry = load_matrix(states, states.shape[1] - 1)
    crossed = dot(g[...], carry, 1, 1)
    rows = rows_of((width, E))
    dq[...] = (scaling * (part[...] + jnp.where(rows < bounds[0], crossed, 0.0))).astype(bf16)


def fetch(pairs, columns, sems, first):
    copies = []
    for i, (a, b) in enumerate(pairs):
        copies.append(pltpu.make_async_copy(a.at[:, columns], b, sems.at[first + i]))
        copies[-1].start()
    return copies


def stage_kernel(dk_part, dv_part, k, v, partial, both, sems):
    ahead = partial.shape[2] // E
    copies = []
    for h in range(ahead):
        at = pl.ds(h * E, E)
        pairs = [(dk_part, partial.at[0]), (dv_part, partial.at[1]), (k, both.at[0]), (v, both.at[1])]
        copies += fetch([(a, b.at[:, at]) for a, b in pairs], at, sems, h * 4)
    for c in copies:
        c.wait()


def right_kernel(
    ends_in, partial, both, states, dk_in, dv_in, k_in, v_in, dk_out, dv_out, rest, rest_both, dk, dv, ends, sems
):
    width, flat = dk_out.shape
    heads = flat // E
    ahead = partial.shape[2] // E
    bring = pltpu.make_async_copy(ends_in, ends, sems.at[0])
    bring.start()
    waits = [[]] * ahead
    for h in range(ahead, heads):
        at = pl.ds((h - ahead) * E, E)
        pairs = [(k_in, rest_both.at[0]), (v_in, rest_both.at[1]), (dk_in, rest.at[0]), (dv_in, rest.at[1])]
        waits.append(fetch([(a, b.at[:, at]) for a, b in pairs], pl.ds(h * E, E), sems, h * 4))
    bring.wait()
    bounds = slab_bounds(ends, lax.axis_index("seq"), width)
    rows = rows_of((width, E))
    copies = []
    for h in range(heads):
        near, kv, place = (partial, both, h) if h < ahead else (rest, rest_both, h - ahead)
        at = slice(place * E, (place + 1) * E)
        mine = slice(h * E, (h + 1) * E)
        for c in waits[h]:
            c.wait()

        def finish(pieces, to, part, operand, axis):
            mats = [load_matrix(states, m, h, states.shape[0] // heads) for m in range(pieces)]
            product = dot(kv[operand, :, at], jnp.concatenate(mats, axis=1 - axis), 1, axis)
            options = [product[:, m * E : (m + 1) * E] for m in range(pieces)]
            to[:, mine] = (near[part, :, at] + pick_rows(rows, bounds[: pieces - 1], options)).astype(bf16)

        columns = pl.ds(h * E, E)
        for i, (a, b, operand, axis) in enumerate(((dk, dk_out, 1, 1), (dv, dv_out, 0, 0))):
            pl.when(bounds[-1] < width)(lambda: finish(PIECES, a, i, operand, axis))
            pl.when(bounds[-1] >= width)(lambda: finish(PIECES - 1, a, i, operand, axis))
            copies.append(pltpu.make_async_copy(a.at[:, columns], b.at[:, columns], sems.at[(heads + h) * 4 + i]))
            copies[-1].start()
    for c in copies:
        c.wait()


def exchange(a):
    return lax.all_to_all(a, "seq", 0, 0, tiled=True)


def per_device(
    prompt_q,
    prompt_k,
    prompt_v,
    prompt_grad,
    cand_q,
    cand_k,
    cand_v,
    readout,
    prompt_ends,
    cand_lengths,
    cand_prompt,
    cand_ranks,
):
    width = prompt_q.shape[0]
    cand_width = cand_q.shape[0]
    flat = prompt_q.shape[1]
    heads = flat // E
    count = lax.axis_size("seq")
    groups = lax.axis_size("head")
    per_slab = cand_lengths.shape[1]
    cands = cand_prompt.shape[0]
    scaling = 1.0 / math.sqrt(E * width)
    rows = flat // count
    share = count // heads
    whole = pl.BlockSpec((width, E), lambda h: (0, h))
    cand_block = pl.BlockSpec((cand_width, E), lambda h: (0, h))
    like = jax.ShapeDtypeStruct

    def parts_block(n):
        return pl.BlockSpec((share, n, rows, E), lambda h: (h, 0, 0, 0))

    def hbm(*arrays):
        return [pltpu.with_memory_space_constraint(a, pltpu.HBM) for a in arrays]

    def near(*arrays):
        return [pltpu.with_memory_space_constraint(a, pltpu.VMEM) for a in arrays]

    prompt_in = (prompt_q, prompt_k, prompt_v, prompt_grad)
    pieces = call(
        sums_kernel,
        in_specs=[ANY] * 3,
        out_specs=VMEM,
        out_shape=like((count, PIECES, rows, E), bf16),
        scratch_shapes=[pltpu.SMEM(prompt_ends.shape, jnp.int32)]
        + [pltpu.VMEM((width, flat), bf16)] * 2
        + [pltpu.SemaphoreType.DMA((heads + 1, 2))],
        name="sums",
    )(*hbm(prompt_ends, prompt_k, prompt_v))
    parts = exchange(pieces)

    pieces, late_in = lax.optimization_barrier((pieces, prompt_in))
    late = max(1, heads // 4)
    partial_shapes = [pltpu.HBM((width, flat), f32)] * 3 + [pltpu.HBM((count, 1, rows, E), bf16)]

    def some_heads(from_head, how_many, arrays, held):
        columns = pl.BlockSpec((width, E), lambda h: (0, h + from_head))
        return call(
            prompt_kernel,
            grid=(how_many,),
            in_specs=[SMEM] + [columns] * 4 + [ANY] * len(held),
            out_specs=[columns] * 3
            + [pl.BlockSpec((share, 1, rows, E), lambda h: (h + from_head, 0, 0, 0))],
            out_shape=partial_shapes,
            input_output_aliases={5 + i: i for i in range(len(held))},
            name="prompt",
        )(prompt_ends, *hbm(*arrays), *hbm(*held))

    partials = some_heads(0, heads - late, late_in, [])
    parts, partials = lax.optimization_barrier((parts, partials))

    body, small = small_first(lambda *refs: chain_kernel(*refs, width=width), (prompt_ends, cand_prompt))
    chained = call(
        body,
        in_specs=[ANY, ANY, VMEM],
        out_specs=VMEM,
        out_shape=like((count, per_slab + 1, rows, E), bf16),
        scratch_shapes=[pltpu.VMEM((prompt_ends.shape[0] + 1, rows, E), f32)] + small,
        name="chain",
    )(prompt_ends, cand_prompt, parts)
    states = exchange(chained)

    chained, cand_in = lax.optimization_barrier((chained, (cand_q, cand_k, cand_v)))
    inside = call(
        inside_kernel,
        grid=(heads,),
        in_specs=[SMEM] + [cand_block] * 3,
        out_specs=cand_block,
        out_shape=like((cand_width, flat), f32),
        name="inside",
    )(cand_lengths, *hbm(*cand_in))

    inside, partials, late_in = lax.optimization_barrier((inside, partials, late_in))
    dq_part, dk_part, dv_part, head_part = some_heads(heads - late, late, late_in, partials)
    states, head_part = lax.optimization_barrier((states, head_part))
    near_q = near(cand_in[0])[0]
    slope, raw = call(
        lambda *refs: scores_kernel(*refs, scaling=scaling),
        in_specs=[SMEM] + [VMEM] * 4,
        out_specs=[VMEM, VMEM],
        out_shape=[pltpu.VMEM((cand_width, flat), f32), like((8, E), f32)],
        name="scores",
    )(cand_lengths, near_q, inside, readout.reshape(1, flat), states)
    raws = [raw]
    for step in range(1, groups):
        raws.append(lax.ppermute(raw, "head", [(i, (i + step) % groups) for i in range(groups)]))
    payload_shape = (count, (per_slab + 1) * rows + SCORE_ROWS, E)
    grads = call(
        lambda *refs: grads_kernel(*refs, scaling=scaling),
        in_specs=[SMEM, VMEM, VMEM, ANY],
        out_specs=VMEM,
        out_shape=pltpu.HBM(payload_shape, bf16),
        scratch_shapes=[pltpu.SemaphoreType.DMA],
        name="grads",
    )(cand_lengths, near_q, *near(slope), *hbm(head_part))
    grads = call(
        lambda *refs: append_kernel(*refs, per_slab=per_slab),
        in_specs=[ANY] + [VMEM] * groups,
        out_specs=ANY,
        out_shape=pltpu.HBM(payload_shape, bf16),
        input_output_aliases={0: 0},
        scratch_shapes=[pltpu.VMEM((SCORE_ROWS, E), bf16), pltpu.SemaphoreType.DMA((count,))],
        name="append",
    )(*hbm(grads), *raws)
    all_grads = exchange(grads)

    grads, late_grad, slope = lax.optimization_barrier((grads, prompt_grad, slope))
    slope_far = call(
        save_kernel,
        in_specs=[VMEM],
        out_specs=ANY,
        out_shape=pltpu.HBM((cand_width, flat), f32),
        scratch_shapes=[pltpu.SemaphoreType.DMA((4,))],
        name="save",
    )(*near(slope))
    prompt_dq = call(
        query_kernel,
        grid=(heads,),
        in_specs=[SMEM, whole, whole, parts_block(per_slab + 1)],
        out_specs=whole,
        out_shape=pltpu.HBM((width, flat), bf16),
        name="query",
    )(prompt_ends, *hbm(dq_part, late_grad), states)
    all_grads, prompt_dq, slope_far = lax.optimization_barrier((all_grads, prompt_dq, slope_far))

    body, small = small_first(lambda *refs: listwise_kernel(*refs, width=width), (prompt_ends, cand_prompt))
    right, coef, loss = call(
        body,
        in_specs=[ANY, ANY] + [VMEM] * 3,
        out_specs=[VMEM] * 3,
        out_shape=[
            like((count, PIECES, rows, E), bf16),
            like((8, E), f32),
            like((1, E), f32),
        ],
        scratch_shapes=[
            pltpu.VMEM((cands, E), f32),
            pltpu.VMEM((cands, E), f32),
            pltpu.VMEM((prompt_ends.shape[0], rows, E), f32),
        ]
        + small,
        name="listwise",
    )(
        prompt_ends,
        cand_prompt,
        cand_prompt.reshape(1, cands),
        cand_ranks.reshape(1, cands),
        all_grads,
    )
    rights = exchange(right)

    cand_dq, cand_dk, cand_dv = call(
        lambda *refs: cand_kernel(*refs, scaling=scaling),
        grid=(heads,),
        in_specs=[SMEM, pl.BlockSpec((8, E), lambda h: (0, 0))]
        + [cand_block] * 4
        + [parts_block(per_slab + 1)],
        out_specs=[cand_block] * 3,
        out_shape=[pltpu.HBM((cand_width, flat), bf16)] * 3,
        name="cand",
    )(cand_lengths, coef, *hbm(*cand_in, slope_far), states)
    cand_dq, late = lax.optimization_barrier((cand_dq, (dk_part, dv_part, prompt_k, prompt_v)))
    ahead = flat // 2
    staged = call(
        stage_kernel,
        in_specs=[ANY] * 4,
        out_specs=[VMEM] * 2,
        out_shape=[pltpu.VMEM((2, width, ahead), f32), pltpu.VMEM((2, width, ahead), bf16)],
        scratch_shapes=[pltpu.SemaphoreType.DMA((heads * 4,))],
        name="stage",
    )(*hbm(*late))
    rights, staged = lax.optimization_barrier((rights, staged))

    prompt_dk, prompt_dv = call(
        right_kernel,
        in_specs=[ANY] + [VMEM] * 3 + [ANY] * 4,
        out_specs=[ANY] * 2,
        out_shape=[pltpu.HBM((width, flat), bf16)] * 2,
        scratch_shapes=[
            pltpu.VMEM((2, width, flat - ahead), f32),
            pltpu.VMEM((2, width, flat - ahead), bf16),
            pltpu.VMEM((width, flat), bf16),
            pltpu.VMEM((width, flat), bf16),
            pltpu.SMEM(prompt_ends.shape, jnp.int32),
            pltpu.SemaphoreType.DMA((8 * heads,)),
        ],
        name="right",
    )(prompt_ends, *near(*staged), rights, *hbm(*late))
    return (
        prompt_dq,
        prompt_dk,
        prompt_dv,
        cand_dq,
        cand_dk,
        cand_dv,
        loss[0, 0],
    )


def solution(mesh):
    tile = P("seq", "head")
    return jax.shard_map(
        per_device,
        mesh=mesh,
        in_specs=(tile,) * 7 + (P("head"), P(), P("seq", None), P(), P()),
        out_specs=(tile,) * 6 + (P(),),
        check_vma=False,
    )
```
